128 devices in a mesh: section: 2 (over y_hi), dp: 32 (over z, x, core), tensor: 2 (over y_lo).
Axes of the slice: x: 4, y: 4 (y_hi: 2, y_lo: 2; y = y_hi * 2 + y_lo), z: 4, core: 2. Of those that a mesh axis runs over, the one named last changes fastest.
Arguments:
- layer_input: bfloat16 [2, 32, 256, 1024], P(None, 'dp'), may hold values from -6 to 6
- cotangent: bfloat16 [2, 32, 256, 1024], P(None, 'dp'), may hold values from -6 to 6
- order: int32 [2], replicated, may hold values from 0 to 1, each once
- ln1_scale: bfloat16 [2, 1024], P('section'), may hold values from 0.099609375 to 1.8984375
- ln1_bias: bfloat16 [2, 1024], P('section'), may hold values from -1.796875 to 1.796875
- ln2_scale: bfloat16 [2, 1024], P('section'), may hold values from 0.099609375 to 1.8984375
- ln2_bias: bfloat16 [2, 1024], P('section'), may hold values from -1.796875 to 1.796875
- qkv_weight: bfloat16 [2, 1024, 3, 1024], P('section', None, None, 'tensor'), may hold values from -0.1875 to 0.1875
- qkv_bias: bfloat16 [2, 3, 1024], P('section', None, 'tensor'), may hold values from -1.796875 to 1.796875
- out_weight: bfloat16 [2, 1024, 1024], P('section', 'tensor'), may hold values from -0.75 to 0.75
- out_bias: bfloat16 [2, 1024], P('section'), may hold values from -3 to 3
- up_weight: bfloat16 [2, 1024, 4096], P('section', None, 'tensor'), may hold values from -0.1875 to 0.1875
- up_bias: bfloat16 [2, 4096], P('section', 'tensor'), may hold values from -3 to 3
- down_weight: bfloat16 [2, 4096, 1024], P('section', 'tensor'), may hold values from -0.09375 to 0.09375
- down_bias: bfloat16 [2, 1024], P('section'), may hold values from -3 to 3
Outputs:
- layer_outputs: bfloat16 [2, 2, 32, 256, 1024], P('section', None, 'dp')
- input_grads: bfloat16 [2, 2, 32, 256, 1024], P('section', None, 'dp')
- ln1_scale_grad: float32 [2, 1024], P('section')
- ln1_bias_grad: float32 [2, 1024], P('section')
- ln2_scale_grad: float32 [2, 1024], P('section')
- ln2_bias_grad: float32 [2, 1024], P('section')
- qkv_weight_grad: float32 [2, 1024, 3, 1024], P('section', None, None, 'tensor')
- qkv_bias_grad: float32 [2, 3, 1024], P('section', None, 'tensor')
- out_weight_grad: float32 [2, 1024, 1024], P('section', 'tensor')
- out_bias_grad: float32 [2, 1024], P('section')
- up_weight_grad: float32 [2, 1024, 4096], P('section', None, 'tensor')
- up_bias_grad: float32 [2, 4096], P('section', 'tensor')
- down_weight_grad: float32 [2, 4096, 1024], P('section', 'tensor')
- down_bias_grad: float32 [2, 1024], P('section')
The draws below stay inside these ranges and needn't reach their ends.
Inputs may be any that keep to these rules, and one draw needn't show every extreme that they name: order names each of the 2 micro-batches once.
All inputs are finite; a program needn't handle non-finite values.
Results may differ from the reference program's by a relative error of at most 0.023.
Values may be sent and summed in bfloat16 or wider, within the bound.
A program may use at most 192 MiB of HBM per device.

```python
import jax
import jax.numpy as jnp
from jax import lax

D = 1024
H = 16
HD = 64
FF = 4096
ROT = 16
SEQ = 256
MICRO = 2
LAYERS = 2
SEQS = 32


def block_levels(key, extent, pieces, smallest, top_value):
    factor_of = 1.0
    for position, blocks in pieces:
        heights = jax.random.uniform(jax.random.fold_in(jax.random.fold_in(key, 6), position), (blocks,), jnp.float32, smallest / len(pieces), top_value / len(pieces))
        factor_of = factor_of * jnp.repeat(jnp.exp(heights), extent[position] // blocks).reshape((-1,) + (1,) * (len(extent) - 1 - position))
    return factor_of


def noise(own_key, extent, spread, bound, cuts=(), kind=jnp.bfloat16):
    array = jax.random.normal(own_key, extent, jnp.float32) * spread
    if len(cuts) > 0:
        array = block_levels(own_key, extent, cuts, -0.22, 0.18) * array
    return jnp.clip(array, min=-bound, max=bound).astype(kind)


def setup_inputs(seed: int = 0) -> dict:
    splits = jax.random.split(jax.random.key(seed), 16)
    return {
        "layer_input": noise(splits[0], (MICRO, SEQS, SEQ, D), 1.0, 6.0, ((1, 32),)),
        "cotangent": noise(splits[1], (MICRO, SEQS, SEQ, D), 1.0, 6.0, ((1, 32),)),
        "order": jax.random.permutation(splits[2], MICRO).astype(jnp.int32),
        "ln1_scale": jnp.clip(1.0 + 0.18 * jax.random.normal(splits[3], (LAYERS, D), jnp.float32), 0.099609375, 1.8984375).astype(jnp.bfloat16),
        "ln1_bias": noise(splits[4], (LAYERS, D), 0.3, 1.796875, ((0, 2),)),
        "ln2_scale": jnp.clip(1.0 + 0.18 * jax.random.normal(splits[5], (LAYERS, D), jnp.float32), 0.099609375, 1.8984375).astype(jnp.bfloat16),
        "ln2_bias": noise(splits[6], (LAYERS, D), 0.3, 1.796875, ((0, 2),)),
        "qkv_weight": noise(splits[7], (LAYERS, D, 3, H * HD), D ** -0.5, 0.1875, ((0, 2), (3, 2))),
        "qkv_bias": noise(splits[8], (LAYERS, 3, H * HD), 0.3, 1.796875, ((0, 2), (2, 2))),
        "out_weight": noise(splits[9], (LAYERS, H * HD, D), (H * HD // 16) ** -0.5, 0.75, ((0, 2), (1, 2))),
        "out_bias": noise(splits[10], (LAYERS, D), 0.5, 3.0, ((0, 2),)),
        "up_weight": noise(splits[11], (LAYERS, D, FF), D ** -0.5, 0.1875, ((0, 2), (2, 2))),
        "up_bias": noise(splits[12], (LAYERS, FF), 0.5, 3.0, ((0, 2), (1, 2))),
        "down_weight": noise(splits[13], (LAYERS, FF, D), FF ** -0.5, 0.09375, ((0, 2), (1, 2))),
        "down_bias": noise(splits[14], (LAYERS, D), 0.5, 3.0, ((0, 2),)),
    }


@jax.custom_vjp
def low(v):
    return lax.optimization_barrier(v.astype(jnp.bfloat16)).astype(jnp.float32)

@jax.custom_vjp
def low_back(v):
    return v

def low_keep(v):
    return (low(v), None)

def low_pass(kept, grad):
    return (grad,)

def back_keep(v):
    return (v, None)

def back_low(kept, grad):
    return (low(grad),)
low.defvjp(low_keep, low_pass)
low_back.defvjp(back_keep, back_low)
EPSILON = 1e-05
HIGHEST = lax.Precision.HIGHEST

def rotary_tables(length):
    half_rot = ROT // 2
    frequency = 1.0 / 10000.0 ** (jnp.arange(half_rot, dtype=jnp.float32) * 2.0 / ROT)
    where_at = jnp.arange(length, dtype=jnp.float32)
    angles = where_at[:, None] * frequency[None, :]
    angles = jnp.concatenate([angles, angles], axis=-1)[:, None, :]
    return (jnp.cos(angles), jnp.sin(angles))

def rotate(vector, cos_table, sin_table):
    half_rot = ROT // 2
    leading = vector[..., :ROT]
    turned = jnp.concatenate([-leading[..., half_rot:], leading[..., :half_rot]], axis=-1)
    return jnp.concatenate([leading * cos_table + turned * sin_table, vector[..., ROT:]], axis=-1)

def standardize(inputs):
    centered = inputs - lax.optimization_barrier(jnp.mean(inputs, axis=-1, keepdims=True))
    inv_std = lax.rsqrt(lax.optimization_barrier(jnp.mean(centered * centered, axis=-1, keepdims=True)) + EPSILON)
    return centered * inv_std

def layer(inputs, params, cos_table, sin_table):
    scale_one, shift_one, scale_two, shift_two, qkv_w, qkv_b, out_w, out_b, up_w, up_b, down_w, down_b = params
    batch_size, length = (inputs.shape[0], inputs.shape[1])
    normed = standardize(inputs)
    first_in = low(normed * scale_one + shift_one)
    second_in = low(normed * scale_two + shift_two)
    projected = jnp.einsum('bsd,dtc->bstc', first_in, qkv_w, precision=HIGHEST) + qkv_b
    projected = low_back(projected).reshape(batch_size, length, 3, H, HD)
    queries = low(rotate(projected[:, :, 0], cos_table, sin_table) * HD ** (-0.5))
    key_vecs = low(rotate(projected[:, :, 1], cos_table, sin_table))
    values = low(projected[:, :, 2])
    scores = low_back(jnp.einsum('bqhe,bkhe->bhqk', queries, key_vecs, precision=HIGHEST))
    causal = jnp.arange(length)[:, None] >= jnp.arange(length)[None, :]
    scores = jnp.where(causal, scores, -1e+30)
    attn_probs = low(jax.nn.softmax(scores, axis=-1))
    context = jnp.einsum('bhqk,bkhe->bqhe', attn_probs, values, precision=HIGHEST)
    context = low(low_back(context)).reshape(batch_size, length, H * HD)
    hidden = low_back(jnp.einsum('bsd,df->bsf', second_in, up_w, precision=HIGHEST) + up_b)
    activated = low(jax.nn.gelu(hidden, approximate=False))
    attn_out = jnp.einsum('bsh,hd->bsd', context, out_w, precision=HIGHEST)
    mlp_out = jnp.einsum('bsf,fd->bsd', activated, down_w, precision=HIGHEST)
    return inputs + attn_out + mlp_out + out_b + down_b

def stack_forward(start_x, shifts, params, cos_table, sin_table):
    current = start_x
    rounded = []
    final_out = start_x
    for level_index in range(LAYERS):
        level_params = tuple((weight_arr[level_index] for weight_arr in params))
        final_out = layer(current, level_params, cos_table, sin_table)
        if level_index + 1 < LAYERS:
            current = low(low_back(final_out)) + shifts[level_index]
            rounded.append(current)
    return (final_out, tuple(rounded))

def reference(layer_input, cotangent, order, ln1_scale, ln1_bias, ln2_scale, ln2_bias, qkv_weight, qkv_bias, out_weight, out_bias, up_weight, up_bias, down_weight, down_bias):
    params = tuple((weight_arr.astype(jnp.float32) for weight_arr in (ln1_scale, ln1_bias, ln2_scale, ln2_bias, qkv_weight, qkv_bias, out_weight, out_bias, up_weight, up_bias, down_weight, down_bias)))
    arrived = jnp.zeros_like(cotangent).at[order].set(cotangent)
    cos_table, sin_table = rotary_tables(SEQ)

    def micro_step(totals, pair_in):
        inputs, upstream = pair_in
        start_x = inputs.astype(jnp.float32)
        shifts = tuple((jnp.zeros_like(start_x) for level_index in range(LAYERS - 1)))

        def forward(start_x, shifts, params):
            return stack_forward(start_x, shifts, params, cos_table, sin_table)
        (final_out, rounded), pullback = jax.vjp(forward, start_x, shifts, params)
        d_start, d_shifts, d_params = pullback((upstream.astype(jnp.float32), tuple((jnp.zeros_like(element) for element in rounded))))
        totals = tuple((running + increment for running, increment in zip(totals, d_params)))
        levels = jnp.stack(list(rounded) + [final_out], axis=0).astype(jnp.bfloat16)
        back_grads = jnp.stack([d_start] + list(d_shifts), axis=0).astype(jnp.bfloat16)
        return (totals, (levels, back_grads))
    zero_grads = tuple((jnp.zeros_like(weight_arr) for weight_arr in params))
    totals, (levels, back_grads) = lax.scan(micro_step, zero_grads, (layer_input, arrived))
    return (jnp.moveaxis(levels, 0, 1), jnp.moveaxis(back_grads, 0, 1), totals[0], totals[1], totals[2], totals[3], totals[4], totals[5], totals[6], totals[7], totals[8], totals[9], totals[10], totals[11])
```

```python
import functools
import jax
import jax.numpy as jnp
from jax import lax
from jax.experimental import pallas as pl
from jax.experimental.pallas import tpu as pltpu
from jax.sharding import PartitionSpec as P

MESH = pl.DeviceIdType.MESH

SLABS = 6
SLAB_ROWS = 2048
HALF = 1024
STREAM = 512
COLS = 512
CHUNK = (128, 32)
RX_ONE = (0, 768)
RX_TWO = (256, 832)
RX_ROWS = 960
SMALL = 32


def mod4(value):
    return lax.rem(value + 4, 4)


class Place:
    def __init__(self):
        self.section = lax.axis_index("section")
        self.tensor = lax.axis_index("tensor")
        dp = lax.axis_index("dp")
        self.core = lax.rem(dp, 2)
        self.x = lax.rem(dp // 2, 4)
        self.z = dp // 8

    def at(self, z, x, core):
        return (self.section, (z * 4 + x) * 2 + core, self.tensor)

    def other_core(self):
        return self.at(self.z, self.x, 1 - self.core)

    def along(self, axis, step):
        if axis == 0:
            return self.at(self.z, mod4(self.x + step), self.core)
        return self.at(mod4(self.z + step), self.x, self.core)

    def position(self, axis):
        return self.x if axis == 0 else self.z


def ds(start, size):
    return pl.ds(pl.multiple_of(start, 16), size)


def take(ref, sem):
    pltpu.make_async_copy(ref, ref, sem).wait()


def put(src, dst, send_sem, recv_sem, device):
    pltpu.make_async_remote_copy(
        src_ref=src, dst_ref=dst, send_sem=send_sem, recv_sem=recv_sem,
        device_id=device, device_id_type=MESH,
    ).start()


def added(*parts):
    total = parts[0].astype(jnp.float32)
    for part in parts[1:]:
        total = total + part.astype(jnp.float32)
    return total.astype(jnp.bfloat16)


class Reduce:
    def __init__(self, place, grads, out, arrived, landing, send, recv):
        self.place, self.grads, self.out = place, grads, out
        self.arrived, self.landing, self.send, self.recv = arrived, landing, send, recv

    def base(self, stream):
        return self.place.core * HALF + stream * STREAM

    def layout(self, stream, phase):
        axis = (stream + phase) % 2
        p = self.place.position(axis)
        start = self.base(stream)
        if phase == 1:
            start = start + self.place.position(stream) * CHUNK[0]
        return axis, p, start, CHUNK[phase]

    def first_sends(self, s, phase, sem):
        h = CHUNK[phase] // 2
        for stream in range(2):
            axis, p, start, size = self.layout(stream, phase)
            far = start + mod4(p + 2) * size
            for side, step in ((0, 1), (1, -1)):
                put(self.grads.at[s, ds(far + side * h, h)],
                    self.landing.at[s, pl.ds(RX_ONE[phase] + (stream * 2 + side) * h, h)],
                    self.send.at[s, 0], self.recv.at[s, sem], self.place.along(axis, step))

    def second_sends(self, s, phase, sem):
        h = CHUNK[phase] // 2
        take(self.landing.at[s, pl.ds(0, 4 * h)], self.recv.at[s, sem - 1])
        for stream in range(2):
            axis, p, start, size = self.layout(stream, phase)
            for side, step in ((0, 1), (1, -1)):
                near = start + mod4(p + step) * size
                rows = ds(near + side * h, h)
                came = pl.ds(RX_ONE[phase] + (stream * 2 + side) * h, h)
                self.grads[s, rows] = added(self.grads[s, rows], self.landing[s, came])
                put(self.grads.at[s, ds(near, size)],
                    self.landing.at[s, pl.ds(RX_TWO[phase] + (stream * 2 + side) * size, size)],
                    self.send.at[s, 0], self.recv.at[s, sem], self.place.along(axis, step))

    def finish(self, s, phase, sem, target):
        size = CHUNK[phase]
        take(self.landing.at[s, pl.ds(0, 4 * size)], self.recv.at[s, sem])
        for stream in range(2):
            axis, p, start, size = self.layout(stream, phase)
            rows = ds(start + p * size, size)
            left = pl.ds(RX_TWO[phase] + stream * 2 * size, size)
            right = pl.ds(RX_TWO[phase] + (stream * 2 + 1) * size, size)
            target[s, rows] = added(self.grads[s, rows], self.landing[s, left], self.landing[s, right])

    def spread(self, s, phase, sem):
        for stream in range(2):
            axis, p, start, size = self.layout(stream, phase)
            rows = ds(start + p * size, size)
            for step in (1, -1):
                put(self.out.at[s, rows], self.out.at[s, rows], self.send.at[s, 1],
                    self.recv.at[s, sem], self.place.along(axis, step))

    def forward(self, s, phase, sem):
        size = CHUNK[phase]
        take(self.out.at[s, pl.ds(0, 4 * size)], self.recv.at[s, sem - 1])
        for stream in range(2):
            axis, p, start, size = self.layout(stream, phase)
            for side, step in ((0, 1), (1, -1)):
                rows = ds(start + mod4(p - step) * size + side * (size // 2), size // 2)
                put(self.out.at[s, rows], self.out.at[s, rows], self.send.at[s, 1],
                    self.recv.at[s, sem], self.place.along(axis, step))

    def to_core(self, s, offsets):
        for stream in range(2):
            axis, p, start, size = self.layout(stream, 0)
            for offset in offsets:
                rows = ds(start + mod4(p + offset) * size, size)
                put(self.out.at[s, rows], self.out.at[s, rows], self.send.at[s, 1],
                    self.recv.at[s, 9], self.place.other_core())

    def step(self, s, k):
        core = self.place.core
        if k == 0:
            put(self.grads.at[s, ds((1 - core) * HALF, HALF)], self.arrived.at[s],
                self.send.at[s, 0], self.recv.at[s, 0], self.place.other_core())
        elif k == 1:
            take(self.arrived.at[s], self.recv.at[s, 0])

            def block(i, _):
                here = ds(core * HALF + i * 128, 128)
                self.grads[s, here] = added(self.grads[s, here], self.arrived[s, ds(i * 128, 128)])
                return 0

            lax.fori_loop(0, HALF // 128, block, 0)
            self.first_sends(s, 0, 1)
        elif k == 2:
            self.second_sends(s, 0, 2)
        elif k == 3:
            self.finish(s, 0, 2, self.grads)
            self.first_sends(s, 1, 3)
        elif k == 4:
            self.second_sends(s, 1, 4)
        elif k == 5:
            self.finish(s, 1, 4, self.out)
            self.spread(s, 1, 5)
        elif k == 6:
            self.forward(s, 1, 6)
        elif k == 7:
            take(self.out.at[s, pl.ds(0, 64)], self.recv.at[s, 6])
            self.spread(s, 0, 7)
            self.to_core(s, (0,))
        elif k == 8:
            self.forward(s, 0, 8)
            self.to_core(s, (1, -1))
        elif k == 9:
            take(self.out.at[s, pl.ds(0, 256)], self.recv.at[s, 8])
            self.to_core(s, (2,))
        elif k == 10:
            take(self.out.at[s, pl.ds(0, 1024)], self.recv.at[s, 9])

    def drain(self, s):
        take(self.grads.at[s, pl.ds(0, 1984)], self.send.at[s, 0])
        take(self.grads.at[s, pl.ds(0, 1984)], self.send.at[s, 1])


class SmallReduce:
    def __init__(self, place, mine, out, landing, pair, send, recv):
        self.place, self.mine, self.out, self.landing, self.pair = place, mine, out, landing, pair
        self.send, self.recv = send, recv

    def exchange(self, axis):
        p = self.place.position(axis)
        for step in (1, 2, 3):
            put(self.landing.at[axis, p], self.landing.at[axis, p], self.send, self.recv.at[1 + axis],
                self.place.along(axis, step))

    def collected(self, axis):
        take(self.landing.at[axis, pl.ds(0, 3)], self.recv.at[1 + axis])
        return added(*[self.landing[axis, j] for j in range(4)])

    def step(self, k):
        half = SMALL // 2
        rows = ds(self.place.core * half, half)
        if k == 0:
            put(self.mine, self.pair, self.send, self.recv.at[0], self.place.other_core())
        elif k == 1:
            take(self.pair, self.recv.at[0])
            self.landing[0, self.place.x] = added(self.mine[rows], self.pair[rows])
            self.exchange(0)
        elif k == 2:
            self.landing[1, self.place.z] = self.collected(0)
            self.exchange(1)
        elif k == 3:
            self.out[rows] = self.collected(1)
            put(self.out.at[rows], self.out.at[rows], self.send, self.recv.at[3], self.place.other_core())
        elif k == 4:
            take(self.out.at[pl.ds(0, half)], self.recv.at[3])

    def drain(self):
        half = SMALL // 2
        take(self.landing.at[0, pl.ds(0, 3)], self.send)
        take(self.landing.at[0, pl.ds(0, 3)], self.send)
        take(self.mine, self.send)
        take(self.out.at[pl.ds(0, half)], self.send)


def greet(devices):
    barrier = pltpu.get_barrier_semaphore()
    for device in devices:
        pl.semaphore_signal(barrier, inc=1, device_id=device, device_id_type=MESH)
    pl.semaphore_wait(barrier, len(devices))


def plane_partners(place):
    return [place.other_core()] + [place.along(axis, step) for axis in (0, 1) for step in (1, 2, 3)]

ORDER = (
    (0, 0), (1, 0), (2, 0), (3, 0), (4, 0), (5, 0), (0, 1), (1, 1),
    (2, 1), (0, 2), (3, 1), (1, 2), (4, 1), (2, 2), (5, 1), (0, 3),
    (3, 2), (1, 3), (4, 2), (2, 3), (5, 2), (0, 4), (3, 3), (1, 4),
    (4, 3), (2, 4), (5, 3), (0, 5), (3, 4), (1, 5), (4, 4), (2, 5),
    (5, 4), (0, 6), (3, 5), (1, 6), (4, 5), (2, 6), (5, 5), (0, 7),
    (3, 6), (1, 7), (4, 6), (2, 7), (5, 6), (0, 8), (3, 7), (1, 8),
    (4, 7), (2, 8), (5, 7), (0, 9), (3, 8), (1, 9), (4, 8), (2, 9),
    (5, 8), (3, 9), (4, 9), (5, 9),
)


def reduce_kernel(given, small_in, out, small_out, grads, arrived, landing, mine, small_landing, pair,
                  send, recv, small_send, small_recv, load):
    place = Place()
    for s in range(SLABS):
        pltpu.make_async_copy(given.at[s], grads.at[s], load.at[s]).start()
    greet(plane_partners(place))
    mine[...] = small_in[...]
    reduce = Reduce(place, grads, out, arrived, landing, send, recv)
    small = SmallReduce(place, mine, small_out, small_landing, pair, small_send, small_recv)
    small.step(0)
    small_step = 1
    for turn, (s, k) in enumerate(ORDER):
        if k == 0:
            pltpu.make_async_copy(given.at[s], grads.at[s], load.at[s]).wait()
        reduce.step(s, k)
        if turn in (12, 20, 28, 36):
            small.step(small_step)
            small_step += 1
    for s in range(SLABS):
        reduce.step(s, 10)
    for s in range(SLABS):
        reduce.drain(s)
    small.drain()


def all_reduce(grads, small):
    bf16, dma = jnp.bfloat16, pltpu.SemaphoreType.DMA
    half = SMALL // 2
    return pl.pallas_call(
        reduce_kernel,
        out_shape=(pltpu.VMEM((SLABS, SLAB_ROWS, COLS), bf16), pltpu.VMEM((SMALL, COLS), bf16)),
        in_specs=[pl.BlockSpec(memory_space=pl.ANY), pl.BlockSpec(memory_space=pltpu.VMEM)],
        out_specs=(pl.BlockSpec(memory_space=pltpu.VMEM), pl.BlockSpec(memory_space=pltpu.VMEM)),
        scratch_shapes=[
            pltpu.VMEM((SLABS, SLAB_ROWS, COLS), bf16),
            pltpu.VMEM((SLABS, HALF, COLS), bf16),
            pltpu.VMEM((SLABS, RX_ROWS, COLS), bf16),
            pltpu.VMEM((SMALL, COLS), bf16),
            pltpu.VMEM((2, 4, half, COLS), bf16),
            pltpu.VMEM((SMALL, COLS), bf16),
            dma((SLABS, 2)),
            dma((SLABS, 10)),
            dma,
            dma((4,)),
            dma((SLABS,)),
        ],
        compiler_params=pltpu.CompilerParams(
            collective_id=0, has_side_effects=True, vmem_limit_bytes=28 * 2**20
        ),
    )(grads, small)


def halves(matrix):
    return jnp.stack([matrix[:, :COLS], matrix[:, COLS:]])


def packed(totals):
    totals = [t.astype(jnp.bfloat16) for t in totals]
    qkv, out, up, down = totals[4], totals[6], totals[8], totals[10]
    up_slabs = up.reshape(1024, 4, COLS).transpose(1, 0, 2).reshape(2, SLAB_ROWS, COLS)
    qkv_part = qkv.transpose(1, 0, 2).reshape(3 * 1024, COLS)
    last = jnp.concatenate([halves(out).reshape(1024, COLS), qkv_part]).reshape(2, SLAB_ROWS, COLS)
    grads = jnp.concatenate([halves(down), up_slabs, last])
    small = jnp.concatenate([totals[i].reshape(-1) for i in (0, 1, 2, 3, 5, 7, 9)])
    small = jnp.pad(small, (0, SMALL * COLS - small.shape[0])).reshape(SMALL, COLS)
    return grads, small


def unpacked(grads, small):
    small = small.reshape(-1).astype(jnp.float32)
    down = jnp.concatenate([grads[0], grads[1]], axis=1)
    up = grads[2:4].reshape(4, 1024, COLS).transpose(1, 0, 2).reshape(1024, 4 * COLS)
    last = grads[4:6].reshape(4, 1024, COLS)
    out = last[0].reshape(2, COLS, COLS).transpose(1, 0, 2).reshape(COLS, 2 * COLS)
    qkv = last[1:].transpose(1, 0, 2)
    return (
        small[0:1024], small[1024:2048], small[2048:3072], small[3072:4096],
        qkv.astype(jnp.float32), small[4096:5632].reshape(3, COLS), out.astype(jnp.float32),
        small[5632:6656], up.astype(jnp.float32), small[6656:8704], down.astype(jnp.float32),
    )


HD = 64
ROT = 16


EPSILON = 1e-05


def passed_along(value, axis, steps):
    count = lax.axis_size(axis)
    leading, last = (max(0, -steps), min(count, count - steps))
    return lax.ppermute(value, axis, [(source, source + steps) for source in range(leading, last)])


def rotary_tables(length):
    half_rot = ROT // 2
    frequency = 1.0 / 10000.0 ** (jnp.arange(half_rot, dtype=jnp.float32) * 2.0 / ROT)
    where_at = jnp.arange(length, dtype=jnp.float32)
    angles = where_at[:, None] * frequency[None, :]
    angles = jnp.concatenate([angles, angles], axis=-1)[:, None, :]
    return (jnp.cos(angles), jnp.sin(angles))


def rotate(vector, cos_table, sin_table):
    half_rot = ROT // 2
    leading = vector[..., :ROT]
    turned = jnp.concatenate([-leading[..., half_rot:], leading[..., :half_rot]], axis=-1)
    return jnp.concatenate([leading * cos_table + turned * sin_table, vector[..., ROT:]], axis=-1)


def unrotate(vector, cos_table, sin_table):
    half_rot = ROT // 2
    leading = vector[..., :ROT]
    weighted = leading * sin_table
    turned = jnp.concatenate([weighted[..., half_rot:], -weighted[..., :half_rot]], axis=-1)
    return jnp.concatenate([leading * cos_table + turned, vector[..., ROT:]], axis=-1)


def gelu_slope(hidden):
    cdf_part = 0.5 * (1.0 + lax.erf(hidden * 0.7071067811865476))
    dens_part = jnp.exp(-0.5 * hidden * hidden) * 0.3989422804014327
    return cdf_part + hidden * dens_part


def standardize(inputs):
    centered = inputs - jnp.mean(inputs, axis=-1, keepdims=True)
    inv_std = lax.rsqrt(jnp.mean(centered * centered, axis=-1, keepdims=True) + EPSILON)
    return (centered * inv_std, inv_std)


def causal_mask(length):
    return jnp.arange(length)[:, None] >= jnp.arange(length)[None, :]


def forward_local(inputs, params, cos_table, sin_table):
    (
        scale_one,
        shift_one,
        scale_two,
        shift_two,
        qkv_w,
        qkv_b,
        out_w,
        out_b,
        up_w,
        up_b,
        down_w,
        down_b,
    ) = params
    batch_size, length = (inputs.shape[0], inputs.shape[1])
    head_count = qkv_w.shape[2] // HD
    normed, inv_std = standardize(inputs)
    first_in = (normed * scale_one.astype(jnp.float32) + shift_one.astype(jnp.float32)).astype(
        jnp.bfloat16
    )
    second_in = (normed * scale_two.astype(jnp.float32) + shift_two.astype(jnp.float32)).astype(
        jnp.bfloat16
    )
    projected = jnp.einsum(
        "bsd,dtc->bstc", first_in, qkv_w, preferred_element_type=jnp.float32
    ) + qkv_b.astype(jnp.float32)
    projected = projected.reshape(batch_size, length, 3, head_count, HD)
    queries = (rotate(projected[:, :, 0], cos_table, sin_table) * HD ** (-0.5)).astype(jnp.bfloat16)
    key_vecs = rotate(projected[:, :, 1], cos_table, sin_table).astype(jnp.bfloat16)
    values = projected[:, :, 2].astype(jnp.bfloat16)
    scores = jnp.einsum("bqhe,bkhe->bhqk", queries, key_vecs, preferred_element_type=jnp.float32)
    scores = jnp.where(causal_mask(length), scores, -1e30)
    row_max = jnp.max(scores, axis=-1, keepdims=True)
    exp_scores = jnp.exp(scores - row_max)
    row_total = jnp.sum(exp_scores, axis=-1, keepdims=True)
    attn_probs = (exp_scores / row_total).astype(jnp.bfloat16)
    log_total = (row_max + jnp.log(row_total))[..., 0]
    context = jnp.einsum("bhqk,bkhe->bqhe", attn_probs, values, preferred_element_type=jnp.float32)
    context = context.astype(jnp.bfloat16).reshape(batch_size, length, head_count * HD)
    hidden = jnp.einsum(
        "bsd,df->bsf", second_in, up_w, preferred_element_type=jnp.float32
    ) + up_b.astype(jnp.float32)
    activated = jax.nn.gelu(hidden, approximate=False).astype(jnp.bfloat16)
    branch_sum = jnp.einsum("bsh,hd->bsd", context, out_w, preferred_element_type=jnp.float32)
    branch_sum = branch_sum + jnp.einsum(
        "bsf,fd->bsd", activated, down_w, preferred_element_type=jnp.float32
    )
    saved = (
        normed,
        inv_std,
        first_in,
        second_in,
        queries.reshape(batch_size, length, head_count * HD),
        key_vecs.reshape(batch_size, length, head_count * HD),
        values.reshape(batch_size, length, head_count * HD),
        log_total,
        context,
        hidden,
        activated,
    )
    return (branch_sum, saved)


def backward_local(upstream, saved, params, cos_table, sin_table):
    (
        normed,
        inv_std,
        first_in,
        second_in,
        queries,
        key_vecs,
        values,
        log_total,
        context,
        hidden,
        activated,
    ) = saved
    (
        scale_one,
        shift_one,
        scale_two,
        shift_two,
        qkv_w,
        qkv_b,
        out_w,
        out_b,
        up_w,
        up_b,
        down_w,
        down_b,
    ) = params
    batch_size, length = (upstream.shape[0], upstream.shape[1])
    head_count = qkv_w.shape[2] // HD
    d_bias_out = jnp.sum(upstream.astype(jnp.float32), axis=(0, 1))
    d_out_w = jnp.einsum("bsh,bsd->hd", context, upstream, preferred_element_type=jnp.float32)
    d_down_w = jnp.einsum("bsf,bsd->fd", activated, upstream, preferred_element_type=jnp.float32)
    d_context = jnp.einsum("bsd,hd->bsh", upstream, out_w, preferred_element_type=jnp.float32)
    d_context = d_context.astype(jnp.bfloat16).reshape(batch_size, length, head_count, HD)
    d_active = jnp.einsum("bsd,fd->bsf", upstream, down_w, preferred_element_type=jnp.float32)
    d_hidden = (d_active * gelu_slope(hidden)).astype(jnp.bfloat16)
    d_up_b = jnp.sum(d_hidden.astype(jnp.float32), axis=(0, 1))
    d_up_w = jnp.einsum("bsd,bsf->df", second_in, d_hidden, preferred_element_type=jnp.float32)
    d_second = jnp.einsum("bsf,df->bsd", d_hidden, up_w, preferred_element_type=jnp.float32)
    query_heads = queries.reshape(batch_size, length, head_count, HD)
    key_heads = key_vecs.reshape(batch_size, length, head_count, HD)
    value_heads = values.reshape(batch_size, length, head_count, HD)
    scores = jnp.einsum(
        "bqhe,bkhe->bhqk", query_heads, key_heads, preferred_element_type=jnp.float32
    )
    attn_probs = jnp.where(causal_mask(length), jnp.exp(scores - log_total[..., None]), 0.0)
    d_values = jnp.einsum(
        "bhqk,bqhe->bkhe",
        attn_probs.astype(jnp.bfloat16),
        d_context,
        preferred_element_type=jnp.float32,
    )
    d_probs = jnp.einsum(
        "bqhe,bkhe->bhqk", d_context, value_heads, preferred_element_type=jnp.float32
    )
    inner_sum = jnp.sum(d_probs * attn_probs, axis=-1, keepdims=True)
    d_scores = (attn_probs * (d_probs - inner_sum)).astype(jnp.bfloat16)
    d_queries = jnp.einsum(
        "bhqk,bkhe->bqhe", d_scores, key_heads, preferred_element_type=jnp.float32
    )
    d_keys = jnp.einsum(
        "bhqk,bqhe->bkhe", d_scores, query_heads, preferred_element_type=jnp.float32
    )
    d_projected = jnp.stack(
        [
            unrotate(d_queries * HD ** (-0.5), cos_table, sin_table),
            unrotate(d_keys, cos_table, sin_table),
            d_values,
        ],
        axis=2,
    )
    d_projected = d_projected.reshape(batch_size, length, 3, head_count * HD).astype(jnp.bfloat16)
    d_qkv_b = jnp.sum(d_projected.astype(jnp.float32), axis=(0, 1))
    d_qkv_w = jnp.einsum("bsd,bstc->dtc", first_in, d_projected, preferred_element_type=jnp.float32)
    d_first = jnp.einsum("bstc,dtc->bsd", d_projected, qkv_w, preferred_element_type=jnp.float32)
    return ((d_qkv_w, d_qkv_b, d_out_w, d_bias_out, d_up_w, d_up_b, d_down_w), (d_first, d_second))


def put_slot(stored, index, value, is_valid):
    previous = lax.dynamic_index_in_dim(stored, index, 0, keepdims=False)
    return lax.dynamic_update_index_in_dim(stored, jnp.where(is_valid, value, previous), index, 0)


def shards(
    layer_input,
    cotangent,
    order,
    ln1_scale,
    ln1_bias,
    ln2_scale,
    ln2_bias,
    qkv_weight,
    qkv_bias,
    out_weight,
    out_bias,
    up_weight,
    up_bias,
    down_weight,
    down_bias,
):
    section_count = lax.axis_size("section")
    section_index = lax.axis_index("section")
    params = tuple(
        (
            entry[0]
            for entry in (
                ln1_scale,
                ln1_bias,
                ln2_scale,
                ln2_bias,
                qkv_weight,
                qkv_bias,
                out_weight,
                out_bias,
                up_weight,
                up_bias,
                down_weight,
                down_bias,
            )
        )
    )
    micro_count = layer_input.shape[0]
    batch_size, length, width = (layer_input.shape[1], layer_input.shape[2], layer_input.shape[3])
    head_width = qkv_weight.shape[3]
    hidden_width = up_weight.shape[2]
    head_count = head_width // HD
    cos_table, sin_table = rotary_tables(length)
    tick_count = micro_count + section_count - 1
    bias_sum = params[7].astype(jnp.float32) + params[11].astype(jnp.float32)

    def forward_tick(tick, carry):
        arriving, stored, out_store = carry
        slot_index = tick - section_index
        is_valid = (slot_index >= 0) & (slot_index < micro_count)
        clipped = jnp.clip(slot_index, 0, micro_count - 1)
        chosen = order[clipped]
        first_input = lax.dynamic_index_in_dim(layer_input, chosen, 0, keepdims=False)
        current = jnp.where(section_index == 0, first_input, arriving)
        branch_sum, saved = forward_local(current.astype(jnp.float32), params, cos_table, sin_table)
        summed = lax.psum(branch_sum, "tensor")
        result = (current.astype(jnp.float32) + summed + bias_sum).astype(jnp.bfloat16)
        stored = tuple(
            (put_slot(entry, clipped, value, is_valid) for entry, value in zip(stored, saved))
        )
        out_store = put_slot(out_store, chosen, result, is_valid)
        arriving = passed_along(result, "section", 1)
        return (arriving, stored, out_store)

    stored = (
        jnp.zeros((micro_count, batch_size, length, width), jnp.float32),
        jnp.zeros((micro_count, batch_size, length, 1), jnp.float32),
        jnp.zeros((micro_count, batch_size, length, width), jnp.bfloat16),
        jnp.zeros((micro_count, batch_size, length, width), jnp.bfloat16),
        jnp.zeros((micro_count, batch_size, length, head_width), jnp.bfloat16),
        jnp.zeros((micro_count, batch_size, length, head_width), jnp.bfloat16),
        jnp.zeros((micro_count, batch_size, length, head_width), jnp.bfloat16),
        jnp.zeros((micro_count, batch_size, head_count, length), jnp.float32),
        jnp.zeros((micro_count, batch_size, length, head_width), jnp.bfloat16),
        jnp.zeros((micro_count, batch_size, length, hidden_width), jnp.float32),
        jnp.zeros((micro_count, batch_size, length, hidden_width), jnp.bfloat16),
    )
    empty_rows = jnp.zeros((batch_size, length, width), jnp.bfloat16)
    out_store = jnp.zeros((micro_count, batch_size, length, width), jnp.bfloat16)
    arriving, stored, out_store = lax.fori_loop(
        0, tick_count, forward_tick, (empty_rows, stored, out_store)
    )

    def backward_tick(tick, carry):
        arriving, totals, grad_store = carry
        slot_index = tick - (section_count - 1 - section_index)
        is_valid = (slot_index >= 0) & (slot_index < micro_count)
        clipped = jnp.clip(slot_index, 0, micro_count - 1)
        chosen = order[clipped]
        given = lax.dynamic_index_in_dim(cotangent, clipped, 0, keepdims=False)
        upstream = jnp.where(section_index == section_count - 1, given, arriving)
        saved = tuple(
            (lax.dynamic_index_in_dim(entry, clipped, 0, keepdims=False) for entry in stored)
        )
        layer_grads, (d_first, d_second) = backward_local(
            upstream, saved, params, cos_table, sin_table
        )
        d_first, d_second = (
            lax.psum(d_first.astype(jnp.bfloat16), "tensor").astype(jnp.float32),
            lax.psum(d_second.astype(jnp.bfloat16), "tensor").astype(jnp.float32),
        )
        normed, inv_std = (saved[0], saved[1])
        norm_part = (
            jnp.sum(d_first * normed, axis=(0, 1)),
            jnp.sum(d_first, axis=(0, 1)),
            jnp.sum(d_second * normed, axis=(0, 1)),
            jnp.sum(d_second, axis=(0, 1)),
        )
        d_normed = d_first * params[0].astype(jnp.float32) + d_second * params[2].astype(
            jnp.float32
        )
        centered_grad = (
            d_normed
            - jnp.mean(d_normed, axis=-1, keepdims=True)
            - normed * jnp.mean(d_normed * normed, axis=-1, keepdims=True)
        )
        to_send = (upstream.astype(jnp.float32) + inv_std * centered_grad).astype(jnp.bfloat16)
        tick_part = tuple(
            (jnp.where(is_valid, grad_part, 0.0) for grad_part in norm_part + layer_grads)
        )
        totals = tuple((running + increment for running, increment in zip(totals, tick_part)))
        grad_store = put_slot(grad_store, chosen, to_send, is_valid)
        arriving = passed_along(to_send, "section", -1)
        return (arriving, totals, grad_store)

    zero_grads = (
        jnp.zeros((width,), jnp.float32),
        jnp.zeros((width,), jnp.float32),
        jnp.zeros((width,), jnp.float32),
        jnp.zeros((width,), jnp.float32),
        jnp.zeros((width, 3, head_width), jnp.float32),
        jnp.zeros((3, head_width), jnp.float32),
        jnp.zeros((head_width, width), jnp.float32),
        jnp.zeros((width,), jnp.float32),
        jnp.zeros((width, hidden_width), jnp.float32),
        jnp.zeros((hidden_width,), jnp.float32),
        jnp.zeros((hidden_width, width), jnp.float32),
    )
    grad_store = jnp.zeros((micro_count, batch_size, length, width), jnp.bfloat16)
    arriving, totals, grad_store = lax.fori_loop(
        0, tick_count, backward_tick, (empty_rows, zero_grads, grad_store)
    )
    totals = unpacked(*all_reduce(*packed(totals)))
    return (
        out_store[None],
        grad_store[None],
        totals[0][None],
        totals[1][None],
        totals[2][None],
        totals[3][None],
        totals[4][None],
        totals[5][None],
        totals[6][None],
        totals[7][None],
        totals[8][None],
        totals[9][None],
        totals[10][None],
        totals[7][None],
    )


def solution(mesh):
    return jax.shard_map(
        shards,
        mesh=mesh,
        in_specs=(
            P(None, "dp", None, None),
            P(None, "dp", None, None),
            P(),
            P("section", None),
            P("section", None),
            P("section", None),
            P("section", None),
            P("section", None, None, "tensor"),
            P("section", None, "tensor"),
            P("section", "tensor", None),
            P("section", None),
            P("section", None, "tensor"),
            P("section", "tensor"),
            P("section", "tensor", None),
            P("section", None),
        ),
        out_specs=(
            P("section", None, "dp", None, None),
            P("section", None, "dp", None, None),
            P("section", None),
            P("section", None),
            P("section", None),
            P("section", None),
            P("section", None, None, "tensor"),
            P("section", None, "tensor"),
            P("section", "tensor", None),
            P("section", None),
            P("section", None, "tensor"),
            P("section", "tensor"),
            P("section", "tensor", None),
            P("section", None),
        ),
        check_vma=False,
    )
```

```python
import jax
import jax.numpy as jnp
import numpy as np
from jax import lax
from jax.experimental import pallas as pl
from jax.experimental.pallas import tpu as pltpu
from jax.sharding import PartitionSpec as P

MESH = pl.DeviceIdType.MESH
VMEM_LIMIT = 51 * 2**20

SLABS = 6
SLAB_ROWS = 2048
HALF = 1024
STREAM = 512
COLS = 512
CHUNK = (128, 32)
RX_ONE = (0, 768)
RX_TWO = (256, 832)
RX_ROWS = 960
SMALL = 32


def mod4(value):
    return lax.rem(value + 4, 4)


class Place:
    def __init__(self):
        self.section = lax.axis_index("section")
        self.tensor = lax.axis_index("tensor")
        dp = lax.axis_index("dp")
        self.core = lax.rem(dp, 2)
        self.x = lax.rem(dp // 2, 4)
        self.z = dp // 8

    def at(self, z, x, core):
        return (self.section, (z * 4 + x) * 2 + core, self.tensor)

    def other_core(self):
        return self.at(self.z, self.x, 1 - self.core)

    def along(self, axis, step):
        if axis == 0:
            return self.at(self.z, mod4(self.x + step), self.core)
        return self.at(mod4(self.z + step), self.x, self.core)

    def position(self, axis):
        return self.x if axis == 0 else self.z


def ds(start, size):
    return pl.ds(pl.multiple_of(start, 16), size)


def take(ref, sem):
    pltpu.make_async_copy(ref, ref, sem).wait()


def put(src, dst, send_sem, recv_sem, device):
    pltpu.make_async_remote_copy(
        src_ref=src, dst_ref=dst, send_sem=send_sem, recv_sem=recv_sem,
        device_id=device, device_id_type=MESH,
    ).start()


def added(*parts):
    total = parts[0].astype(jnp.float32)
    for part in parts[1:]:
        total = total + part.astype(jnp.float32)
    return total.astype(jnp.bfloat16)


class Reduce:
    def __init__(self, place, grads, out, arrived, landing, send, recv):
        self.place, self.grads, self.out = place, grads, out
        self.arrived, self.landing, self.send, self.recv = arrived, landing, send, recv

    def base(self, stream):
        return self.place.core * HALF + stream * STREAM

    def layout(self, stream, phase):
        axis = (stream + phase) % 2
        p = self.place.position(axis)
        start = self.base(stream)
        if phase == 1:
            start = start + self.place.position(stream) * CHUNK[0]
        return axis, p, start, CHUNK[phase]

    def first_sends(self, s, phase, sem):
        h = CHUNK[phase] // 2
        for stream in range(2):
            axis, p, start, size = self.layout(stream, phase)
            far = start + mod4(p + 2) * size
            for side, step in ((0, 1), (1, -1)):
                put(self.grads.at[s, ds(far + side * h, h)],
                    self.landing.at[s, pl.ds(RX_ONE[phase] + (stream * 2 + side) * h, h)],
                    self.send.at[s, 0], self.recv.at[s, sem], self.place.along(axis, step))

    def second_sends(self, s, phase, sem):
        h = CHUNK[phase] // 2
        take(self.landing.at[s, pl.ds(0, 4 * h)], self.recv.at[s, sem - 1])
        for stream in range(2):
            axis, p, start, size = self.layout(stream, phase)
            for side, step in ((0, 1), (1, -1)):
                near = start + mod4(p + step) * size
                rows = ds(near + side * h, h)
                came = pl.ds(RX_ONE[phase] + (stream * 2 + side) * h, h)
                self.grads[s, rows] = added(self.grads[s, rows], self.landing[s, came])
                put(self.grads.at[s, ds(near, size)],
                    self.landing.at[s, pl.ds(RX_TWO[phase] + (stream * 2 + side) * size, size)],
                    self.send.at[s, 0], self.recv.at[s, sem], self.place.along(axis, step))

    def finish(self, s, phase, sem, target):
        size = CHUNK[phase]
        take(self.landing.at[s, pl.ds(0, 4 * size)], self.recv.at[s, sem])
        for stream in range(2):
            axis, p, start, size = self.layout(stream, phase)
            rows = ds(start + p * size, size)
            left = pl.ds(RX_TWO[phase] + stream * 2 * size, size)
            right = pl.ds(RX_TWO[phase] + (stream * 2 + 1) * size, size)
            target[s, rows] = added(self.grads[s, rows], self.landing[s, left], self.landing[s, right])

    def spread(self, s, phase, sem):
        for stream in range(2):
            axis, p, start, size = self.layout(stream, phase)
            rows = ds(start + p * size, size)
            for step in (1, -1):
                put(self.out.at[s, rows], self.out.at[s, rows], self.send.at[s, 1],
                    self.recv.at[s, sem], self.place.along(axis, step))

    def forward(self, s, phase, sem):
        size = CHUNK[phase]
        take(self.out.at[s, pl.ds(0, 4 * size)], self.recv.at[s, sem - 1])
        for stream in range(2):
            axis, p, start, size = self.layout(stream, phase)
            for side, step in ((0, 1), (1, -1)):
                rows = ds(start + mod4(p - step) * size + side * (size // 2), size // 2)
                put(self.out.at[s, rows], self.out.at[s, rows], self.send.at[s, 1],
                    self.recv.at[s, sem], self.place.along(axis, step))

    def to_core(self, s, offsets):
        for stream in range(2):
            axis, p, start, size = self.layout(stream, 0)
            for offset in offsets:
                rows = ds(start + mod4(p + offset) * size, size)
                put(self.out.at[s, rows], self.out.at[s, rows], self.send.at[s, 1],
                    self.recv.at[s, 9], self.place.other_core())

    def step(self, s, k):
        core = self.place.core
        if k == 0:
            put(self.grads.at[s, ds((1 - core) * HALF, HALF)], self.arrived.at[s],
                self.send.at[s, 0], self.recv.at[s, 0], self.place.other_core())
        elif k == 1:
            take(self.arrived.at[s], self.recv.at[s, 0])

            def block(i, _):
                here = ds(core * HALF + i * 128, 128)
                self.grads[s, here] = added(self.grads[s, here], self.arrived[s, ds(i * 128, 128)])
                return 0

            lax.fori_loop(0, HALF // 128, block, 0)
            self.first_sends(s, 0, 1)
        elif k == 2:
            self.second_sends(s, 0, 2)
        elif k == 3:
            self.finish(s, 0, 2, self.grads)
            self.first_sends(s, 1, 3)
        elif k == 4:
            self.second_sends(s, 1, 4)
        elif k == 5:
            self.finish(s, 1, 4, self.out)
            self.spread(s, 1, 5)
        elif k == 6:
            self.forward(s, 1, 6)
        elif k == 7:
            take(self.out.at[s, pl.ds(0, 64)], self.recv.at[s, 6])
            self.spread(s, 0, 7)
            self.to_core(s, (0,))
        elif k == 8:
            self.forward(s, 0, 8)
            self.to_core(s, (1, -1))
        elif k == 9:
            take(self.out.at[s, pl.ds(0, 256)], self.recv.at[s, 8])
            self.to_core(s, (2,))
        elif k == 10:
            take(self.out.at[s, pl.ds(0, 1024)], self.recv.at[s, 9])

    def drain(self, s):
        take(self.grads.at[s, pl.ds(0, 1984)], self.send.at[s, 0])
        take(self.grads.at[s, pl.ds(0, 1984)], self.send.at[s, 1])


class SmallReduce:
    def __init__(self, place, mine, out, landing, pair, send, recv):
        self.place, self.mine, self.out, self.landing, self.pair = place, mine, out, landing, pair
        self.send, self.recv = send, recv

    def exchange(self, axis):
        p = self.place.position(axis)
        for step in (1, 2, 3):
            put(self.landing.at[axis, p], self.landing.at[axis, p], self.send, self.recv.at[1 + axis],
                self.place.along(axis, step))

    def collected(self, axis):
        take(self.landing.at[axis, pl.ds(0, 3)], self.recv.at[1 + axis])
        return added(*[self.landing[axis, j] for j in range(4)])

    def step(self, k):
        half = SMALL // 2
        rows = ds(self.place.core * half, half)
        if k == 0:
            put(self.mine, self.pair, self.send, self.recv.at[0], self.place.other_core())
        elif k == 1:
            take(self.pair, self.recv.at[0])
            self.landing[0, self.place.x] = added(self.mine[rows], self.pair[rows])
            self.exchange(0)
        elif k == 2:
            self.landing[1, self.place.z] = self.collected(0)
            self.exchange(1)
        elif k == 3:
            self.out[rows] = self.collected(1)
            put(self.out.at[rows], self.out.at[rows], self.send, self.recv.at[3], self.place.other_core())
        elif k == 4:
            take(self.out.at[pl.ds(0, half)], self.recv.at[3])

    def drain(self):
        half = SMALL // 2
        take(self.landing.at[0, pl.ds(0, 3)], self.send)
        take(self.landing.at[0, pl.ds(0, 3)], self.send)
        take(self.mine, self.send)
        take(self.out.at[pl.ds(0, half)], self.send)


def greet(devices):
    barrier = pltpu.get_barrier_semaphore()
    for device in devices:
        pl.semaphore_signal(barrier, inc=1, device_id=device, device_id_type=MESH)
    pl.semaphore_wait(barrier, len(devices))


def plane_partners(place):
    return [place.other_core()] + [place.along(axis, step) for axis in (0, 1) for step in (1, 2, 3)]


ORDER = (
    (0, 0), (1, 0), (2, 0), (3, 0), (4, 0), (5, 0), (0, 1), (1, 1),
    (2, 1), (0, 2), (3, 1), (1, 2), (4, 1), (2, 2), (5, 1), (0, 3),
    (3, 2), (1, 3), (4, 2), (2, 3), (5, 2), (0, 4), (3, 3), (1, 4),
    (4, 3), (2, 4), (5, 3), (0, 5), (3, 4), (1, 5), (4, 4), (2, 5),
    (5, 4), (0, 6), (3, 5), (1, 6), (4, 5), (2, 6), (5, 5), (0, 7),
    (3, 6), (1, 7), (4, 6), (2, 7), (5, 6), (0, 8), (3, 7), (1, 8),
    (4, 7), (2, 8), (5, 7), (0, 9), (3, 8), (1, 9), (4, 8), (2, 9),
    (5, 8), (3, 9), (4, 9), (5, 9),
)

SEQ = 256
TOKENS = 2 * SEQ
OWN = SEQ // 2
WIDTH = 1024
HEAD = 64
ROT = 16
EPSILON = 1e-05
BF16 = jnp.bfloat16
F32 = jnp.float32


def nn(a, b):
    return lax.dot_general(a, b, (((1,), (0,)), ((), ())), preferred_element_type=F32)


def nt(a, b):
    return lax.dot_general(a, b, (((1,), (1,)), ((), ())), preferred_element_type=F32)


def tn(a, b):
    return lax.dot_general(a, b, (((0,), (0,)), ((), ())), preferred_element_type=F32)


def wide(ref):
    return ref[...].astype(F32)


def block(index, size):
    return pl.ds(pl.multiple_of(index * size, size), size)


def rotary_tables():
    frequency = (1.0 / 10000.0 ** (np.arange(ROT // 2) * 2.0 / ROT)).astype(np.float32)
    angles = np.arange(SEQ, dtype=np.float32)[:, None] * frequency[None, :]
    cos, sin = np.cos(angles), np.sin(angles)
    cos_table = np.ones((SEQ, 128), np.float32)
    low_sin, high_sin = np.zeros((SEQ, 128), np.float32), np.zeros((SEQ, 128), np.float32)
    for head in range(128 // HEAD):
        first, second = head * HEAD, head * HEAD + ROT // 2
        cos_table[:, first:second] = cos
        cos_table[:, second:second + ROT // 2] = cos
        low_sin[:, first:second] = sin
        high_sin[:, second:second + ROT // 2] = sin
    return cos_table, low_sin, high_sin


def rotated(u, tables, sign):
    cos, low_sin, high_sin = tables
    ahead = pltpu.roll(u, 128 - ROT // 2, 1)
    behind = pltpu.roll(u, ROT // 2, 1)
    return u * cos + (behind * high_sin - ahead * low_sin) * sign


class Layer:
    def __init__(self, refs):
        self.__dict__.update(refs)

    def up_block(self, n, rows):
        return self.out.at[4 + n // 2, pl.ds((n % 2) * WIDTH + rows[0], rows[1])]

    def norm(self, m):
        rows = block(m, SEQ)
        x = wide(self.x.at[rows])
        mean = jnp.mean(x, axis=1, keepdims=True)
        centered = x - mean
        rstd = lax.rsqrt(jnp.mean(centered * centered, axis=1, keepdims=True) + EPSILON)
        normed = centered * rstd
        self.mean[rows] = mean
        self.rstd[rows] = rstd
        self.first_in[rows] = (normed * wide(self.ln1_scale) + wide(self.ln1_bias)).astype(BF16)
        self.second_in[rows] = (normed * wide(self.ln2_scale) + wide(self.ln2_bias)).astype(BF16)

    def project(self, m):
        rows = block(m, SEQ)
        tables = (self.cos[...], self.low_sin[...], self.high_sin[...])
        bias = wide(self.qkv_bias)
        for t in range(3):
            part = nn(self.first_in[rows], self.qkv_w[t]) + bias[t:t + 1]
            for lane in range(0, COLS, 128):
                piece = part[:, lane:lane + 128]
                if t < 2:
                    piece = rotated(piece, tables, 1.0)
                if t == 0:
                    piece = piece * HEAD ** -0.5
                self.qkv[t, rows, pl.ds(lane, 128)] = piece.astype(BF16)

    def attend(self, m):
        rows = block(m, SEQ)
        causal = (lax.broadcasted_iota(jnp.int32, (SEQ, SEQ), 0)
                  >= lax.broadcasted_iota(jnp.int32, (SEQ, SEQ), 1))
        lane = lax.broadcasted_iota(jnp.int32, (SEQ, 128), 1)

        def pair(hp, _):
            lanes = block(hp, 128)
            q, k, v = (self.qkv[t, rows, lanes] for t in range(3))
            context = None
            for h in range(2):
                keep = (lane < HEAD) if h == 0 else (lane >= HEAD)
                zero = jnp.zeros_like(q)
                scores = jnp.where(causal, nt(jnp.where(keep, q, zero), k), -1e30)
                exp = jnp.exp(scores - jnp.max(scores, axis=1, keepdims=True))
                probs = (exp * (1.0 / jnp.sum(exp, axis=1, keepdims=True))).astype(BF16)
                self.probs[m, hp * 2 + h] = probs
                part = nn(probs, jnp.where(keep, v, zero))
                context = part if context is None else context + part
            self.context[rows, lanes] = context.astype(BF16)
            return 0

        lax.fori_loop(0, 4, pair, 0)

    def up(self, m):
        rows = block(m, SEQ)
        bias = wide(self.up_bias)
        for n in range(4):
            hidden = nn(self.second_in[rows], self.up_block(n, (0, WIDTH))[...])
            hidden = hidden + bias[:, n * COLS:(n + 1) * COLS]
            cdf = 0.5 * (1.0 + lax.erf(hidden * 0.7071067811865476))
            density = jnp.exp(-0.5 * hidden * hidden) * 0.3989422804014327
            lanes = pl.ds(n * COLS, COLS)
            self.activated[rows, lanes] = (hidden * cdf).astype(BF16)
            self.slope[rows, lanes] = (cdf + hidden * density).astype(BF16)

    def branches(self, m):
        rows = block(m, SEQ)
        for j in range(2):
            lanes = pl.ds(j * COLS, COLS)
            total = nn(self.context[rows], self.out_w[:, lanes])
            total = total + nn(self.activated[rows], self.out[2 + j])
            self.partial[m, :, lanes] = total.astype(BF16)

    def back_branches(self, m):
        rows = block(m, SEQ)
        upstream = self.upstream[rows]
        self.d_context[rows] = nt(upstream, self.out_w[...]).astype(BF16)
        for n in range(4):
            down = pl.ds(n * COLS, COLS)
            part = nt(upstream[:, :COLS], self.out[2, down]) + nt(upstream[:, COLS:], self.out[3, down])
            self.d_hidden[rows, down] = part.astype(BF16)

    def back_gelu(self, m):
        rows = block(m, SEQ)
        for n in range(4):
            lanes = pl.ds(n * COLS, COLS)
            self.d_hidden[rows, lanes] = (
                wide(self.d_hidden.at[rows, lanes]) * wide(self.slope.at[rows, lanes])
            ).astype(BF16)

    def back_attend(self, m):
        rows = block(m, SEQ)
        lane = lax.broadcasted_iota(jnp.int32, (SEQ, 128), 1)
        tables = (self.cos[...], self.low_sin[...], self.high_sin[...])

        def pair(hp, _):
            lanes = block(hp, 128)
            q, k, v = (self.qkv[t, rows, lanes] for t in range(3))
            d_context = self.d_context[rows, lanes]
            totals = [None, None, None]
            for h in range(2):
                keep = (lane < HEAD) if h == 0 else (lane >= HEAD)
                zero = jnp.zeros_like(q)
                d_mine = jnp.where(keep, d_context, zero)
                probs = self.probs[m, hp * 2 + h]
                wide_probs = probs.astype(F32)
                d_probs = nt(d_mine, v)
                inner = jnp.sum(d_probs * wide_probs, axis=1, keepdims=True)
                d_scores = (wide_probs * (d_probs - inner)).astype(BF16)
                parts = (nn(d_scores, jnp.where(keep, k, zero)),
                         tn(d_scores, jnp.where(keep, q, zero)),
                         tn(probs, d_mine))
                totals = [b if a is None else a + b for a, b in zip(totals, parts)]
            d_query = rotated(totals[0] * HEAD ** -0.5, tables, -1.0)
            d_key = rotated(totals[1], tables, -1.0)
            for t, part in enumerate((d_query, d_key, totals[2])):
                self.d_projected[t, rows, lanes] = part.astype(BF16)
            return 0

        lax.fori_loop(0, 4, pair, 0)

    def back_inputs(self, m):
        rows = block(m, SEQ)
        mean, rstd = self.mean[rows], self.rstd[rows]
        for j in range(2):
            lanes = pl.ds(j * COLS, COLS)
            d_second = None
            for n in range(4):
                part = nt(self.d_hidden[rows, pl.ds(n * COLS, COLS)], self.up_block(n, (j * COLS, COLS))[...])
                d_second = part if d_second is None else d_second + part
            d_first = None
            for t in range(3):
                part = nt(self.d_projected[t, rows], self.qkv_w[t, lanes])
                d_first = part if d_first is None else d_first + part
            normed = (wide(self.x.at[rows, lanes]) - mean) * rstd
            sums = (d_first * normed, d_first, d_second * normed, d_second)
            for i, value in enumerate(sums):
                row = pl.ds(2 * i + j, 1)
                self.vectors[row] = self.vectors[row] + jnp.sum(value, axis=0, keepdims=True)
            d_normed = d_first * wide(self.ln1_scale.at[:, lanes]) + d_second * wide(self.ln2_scale.at[:, lanes])
            self.partial[m, :, lanes] = d_normed.astype(BF16)

    def weight_sums(self, grads):
        def down(i, _):
            c, r = i // 4, lax.rem(i, 4)
            grads[c, block(r, COLS)] = tn(
                self.activated[:, block(r, COLS)], self.upstream[:, block(c, COLS)]).astype(BF16)
            return 0

        def out(c, _):
            grads[4, block(c, COLS)] = tn(self.context[...], self.upstream[:, block(c, COLS)]).astype(BF16)
            return 0

        def up(i, _):
            n, r = i // 2, lax.rem(i, 2)
            grads[2 + n // 2, block(lax.rem(n, 2) * 2 + r, COLS)] = tn(
                self.second_in[:, block(r, COLS)], self.d_hidden[:, block(n, COLS)]).astype(BF16)
            return 0

        def qkv(i, _):
            t, r = i // 2, lax.rem(i, 2)
            row = i + 2
            grads[4 + row // 4, block(lax.rem(row, 4), COLS)] = tn(
                self.first_in[:, block(r, COLS)], self.d_projected[t]).astype(BF16)
            return 0

        return down, out, up, qkv

    def bias_sums(self):
        for t in range(3):
            self.vectors[pl.ds(8 + t, 1)] = jnp.sum(wide(self.d_projected.at[t]), axis=0, keepdims=True)
        for j in range(2):
            lanes = pl.ds(j * COLS, COLS)
            self.vectors[pl.ds(11 + j, 1)] = jnp.sum(wide(self.upstream.at[:, lanes]), axis=0, keepdims=True)
        for n in range(4):
            lanes = pl.ds(n * COLS, COLS)
            self.vectors[pl.ds(13 + n, 1)] = jnp.sum(wide(self.d_hidden.at[:, lanes]), axis=0, keepdims=True)


INPUTS = ("x_in", "cot_in", "order", "ln1_scale", "ln1_bias", "ln2_scale", "ln2_bias", "qkv_in", "qkv_bias",
          "out_in", "out_bias", "up_in", "up_bias", "down_in", "down_bias", "cos", "low_sin", "high_sin")
IN_HBM = ("x_in", "cot_in", "qkv_in", "out_in", "up_in", "down_in")
OUTPUTS = ("y_out", "g_out", "out", "small_out")
DMA = pltpu.SemaphoreType.DMA
SCRATCH = dict(
    grads=pltpu.VMEM((SLABS, SLAB_ROWS, COLS), BF16),
    arrived=pltpu.VMEM((SLABS, HALF, COLS), BF16),
    landing=pltpu.VMEM((SLABS, RX_ROWS, COLS), BF16),
    x=pltpu.VMEM((TOKENS, WIDTH), BF16),
    upstream=pltpu.VMEM((TOKENS, WIDTH), BF16),
    first_in=pltpu.VMEM((TOKENS, WIDTH), BF16),
    second_in=pltpu.VMEM((TOKENS, WIDTH), BF16),
    qkv=pltpu.VMEM((3, TOKENS, COLS), BF16),
    d_projected=pltpu.VMEM((3, TOKENS, COLS), BF16),
    context=pltpu.VMEM((TOKENS, COLS), BF16),
    d_context=pltpu.VMEM((TOKENS, COLS), BF16),
    probs=pltpu.VMEM((2, 8, SEQ, SEQ), BF16),
    activated=pltpu.VMEM((TOKENS, 4 * COLS), BF16),
    slope=pltpu.VMEM((TOKENS, 4 * COLS), BF16),
    d_hidden=pltpu.VMEM((TOKENS, 4 * COLS), BF16),
    partial=pltpu.VMEM((2, SEQ, WIDTH), BF16),
    came=pltpu.VMEM((2, 2, OWN, WIDTH), BF16),
    mine=pltpu.VMEM((2, 2, OWN, WIDTH), BF16),
    mean=pltpu.VMEM((TOKENS, 1), F32),
    rstd=pltpu.VMEM((TOKENS, 1), F32),
    vectors=pltpu.VMEM((SMALL, COLS), F32),
    qkv_w=pltpu.VMEM((3, WIDTH, COLS), BF16),
    out_w=pltpu.VMEM((COLS, WIDTH), BF16),
    small_mine=pltpu.VMEM((SMALL, COLS), BF16),
    small_landing=pltpu.VMEM((2, 4, SMALL // 2, COLS), BF16),
    small_pair=pltpu.VMEM((SMALL, COLS), BF16),
    norms=pltpu.VMEM((2, 16, COLS), BF16),
    send=DMA((SLABS, 2)),
    recv=DMA((SLABS, 10)),
    small_send=DMA,
    small_recv=DMA((4,)),
    load=DMA((5,)),
    pair_send=DMA((2, 2)),
    pair_recv=DMA((2, 2)),
    next_send=DMA((2,)),
    next_recv=DMA((2,)),
    copy_send=DMA((2, 2)),
    copy_recv=DMA((2, 2)),
    copy_own=DMA((2, 2)),
    norms_sem=DMA((2,)),
)


def layer_kernel(*refs):
    names = INPUTS + OUTPUTS + tuple(SCRATCH)
    r = dict(zip(names, refs))
    layer = Layer(r)
    place = Place()
    section, tensor = place.section, place.tensor
    first, last = section == 0, section == 1
    dp = lax.axis_index("dp")
    partner = (section, dp, 1 - tensor)
    beyond = [(1 - section, dp, t) for t in range(2)]
    load = r["load"]
    out, x, upstream = r["out"], r["x"], r["upstream"]

    def fetch(src, dst, sem):
        pltpu.make_async_copy(src, dst, load.at[sem]).start()

    @pl.when(first)
    def _():
        fetch(r["x_in"], x, 0)

    @pl.when(last)
    def _():
        fetch(r["cot_in"], r["activated"].at[:, pl.ds(0, WIDTH)], 0)
        fetch(r["out_in"], r["out_w"], 3)
        for c in range(2):
            fetch(r["down_in"].at[:, pl.ds(c * COLS, COLS)], out.at[2 + c], 4)

    fetch(r["qkv_in"], r["qkv_w"], 1)
    for n in range(4):
        fetch(r["up_in"].at[:, pl.ds(n * COLS, COLS)], layer.up_block(n, (0, WIDTH)), 2)

    @pl.when(first)
    def _():
        fetch(r["out_in"], r["out_w"], 3)
        for c in range(2):
            fetch(r["down_in"].at[:, pl.ds(c * COLS, COLS)], out.at[2 + c], 4)

    greet(plane_partners(place) + [partner] + beyond)
    r["vectors"][...] = jnp.zeros((SMALL, COLS), F32)

    @pl.when(first)
    def _():
        take(x, load.at[0])

    @pl.when(last)
    def _():
        given = r["activated"]
        take(upstream, load.at[0])
        swap = r["order"][0] != 0
        one, two = given[pl.ds(0, SEQ), pl.ds(0, WIDTH)], given[pl.ds(SEQ, SEQ), pl.ds(0, WIDTH)]
        upstream[pl.ds(0, SEQ)] = jnp.where(swap, two, one)
        upstream[pl.ds(SEQ, SEQ)] = jnp.where(swap, one, two)
        take(r["out_w"], load.at[3])
        take(out.at[pl.ds(2, 2)], load.at[4])

        def each(m, _):
            layer.back_branches(m)
            return 0

        lax.fori_loop(0, 2, each, 0)

    take(r["qkv_w"], load.at[1])

    def exchange(m, kind):
        rows = ds((1 - tensor) * OWN, OWN)
        put(r["partial"].at[m, rows], r["came"].at[kind, m], r["pair_send"].at[kind, m],
            r["pair_recv"].at[kind, m], partner)

    def rows_of(m):
        return ds(m * SEQ + tensor * OWN, OWN)

    def summed(m, kind):
        take(r["came"].at[kind, m], r["pair_recv"].at[kind, m])
        take(r["came"].at[kind, m], r["pair_send"].at[kind, m])
        return wide(r["partial"].at[m, ds(tensor * OWN, OWN)]) + wide(r["came"].at[kind, m])

    def hand_on(m, kind, result, target, sender):
        mine, rows = r["mine"].at[kind, m], rows_of(m)
        mine[...] = result.astype(BF16)

        @pl.when(sender)
        def _():
            for device in beyond:
                put(mine, target.at[rows], r["next_send"].at[m], r["next_recv"].at[m], device)

        final = r["g_out"] if kind else r["y_out"]
        put(mine, final.at[rows], r["copy_send"].at[kind, m], r["copy_recv"].at[kind, m], partner)
        pltpu.make_async_copy(mine, final.at[rows], r["copy_own"].at[kind, m]).start()

    def finish_forward(m):
        bias = wide(r["out_bias"]) + wide(r["down_bias"])
        result = wide(x.at[rows_of(m)]) + summed(m, 0) + bias
        hand_on(m, 0, result, x, first)

    def finish_backward(m):
        rows = rows_of(m)
        d_normed = summed(m, 1)
        rstd = r["rstd"][rows]
        normed = (wide(x.at[rows]) - r["mean"][rows]) * rstd
        centered = (d_normed - jnp.mean(d_normed, axis=1, keepdims=True)
                    - normed * jnp.mean(d_normed * normed, axis=1, keepdims=True))
        hand_on(m, 1, wide(upstream.at[rows]) + rstd * centered, upstream, last)

    def finish(j):
        m = lax.rem(j, 2)
        forward = first == (j < 2)

        @pl.when(forward)
        def _():
            finish_forward(m)

        @pl.when(jnp.logical_not(forward))
        def _():
            finish_backward(m)

    def tick(i, _):
        m = lax.rem(i, 2)
        early = i < 2

        @pl.when(early)
        def _():
            @pl.when(last)
            def _():
                take(x.at[pl.ds(0, SEQ)], r["next_recv"].at[m])

            layer.norm(m)
            layer.project(m)
            layer.attend(m)

        @pl.when(i > 0)
        def _():
            finish(i - 1)

        @pl.when(i == 0)
        def _():
            take(out.at[pl.ds(4, 2)], load.at[2])

        @pl.when(early)
        def _():
            layer.up(m)

        @pl.when(jnp.logical_and(first, i == 0))
        def _():
            take(r["out_w"], load.at[3])
            take(out.at[pl.ds(2, 2)], load.at[4])

        forward = first == early

        @pl.when(forward)
        def _():
            layer.branches(m)
            exchange(m, 0)

        @pl.when(jnp.logical_not(forward))
        def _():
            @pl.when(first)
            def _():
                take(upstream.at[pl.ds(0, SEQ)], r["next_recv"].at[m])
                layer.back_branches(m)

            layer.back_gelu(m)
            layer.back_attend(m)
            layer.back_inputs(m)
            exchange(m, 1)

        return 0

    lax.fori_loop(0, 4, tick, 0)
    grads = r["grads"]
    reduce = Reduce(place, grads, out, r["arrived"], r["landing"], r["send"], r["recv"])
    small = SmallReduce(place, r["small_mine"], r["small_out"], r["small_landing"], r["small_pair"],
                        r["small_send"], r["small_recv"])
    down, out_sum, up, qkv = layer.weight_sums(grads)
    lax.fori_loop(0, 4, down, 0)
    reduce.step(0, 0)
    lax.fori_loop(4, 8, down, 0)
    reduce.step(1, 0)
    lax.fori_loop(0, 4, up, 0)
    reduce.step(2, 0)
    reduce.step(0, 1)
    lax.fori_loop(4, 8, up, 0)
    reduce.step(3, 0)
    reduce.step(1, 1)
    lax.fori_loop(0, 2, out_sum, 0)
    lax.fori_loop(0, 2, qkv, 0)
    reduce.step(4, 0)
    reduce.step(0, 2)
    lax.fori_loop(2, 6, qkv, 0)
    reduce.step(5, 0)
    finish(3)
    layer.bias_sums()
    vectors = r["vectors"]
    norms = r["norms"]
    norms[0] = vectors[pl.ds(0, 16)].astype(BF16)
    put(norms.at[0], norms.at[1], r["norms_sem"].at[0], r["norms_sem"].at[1], partner)
    r["small_mine"][...] = vectors[...].astype(BF16)
    started = {(s, 0) for s in range(SLABS)} | {(0, 1), (1, 1), (0, 2)}
    small_step = 0
    for turn, (s, k) in enumerate(o for o in ORDER if o not in started):
        reduce.step(s, k)
        if turn in (4, 12, 20, 28, 36):
            if small_step == 0:
                take(norms.at[1], r["norms_sem"].at[1])
                sums = wide(norms.at[0]) + wide(norms.at[1])
                ln_row = lax.broadcasted_iota(jnp.int32, (16, COLS), 0) < 8
                r["small_mine"][pl.ds(0, 16)] = jnp.where(ln_row, sums, vectors[pl.ds(0, 16)]).astype(BF16)
            small.step(small_step)
            small_step += 1
    for s in range(SLABS):
        reduce.step(s, 10)
    for s in range(SLABS):
        reduce.drain(s)
    small.drain()
    take(norms.at[0], r["norms_sem"].at[0])
    for m in range(2):
        for kind in range(2):
            take(r["mine"].at[kind, m], r["copy_send"].at[kind, m])
            take(r["mine"].at[kind, m], r["copy_recv"].at[kind, m])
            take(r["mine"].at[kind, m], r["copy_own"].at[kind, m])
        take(x.at[pl.ds(0, SEQ)], r["next_send"].at[m])


def layer_call(*args):
    hbm, vmem = pl.BlockSpec(memory_space=pl.ANY), pl.BlockSpec(memory_space=pltpu.VMEM)
    smem = pl.BlockSpec(memory_space=pltpu.SMEM)
    rows = jax.ShapeDtypeStruct((TOKENS, WIDTH), BF16)
    return pl.pallas_call(
        layer_kernel,
        out_shape=(rows, rows, pltpu.VMEM((SLABS, SLAB_ROWS, COLS), BF16), pltpu.VMEM((SMALL, COLS), BF16)),
        in_specs=[hbm if name in IN_HBM else smem if name == "order" else vmem for name in INPUTS],
        out_specs=(hbm, hbm, vmem, vmem),
        scratch_shapes=list(SCRATCH.values()),
        compiler_params=pltpu.CompilerParams(
            collective_id=0, has_side_effects=True, vmem_limit_bytes=VMEM_LIMIT
        ),
    )(*args)


def widen_kernel(given, down, up, out, qkv, staged, sems):
    def target(i):
        slab, r = divmod(i, 4)
        rows = pl.ds(r * COLS, COLS)
        if slab < 2:
            return down.at[rows, pl.ds(slab * COLS, COLS)]
        if slab < 4:
            n = (slab - 2) * 2 + r // 2
            return up.at[pl.ds((r % 2) * COLS, COLS), pl.ds(n * COLS, COLS)]
        i -= 16
        if i < 2:
            return out.at[:, pl.ds(i * COLS, COLS)]
        t, r = divmod(i - 2, 2)
        return qkv.at[t, pl.ds(r * COLS, COLS)]

    count, depth = SLABS * 4, 4
    copies = []
    for i in range(count):
        if i >= depth:
            copies[i - depth].wait()
        slab, r = divmod(i, 4)
        slot = i % depth
        staged[slot] = given[slab, pl.ds(r * COLS, COLS)].astype(F32)
        copies.append(pltpu.make_async_copy(staged.at[slot], target(i), sems.at[slot]))
        copies[i].start()
    for i in range(count - depth, count):
        copies[i].wait()


def widened(grads):
    hbm, vmem = pl.BlockSpec(memory_space=pl.ANY), pl.BlockSpec(memory_space=pltpu.VMEM)
    shapes = ((2048, WIDTH), (WIDTH, 2048), (COLS, WIDTH), (3, WIDTH, COLS))
    return pl.pallas_call(
        widen_kernel,
        out_shape=tuple(jax.ShapeDtypeStruct(shape, F32) for shape in shapes),
        in_specs=[vmem],
        out_specs=(hbm,) * 4,
        scratch_shapes=[pltpu.VMEM((4, COLS, COLS), F32), DMA((4,))],
    )(grads)


def shards(layer_input, cotangent, order, ln1_scale, ln1_bias, ln2_scale, ln2_bias, qkv_weight, qkv_bias,
           out_weight, out_bias, up_weight, up_bias, down_weight, down_bias):
    cos, low_sin, high_sin = (jnp.asarray(table) for table in rotary_tables())
    y, g, grads, small = layer_call(
        layer_input.reshape(TOKENS, WIDTH), cotangent.reshape(TOKENS, WIDTH), order,
        ln1_scale, ln1_bias, ln2_scale, ln2_bias,
        qkv_weight[0].transpose(1, 0, 2), qkv_bias[0], out_weight[0], out_bias, up_weight[0], up_bias,
        down_weight[0], down_bias, cos, low_sin, high_sin,
    )
    down, up, out, qkv = widened(grads)
    small = small.astype(F32)
    rows = (1, 2, 1, SEQ, WIDTH)
    norms = [small[2 * i:2 * i + 2].reshape(1, WIDTH) for i in range(4)]
    bias = small[11:13].reshape(1, WIDTH)
    return (y.reshape(rows), g.reshape(rows), *norms, qkv.transpose(1, 0, 2)[None], small[8:11][None],
            out[None], bias, up[None], small[13:17].reshape(1, 2048), down[None], bias)


def solution(mesh):
    return jax.shard_map(
        shards,
        mesh=mesh,
        in_specs=(
            P(None, "dp", None, None),
            P(None, "dp", None, None),
            P(),
            P("section", None),
            P("section", None),
            P("section", None),
            P("section", None),
            P("section", None, None, "tensor"),
            P("section", None, "tensor"),
            P("section", "tensor", None),
            P("section", None),
            P("section", None, "tensor"),
            P("section", "tensor"),
            P("section", "tensor", None),
            P("section", None),
        ),
        out_specs=(
            P("section", None, "dp", None, None),
            P("section", None, "dp", None, None),
            P("section", None),
            P("section", None),
            P("section", None),
            P("section", None),
            P("section", None, None, "tensor"),
            P("section", None, "tensor"),
            P("section", "tensor", None),
            P("section", None),
            P("section", None, "tensor"),
            P("section", "tensor"),
            P("section", "tensor", None),
            P("section", None),
        ),
        check_vma=False,
    )
```

```python
import jax
import jax.numpy as jnp
import numpy as np
from jax import lax
from jax.experimental import pallas as pl
from jax.experimental.pallas import tpu as pltpu
from jax.sharding import PartitionSpec as P

MESH = pl.DeviceIdType.MESH
VMEM_LIMIT = 50 * 2**20

SLABS = 6
SLAB_ROWS = 2048
HALF = 1024
STREAM = 512
COLS = 512
CHUNK = (128, 32)
RX_ONE = (0, 768)
RX_TWO = (256, 832)
RX_ROWS = 960
SMALL = 32


def mod4(value):
    return lax.rem(value + 4, 4)


class Place:
    def __init__(self):
        self.section = lax.axis_index("section")
        self.tensor = lax.axis_index("tensor")
        dp = lax.axis_index("dp")
        self.core = lax.rem(dp, 2)
        self.x = lax.rem(dp // 2, 4)
        self.z = dp // 8

    def at(self, z, x, core):
        return (self.section, (z * 4 + x) * 2 + core, self.tensor)

    def other_core(self):
        return self.at(self.z, self.x, 1 - self.core)

    def along(self, axis, step):
        if axis == 0:
            return self.at(self.z, mod4(self.x + step), self.core)
        return self.at(mod4(self.z + step), self.x, self.core)

    def position(self, axis):
        return self.x if axis == 0 else self.z


def ds(start, size):
    return pl.ds(pl.multiple_of(start, 16), size)


def take(ref, sem):
    pltpu.make_async_copy(ref, ref, sem).wait()


def put(src, dst, send_sem, recv_sem, device):
    pltpu.make_async_remote_copy(
        src_ref=src, dst_ref=dst, send_sem=send_sem, recv_sem=recv_sem,
        device_id=device, device_id_type=MESH,
    ).start()


def added(*parts):
    total = parts[0].astype(jnp.float32)
    for part in parts[1:]:
        total = total + part.astype(jnp.float32)
    return total.astype(jnp.bfloat16)


class Reduce:
    def __init__(self, place, grads, out, arrived, landing, send, recv):
        self.place, self.grads, self.out = place, grads, out
        self.arrived, self.landing, self.send, self.recv = arrived, landing, send, recv

    def base(self, stream):
        return self.place.core * HALF + stream * STREAM

    def layout(self, stream, phase):
        axis = (stream + phase) % 2
        p = self.place.position(axis)
        start = self.base(stream)
        if phase == 1:
            start = start + self.place.position(stream) * CHUNK[0]
        return axis, p, start, CHUNK[phase]

    def first_sends(self, s, phase, sem):
        h = CHUNK[phase] // 2
        for stream in range(2):
            axis, p, start, size = self.layout(stream, phase)
            far = start + mod4(p + 2) * size
            for side, step in ((0, 1), (1, -1)):
                put(self.grads.at[s, ds(far + side * h, h)],
                    self.landing.at[s, pl.ds(RX_ONE[phase] + (stream * 2 + side) * h, h)],
                    self.send.at[s, 0], self.recv.at[s, sem], self.place.along(axis, step))

    def second_sends(self, s, phase, sem):
        h = CHUNK[phase] // 2
        take(self.landing.at[s, pl.ds(0, 4 * h)], self.recv.at[s, sem - 1])
        for stream in range(2):
            axis, p, start, size = self.layout(stream, phase)
            for side, step in ((0, 1), (1, -1)):
                near = start + mod4(p + step) * size
                rows = ds(near + side * h, h)
                came = pl.ds(RX_ONE[phase] + (stream * 2 + side) * h, h)
                self.grads[s, rows] = added(self.grads[s, rows], self.landing[s, came])
                put(self.grads.at[s, ds(near, size)],
                    self.landing.at[s, pl.ds(RX_TWO[phase] + (stream * 2 + side) * size, size)],
                    self.send.at[s, 0], self.recv.at[s, sem], self.place.along(axis, step))

    def finish(self, s, phase, sem, target):
        size = CHUNK[phase]
        take(self.landing.at[s, pl.ds(0, 4 * size)], self.recv.at[s, sem])
        for stream in range(2):
            axis, p, start, size = self.layout(stream, phase)
            rows = ds(start + p * size, size)
            left = pl.ds(RX_TWO[phase] + stream * 2 * size, size)
            right = pl.ds(RX_TWO[phase] + (stream * 2 + 1) * size, size)
            target[s, rows] = added(self.grads[s, rows], self.landing[s, left], self.landing[s, right])

    def spread(self, s, phase, sem):
        for stream in range(2):
            axis, p, start, size = self.layout(stream, phase)
            rows = ds(start + p * size, size)
            for step in (1, -1):
                put(self.out.at[s, rows], self.out.at[s, rows], self.send.at[s, 1],
                    self.recv.at[s, sem], self.place.along(axis, step))

    def forward(self, s, phase, sem):
        size = CHUNK[phase]
        take(self.out.at[s, pl.ds(0, 4 * size)], self.recv.at[s, sem - 1])
        for stream in range(2):
            axis, p, start, size = self.layout(stream, phase)
            for side, step in ((0, 1), (1, -1)):
                rows = ds(start + mod4(p - step) * size + side * (size // 2), size // 2)
                put(self.out.at[s, rows], self.out.at[s, rows], self.send.at[s, 1],
                    self.recv.at[s, sem], self.place.along(axis, step))

    def to_core(self, s, offsets):
        for stream in range(2):
            axis, p, start, size = self.layout(stream, 0)
            for offset in offsets:
                rows = ds(start + mod4(p + offset) * size, size)
                put(self.out.at[s, rows], self.out.at[s, rows], self.send.at[s, 1],
                    self.recv.at[s, 9], self.place.other_core())

    def step(self, s, k):
        core = self.place.core
        if k == 0:
            put(self.grads.at[s, ds((1 - core) * HALF, HALF)], self.arrived.at[s],
                self.send.at[s, 0], self.recv.at[s, 0], self.place.other_core())
        elif k == 1:
            take(self.arrived.at[s], self.recv.at[s, 0])

            def block(i, _):
                here = ds(core * HALF + i * 128, 128)
                self.grads[s, here] = added(self.grads[s, here], self.arrived[s, ds(i * 128, 128)])
                return 0

            lax.fori_loop(0, HALF // 128, block, 0)
            self.first_sends(s, 0, 1)
        elif k == 2:
            self.second_sends(s, 0, 2)
        elif k == 3:
            self.finish(s, 0, 2, self.grads)
            self.first_sends(s, 1, 3)
        elif k == 4:
            self.second_sends(s, 1, 4)
        elif k == 5:
            self.finish(s, 1, 4, self.out)
            self.spread(s, 1, 5)
        elif k == 6:
            self.forward(s, 1, 6)
        elif k == 7:
            take(self.out.at[s, pl.ds(0, 64)], self.recv.at[s, 6])
            self.spread(s, 0, 7)
            self.to_core(s, (0,))
        elif k == 8:
            self.forward(s, 0, 8)
            self.to_core(s, (1, -1))
        elif k == 9:
            take(self.out.at[s, pl.ds(0, 256)], self.recv.at[s, 8])
            self.to_core(s, (2,))
        elif k == 10:
            take(self.out.at[s, pl.ds(0, 1024)], self.recv.at[s, 9])

    def drain(self, s):
        take(self.grads.at[s, pl.ds(0, 1984)], self.send.at[s, 0])
        take(self.grads.at[s, pl.ds(0, 1984)], self.send.at[s, 1])


class SmallReduce:
    def __init__(self, place, mine, out, landing, pair, send, recv):
        self.place, self.mine, self.out, self.landing, self.pair = place, mine, out, landing, pair
        self.send, self.recv = send, recv

    def exchange(self, axis):
        p = self.place.position(axis)
        for step in (1, 2, 3):
            put(self.landing.at[axis, p], self.landing.at[axis, p], self.send, self.recv.at[1 + axis],
                self.place.along(axis, step))

    def collected(self, axis):
        take(self.landing.at[axis, pl.ds(0, 3)], self.recv.at[1 + axis])
        return added(*[self.landing[axis, j] for j in range(4)])

    def step(self, k):
        half = SMALL // 2
        rows = ds(self.place.core * half, half)
        if k == 0:
            put(self.mine, self.pair, self.send, self.recv.at[0], self.place.other_core())
        elif k == 1:
            take(self.pair, self.recv.at[0])
            self.landing[0, self.place.x] = added(self.mine[rows], self.pair[rows])
            self.exchange(0)
        elif k == 2:
            self.landing[1, self.place.z] = self.collected(0)
            self.exchange(1)
        elif k == 3:
            self.out[rows] = self.collected(1)
            put(self.out.at[rows], self.out.at[rows], self.send, self.recv.at[3], self.place.other_core())
        elif k == 4:
            take(self.out.at[pl.ds(0, half)], self.recv.at[3])

    def drain(self):
        half = SMALL // 2
        take(self.landing.at[0, pl.ds(0, 3)], self.send)
        take(self.landing.at[0, pl.ds(0, 3)], self.send)
        take(self.mine, self.send)
        take(self.out.at[pl.ds(0, half)], self.send)


def greet(devices):
    for device in devices:
        pl.semaphore_signal(pltpu.get_barrier_semaphore(), inc=1, device_id=device, device_id_type=MESH)


def met(count):
    pl.semaphore_wait(pltpu.get_barrier_semaphore(), count)


def plane_partners(place):
    return [place.other_core()] + [place.along(axis, step) for axis in (0, 1) for step in (1, 2, 3)]


PLAN = (
    "down0", (0, 0), "down1", (1, 0), "back", (0, 1), "up0", (1, 1),
    (2, 0), "up1", (3, 0), (0, 2), "attend", (2, 1), (1, 2), (3, 1),
    (0, 3), "inputs", (2, 2), "last0", (1, 3), (4, 0), "last1", (3, 2),
    (0, 4), (5, 0), "finish0", "finish1", "sums", "copies", (4, 1), (2, 3),
    (1, 4), "norms", "small0", (5, 1), (3, 3), (0, 5), (4, 2), (2, 4),
    (1, 5), (5, 2), (3, 4), (0, 6), "small1", (4, 3), (2, 5), (1, 6),
    (5, 3), (3, 5), (0, 7), (4, 4), (2, 6), "small2", (1, 7), (5, 4),
    (3, 6), (0, 8), (4, 5), (2, 7), (1, 8), (5, 5), "small3", (3, 7),
    (0, 9), (4, 6), (2, 8), (1, 9), (5, 6), (3, 8), (4, 7), "small4",
    (2, 9), (5, 7), (3, 9), (4, 8), (5, 8), (4, 9), (5, 9),
)

SEQ = 256
TOKENS = 2 * SEQ
OWN = SEQ // 2
PARTS = 8
PART = OWN // PARTS
WIDTH = 1024
HEAD = 64
ROT = 16
EPSILON = 1e-05
BF16 = jnp.bfloat16
F32 = jnp.float32


def nn(a, b):
    return lax.dot_general(a, b, (((1,), (0,)), ((), ())), preferred_element_type=F32)


def nt(a, b):
    return lax.dot_general(a, b, (((1,), (1,)), ((), ())), preferred_element_type=F32)


def tn(a, b):
    return lax.dot_general(a, b, (((0,), (0,)), ((), ())), preferred_element_type=F32)


def wide(ref):
    return ref[...].astype(F32)


def block(index, size):
    return pl.ds(pl.multiple_of(index * size, size), size)


def one_head(pair, h):
    lane = lax.broadcasted_iota(jnp.int32, pair.shape, 1)
    return jnp.where((lane < HEAD) if h == 0 else (lane >= HEAD), pair, jnp.zeros_like(pair))


def rotary_tables():
    frequency = (1.0 / 10000.0 ** (np.arange(ROT // 2) * 2.0 / ROT)).astype(np.float32)
    angles = np.arange(SEQ, dtype=np.float32)[:, None] * frequency[None, :]
    cos, sin = np.cos(angles), np.sin(angles)
    cos_table = np.ones((SEQ, 128), np.float32)
    low_sin, high_sin = np.zeros((SEQ, 128), np.float32), np.zeros((SEQ, 128), np.float32)
    for head in range(128 // HEAD):
        first, second = head * HEAD, head * HEAD + ROT // 2
        cos_table[:, first:second] = cos
        cos_table[:, second:second + ROT // 2] = cos
        low_sin[:, first:second] = sin
        high_sin[:, second:second + ROT // 2] = sin
    return cos_table, low_sin, high_sin


def rotated(u, tables, sign):
    cos, low_sin, high_sin = tables
    ahead = pltpu.roll(u, 128 - ROT // 2, 1)
    behind = pltpu.roll(u, ROT // 2, 1)
    return u * cos + (behind * high_sin - ahead * low_sin) * sign


class Layer:
    def __init__(self, refs):
        self.__dict__.update(refs)

    def up_block(self, n, rows):
        return self.out.at[4 + n // 2, pl.ds((n % 2) * WIDTH + rows[0], rows[1])]

    def slope_block(self, m, n):
        return self.grads.at[4, ds(n * COLS + m * SEQ, SEQ)]

    def norm(self, m):
        rows = block(m, SEQ)
        x = wide(self.x.at[rows])
        mean = jnp.mean(x, axis=1, keepdims=True)
        centered = x - mean
        rstd = lax.rsqrt(jnp.mean(centered * centered, axis=1, keepdims=True) + EPSILON)
        normed = centered * rstd
        self.mean[rows] = mean
        self.rstd[rows] = rstd
        self.first_in[rows] = (normed * wide(self.ln1_scale) + wide(self.ln1_bias)).astype(BF16)
        self.second_in[rows] = (normed * wide(self.ln2_scale) + wide(self.ln2_bias)).astype(BF16)

    def project(self, m):
        rows = block(m, SEQ)
        tables = (self.cos[...], self.low_sin[...], self.high_sin[...])
        bias = wide(self.qkv_bias)
        for t in range(3):
            part = nn(self.first_in[rows], self.qkv_w[t]) + bias[t:t + 1]
            for lane in range(0, COLS, 128):
                piece = part[:, lane:lane + 128]
                if t < 2:
                    piece = rotated(piece, tables, 1.0)
                if t == 0:
                    piece = piece * HEAD ** -0.5
                self.qkv[t, rows, pl.ds(lane, 128)] = piece.astype(BF16)

    def attend(self, m):
        rows = block(m, SEQ)
        causal = (lax.broadcasted_iota(jnp.int32, (SEQ, SEQ), 0)
                  >= lax.broadcasted_iota(jnp.int32, (SEQ, SEQ), 1))
        for hp in range(4):
            lanes = pl.ds(hp * 128, 128)
            q, k, v = (self.qkv[t, rows, lanes] for t in range(3))
            context = None
            for h in range(2):
                scores = jnp.where(causal, nt(one_head(q, h), k), -1e30)
                exp = jnp.exp(scores - jnp.max(scores, axis=1, keepdims=True))
                probs = (exp * (1.0 / jnp.sum(exp, axis=1, keepdims=True))).astype(BF16)
                self.probs[m, hp * 2 + h] = probs
                part = nn(probs, one_head(v, h))
                context = part if context is None else context + part
            self.context[rows, lanes] = context.astype(BF16)

    def up(self, m):
        rows = block(m, SEQ)
        bias = wide(self.up_bias)
        for n in range(4):
            hidden = nn(self.second_in[rows], self.up_block(n, (0, WIDTH))[...])
            hidden = hidden + bias[:, n * COLS:(n + 1) * COLS]
            cdf = 0.5 * (1.0 + lax.erf(hidden * 0.7071067811865476))
            density = jnp.exp(-0.5 * hidden * hidden) * 0.3989422804014327
            lanes = pl.ds(n * COLS, COLS)
            self.activated[rows, lanes] = (hidden * cdf).astype(BF16)
            self.slope_block(m, n)[...] = (cdf + hidden * density).astype(BF16)

    def branches(self, m):
        rows = block(m, SEQ)
        for j in range(2):
            lanes = pl.ds(j * COLS, COLS)
            total = nn(self.context[rows], self.out_w[:, lanes])
            total = total + nn(self.activated[rows], self.out[2 + j])
            self.partial[m, :, lanes] = total.astype(BF16)

    def back_branches(self, m):
        rows = block(m, SEQ)
        upstream = self.upstream[rows]
        self.d_context[rows] = nt(upstream, self.out_w[...]).astype(BF16)
        for n in range(4):
            down = pl.ds(n * COLS, COLS)
            part = nt(upstream[:, :COLS], self.out[2, down]) + nt(upstream[:, COLS:], self.out[3, down])
            self.d_hidden[rows, down] = part.astype(BF16)

    def back_gelu(self, m):
        rows = block(m, SEQ)
        for n in range(4):
            lanes = pl.ds(n * COLS, COLS)
            self.d_hidden[rows, lanes] = (
                wide(self.d_hidden.at[rows, lanes]) * wide(self.slope_block(m, n))
            ).astype(BF16)

    def back_attend(self, m):
        rows = block(m, SEQ)
        tables = (self.cos[...], self.low_sin[...], self.high_sin[...])
        for hp in range(4):
            lanes = pl.ds(hp * 128, 128)
            q, k, v = (self.qkv[t, rows, lanes] for t in range(3))
            d_context = self.d_context[rows, lanes]
            probs = [self.probs[m, hp * 2 + h] for h in range(2)]
            d_mine = [one_head(d_context, h) for h in range(2)]
            d_scores = []
            for h in range(2):
                wide_probs = probs[h].astype(F32)
                weighted = nt(d_mine[h], v) * wide_probs
                inner = jnp.sum(weighted, axis=1, keepdims=True)
                d_scores.append((weighted - wide_probs * inner).astype(BF16))
            both = [jnp.concatenate([one_head(u, 0), one_head(u, 1)], axis=0) for u in (q, k)]
            d_query = nn(jnp.concatenate(d_scores, axis=1), both[1])
            d_key = tn(jnp.concatenate(d_scores, axis=0), both[0])
            d_value = tn(jnp.concatenate(probs, axis=0), jnp.concatenate(d_mine, axis=0))
            d_query = rotated(d_query * HEAD ** -0.5, tables, -1.0)
            d_key = rotated(d_key, tables, -1.0)
            for t, part in enumerate((d_query, d_key, d_value)):
                self.d_projected[t, rows, lanes] = part.astype(BF16)

    def back_inputs(self, m):
        rows = block(m, SEQ)
        mean, rstd = self.mean[rows], self.rstd[rows]
        for j in range(2):
            lanes = pl.ds(j * COLS, COLS)
            d_second = None
            for n in range(4):
                part = nt(self.d_hidden[rows, pl.ds(n * COLS, COLS)], self.up_block(n, (j * COLS, COLS))[...])
                d_second = part if d_second is None else d_second + part
            d_first = None
            for t in range(3):
                part = nt(self.d_projected[t, rows], self.qkv_w[t, lanes])
                d_first = part if d_first is None else d_first + part
            normed = (wide(self.x.at[rows, lanes]) - mean) * rstd
            sums = (d_first * normed, d_first, d_second * normed, d_second)
            for i, value in enumerate(sums):
                row = pl.ds(2 * i + j, 1)
                self.vectors[row] = self.vectors[row] + jnp.sum(value, axis=0, keepdims=True)
            d_normed = d_first * wide(self.ln1_scale.at[:, lanes]) + d_second * wide(self.ln2_scale.at[:, lanes])
            self.partial[m, :, lanes] = d_normed.astype(BF16)

    def weight_sum(self, name):
        def product(left, columns, targets):
            turned = left[:, columns].T
            for right, b in targets:
                self.grads[b // 4, pl.ds((b % 4) * COLS, COLS)] = nn(turned, right).astype(BF16)

        upstream = [self.upstream[:, pl.ds(c * COLS, COLS)] for c in range(2)]
        if name in ("down0", "down1"):
            for r in (0, 1) if name == "down0" else (2, 3):
                product(self.activated, pl.ds(r * COLS, COLS), [(upstream[c], 2 * r + c) for c in range(2)])
        elif name in ("up0", "up1"):
            r = int(name == "up1")
            d_hidden = [self.d_hidden[:, pl.ds(n * COLS, COLS)] for n in range(4)]
            product(self.second_in, pl.ds(r * COLS, COLS), [(d_hidden[n], 8 + 4 * r + n) for n in range(4)])
        else:
            r = int(name == "last1")
            if r == 0:
                product(self.context, pl.ds(0, COLS), [(upstream[c], 16 + c) for c in range(2)])
            d_projected = [self.d_projected[t] for t in range(3)]
            product(self.first_in, pl.ds(r * COLS, COLS), [(d_projected[t], 18 + 3 * r + t) for t in range(3)])

    def bias_sums(self):
        for t in range(3):
            self.vectors[pl.ds(8 + t, 1)] = jnp.sum(wide(self.d_projected.at[t]), axis=0, keepdims=True)
        for j in range(2):
            lanes = pl.ds(j * COLS, COLS)
            self.vectors[pl.ds(11 + j, 1)] = jnp.sum(wide(self.upstream.at[:, lanes]), axis=0, keepdims=True)
        for n in range(4):
            lanes = pl.ds(n * COLS, COLS)
            self.vectors[pl.ds(13 + n, 1)] = jnp.sum(wide(self.d_hidden.at[:, lanes]), axis=0, keepdims=True)


INPUTS = ("x_in", "cot_in", "order", "ln1_scale", "ln1_bias", "ln2_scale", "ln2_bias", "qkv_in", "qkv_bias",
          "out_in", "out_bias", "up_in", "up_bias", "down_in", "down_bias", "cos", "low_sin", "high_sin")
IN_HBM = ("x_in", "cot_in", "qkv_in", "out_in", "up_in", "down_in")
OUTPUTS = ("y_out", "g_out", "out", "small_out")
DMA = pltpu.SemaphoreType.DMA
SCRATCH = dict(
    grads=pltpu.VMEM((SLABS, SLAB_ROWS, COLS), BF16),
    arrived=pltpu.VMEM((SLABS, HALF, COLS), BF16),
    landing=pltpu.VMEM((SLABS, RX_ROWS, COLS), BF16),
    x=pltpu.VMEM((TOKENS, WIDTH), BF16),
    upstream=pltpu.VMEM((TOKENS, WIDTH), BF16),
    first_in=pltpu.VMEM((TOKENS, WIDTH), BF16),
    second_in=pltpu.VMEM((TOKENS, WIDTH), BF16),
    qkv=pltpu.VMEM((3, TOKENS, COLS), BF16),
    d_projected=pltpu.VMEM((3, TOKENS, COLS), BF16),
    context=pltpu.VMEM((TOKENS, COLS), BF16),
    d_context=pltpu.VMEM((TOKENS, COLS), BF16),
    probs=pltpu.VMEM((2, 8, SEQ, SEQ), BF16),
    activated=pltpu.VMEM((TOKENS, 4 * COLS), BF16),
    d_hidden=pltpu.VMEM((TOKENS, 4 * COLS), BF16),
    partial=pltpu.VMEM((2, SEQ, WIDTH), BF16),
    came=pltpu.VMEM((2, 2, OWN, WIDTH), BF16),
    mine=pltpu.VMEM((2, 2, OWN, WIDTH), BF16),
    mean=pltpu.VMEM((TOKENS, 1), F32),
    rstd=pltpu.VMEM((TOKENS, 1), F32),
    vectors=pltpu.VMEM((SMALL, COLS), F32),
    qkv_w=pltpu.VMEM((3, WIDTH, COLS), BF16),
    out_w=pltpu.VMEM((COLS, WIDTH), BF16),
    small_mine=pltpu.VMEM((SMALL, COLS), BF16),
    small_landing=pltpu.VMEM((2, 4, SMALL // 2, COLS), BF16),
    small_pair=pltpu.VMEM((SMALL, COLS), BF16),
    norms=pltpu.VMEM((2, 16, COLS), BF16),
    send=DMA((SLABS, 2)),
    recv=DMA((SLABS, 10)),
    small_send=DMA,
    small_recv=DMA((4,)),
    load=DMA((5,)),
    pair_send=DMA((2, 2)),
    pair_recv=DMA((2, 2, PARTS)),
    next_send=DMA((2,)),
    next_recv=DMA((2, PARTS)),
    far_send=DMA((2,)),
    far_recv=DMA((2,)),
    copy_send=DMA((2, 2)),
    copy_recv=DMA((2, 2)),
    copy_own=DMA((2, 2)),
    norms_sem=DMA((2,)),
)


class Refs:
    def __init__(self, pairs):
        self.__dict__.update(pairs)


def layer_kernel(*refs):
    names = INPUTS + OUTPUTS + tuple(SCRATCH)
    r = Refs(zip(names, refs))
    layer = Layer(vars(r))
    place = Place()
    section, tensor = place.section, place.tensor
    first, last = section == 0, section == 1
    dp = lax.axis_index("dp")
    partner = (section, dp, 1 - tensor)
    near = (1 - section, dp, 1 - tensor)
    others = plane_partners(place) + [partner, near]
    load = r.load
    out, x, upstream = r.out, r.x, r.upstream

    greet(others)

    def fetch(src, dst, sem):
        pltpu.make_async_copy(src, dst, load.at[sem]).start()

    def fetch_out():
        fetch(r.out_in, r.out_w, 3)
        for c in range(2):
            fetch(r.down_in.at[:, pl.ds(c * COLS, COLS)], out.at[2 + c], 4)

    def fetch_up():
        for n in range(4):
            fetch(r.up_in.at[:, pl.ds(n * COLS, COLS)], layer.up_block(n, (0, WIDTH)), 2)

    @pl.when(first)
    def _():
        fetch(r.x_in, x, 0)
        fetch(r.qkv_in, r.qkv_w, 1)
        take(x, load.at[0])
        fetch_up()
        fetch_out()

    @pl.when(last)
    def _():
        fetch(r.cot_in, r.activated.at[:, pl.ds(0, WIDTH)], 0)
        fetch_out()
        fetch(r.qkv_in, r.qkv_w, 1)
        fetch_up()

    @pl.when(last)
    def _():
        given = r.activated
        take(upstream, load.at[0])
        swap = r.order[0] != 0
        one, two = given[pl.ds(0, SEQ), pl.ds(0, WIDTH)], given[pl.ds(SEQ, SEQ), pl.ds(0, WIDTH)]
        upstream[pl.ds(0, SEQ)] = jnp.where(swap, two, one)
        upstream[pl.ds(SEQ, SEQ)] = jnp.where(swap, one, two)
        take(r.out_w, load.at[3])
        take(out.at[pl.ds(2, 2)], load.at[4])

        def each(m, _):
            layer.back_branches(m)
            return 0

        lax.fori_loop(0, 2, each, 0)
        met(len(others))

    r.vectors[...] = jnp.zeros((SMALL, COLS), F32)

    def part_of(start, c):
        return ds(start + c * PART, PART)

    def exchange(m, kind):
        for c in range(PARTS):
            put(r.partial.at[m, part_of((1 - tensor) * OWN, c)], r.came.at[kind, m, part_of(0, c)],
                r.pair_send.at[kind, m], r.pair_recv.at[kind, m, c], partner)

    def finish_part(m, kind, c):
        rows = part_of(m * SEQ + tensor * OWN, c)
        here = part_of(0, c)
        came = r.came.at[kind, m, here]
        take(came, r.pair_recv.at[kind, m, c])
        total = wide(r.partial.at[m, part_of(tensor * OWN, c)]) + wide(came)
        if kind == 0:
            result = wide(x.at[rows]) + total + (wide(r.out_bias) + wide(r.down_bias))
        else:
            rstd = r.rstd[rows]
            normed = (wide(x.at[rows]) - r.mean[rows]) * rstd
            centered = (total - jnp.mean(total, axis=1, keepdims=True)
                        - normed * jnp.mean(total * normed, axis=1, keepdims=True))
            result = wide(upstream.at[rows]) + rstd * centered
        mine = r.mine.at[kind, m, here]
        mine[...] = result.astype(BF16)
        target = upstream if kind else x

        @pl.when(last if kind else first)
        def _():
            put(mine, target.at[rows], r.next_send.at[m], r.next_recv.at[m, c], near)

    def finish_parts(m, kind, parts):
        for c in parts:
            finish_part(m, kind, c)
        if PARTS - 1 in parts:
            take(r.came.at[kind, m], r.pair_send.at[kind, m])

    def finish(m):
        for kind, chosen in ((0, last), (1, first)):
            @pl.when(chosen)
            def _(kind=kind):
                finish_parts(m, kind, range(PARTS))

    def pass_on(m, target, parts):
        for c in parts:
            rows = target.at[part_of(m * SEQ + (1 - tensor) * OWN, c)]
            take(rows, r.next_recv.at[m, c])
            put(rows, rows, r.far_send.at[m], r.far_recv.at[m], partner)

    def arrived(m, target):
        take(target.at[pl.ds(0, OWN)], r.far_recv.at[m])

    def arrive(m, target):
        pass_on(m, target, range(PARTS))
        arrived(m, target)

    def tick(i, _):
        m = i

        def when(condition, action, *args):
            if isinstance(args[-1], range) and not args[-1]:
                return

            @pl.when(condition)
            def _():
                action(*args)

        def meanwhile(first_parts, next_parts, last_parts):
            when(jnp.logical_and(first, i == 1), finish_parts, 0, 0, first_parts)
            when(jnp.logical_and(last, i == 0), pass_on, 1, x, next_parts)
            when(jnp.logical_and(last, i == 1), finish_parts, 0, 1, last_parts)

        none = range(0)
        when(jnp.logical_and(last, i == 0), arrive, 0, x)
        when(jnp.logical_and(last, i == 1), arrived, 1, x)
        layer.norm(m)
        when(i == 0, take, r.qkv_w, load.at[1])
        layer.project(m)
        meanwhile(none, range(0, 2), none)
        layer.attend(m)
        meanwhile(range(0, 1), range(2, 5), range(0, 1))
        when(i == 0, take, out.at[pl.ds(4, 2)], load.at[2])
        layer.up(m)
        meanwhile(range(1, 4), range(5, PARTS), range(1, 3))

        @pl.when(jnp.logical_and(first, i == 0))
        def _():
            take(r.out_w, load.at[3])
            take(out.at[pl.ds(2, 2)], load.at[4])
            met(len(others))

        @pl.when(first)
        def _():
            layer.branches(m)
            meanwhile(range(4, PARTS), none, none)
            exchange(m, 0)

        @pl.when(last)
        def _():
            layer.back_gelu(m)
            layer.back_attend(m)
            meanwhile(none, none, range(3, 7))
            layer.back_inputs(m)
            meanwhile(none, none, range(7, PARTS))
            exchange(m, 1)

        return 0

    lax.fori_loop(0, 2, tick, 0)

    @pl.when(first)
    def _():
        finish_parts(1, 0, range(PARTS))
        arrive(0, upstream)
        layer.back_branches(0)
        layer.back_gelu(0)
        arrive(1, upstream)

    @pl.when(last)
    def _():
        finish_parts(1, 1, range(PARTS))

        def each(m, _):
            layer.branches(m)
            exchange(m, 0)
            return 0

        lax.fori_loop(0, 2, each, 0)

    grads = r.grads
    reduce = Reduce(place, grads, out, r.arrived, r.landing, r.send, r.recv)
    small = SmallReduce(place, r.small_mine, r.small_out, r.small_landing, r.small_pair,
                        r.small_send, r.small_recv)
    vectors, norms = r.vectors, r.norms

    def back(name):
        @pl.when(first)
        def _():
            if name == "back":
                layer.back_branches(1)
                layer.back_gelu(1)
                return

            def each(m, _):
                if name == "attend":
                    layer.back_attend(m)
                else:
                    layer.back_inputs(m)
                    exchange(m, 1)
                return 0

            lax.fori_loop(0, 2, each, 0)

    def sums():
        layer.bias_sums()
        norms[0] = vectors[pl.ds(0, 16)].astype(BF16)
        put(norms.at[0], norms.at[1], r.norms_sem.at[0], r.norms_sem.at[1], partner)
        r.small_mine[...] = vectors[...].astype(BF16)

    def norm_sums():
        take(norms.at[1], r.norms_sem.at[1])
        both = wide(norms.at[0]) + wide(norms.at[1])
        ln_row = lax.broadcasted_iota(jnp.int32, (16, COLS), 0) < 8
        r.small_mine[pl.ds(0, 16)] = jnp.where(ln_row, both, vectors[pl.ds(0, 16)]).astype(BF16)

    def copies():
        for m in range(2):
            for kind, final in ((0, r.y_out), (1, r.g_out)):
                rows = final.at[ds(m * SEQ + tensor * OWN, OWN)]
                mine = r.mine.at[kind, m]
                put(mine, rows, r.copy_send.at[kind, m], r.copy_recv.at[kind, m], partner)
                pltpu.make_async_copy(mine, rows, r.copy_own.at[kind, m]).start()

    for item in PLAN:
        if not isinstance(item, str):
            reduce.step(*item)
        elif item in ("back", "attend", "inputs"):
            back(item)
        elif item.startswith("finish"):
            finish(int(item[-1]))
        elif item.startswith("small"):
            small.step(int(item[-1]))
        elif item == "sums":
            sums()
        elif item == "norms":
            norm_sums()
        elif item == "copies":
            copies()
        else:
            layer.weight_sum(item)
    for s in range(SLABS):
        reduce.step(s, 10)
    for s in range(SLABS):
        reduce.drain(s)
    small.drain()
    take(norms.at[0], r.norms_sem.at[0])
    for m in range(2):
        for kind in range(2):
            take(r.mine.at[kind, m], r.copy_send.at[kind, m])
            take(r.mine.at[kind, m], r.copy_recv.at[kind, m])
            take(r.mine.at[kind, m], r.copy_own.at[kind, m])
        take(x.at[pl.ds(0, OWN)], r.next_send.at[m])
        take(x.at[pl.ds(0, OWN)], r.far_send.at[m])


def layer_call(*args):
    hbm, vmem = pl.BlockSpec(memory_space=pl.ANY), pl.BlockSpec(memory_space=pltpu.VMEM)
    smem = pl.BlockSpec(memory_space=pltpu.SMEM)
    rows = jax.ShapeDtypeStruct((TOKENS, WIDTH), BF16)
    return pl.pallas_call(
        layer_kernel,
        out_shape=(rows, rows, pltpu.VMEM((SLABS, SLAB_ROWS, COLS), BF16), pltpu.VMEM((SMALL, COLS), BF16)),
        in_specs=[hbm if name in IN_HBM else smem if name == "order" else vmem for name in INPUTS],
        out_specs=(hbm, hbm, vmem, vmem),
        scratch_shapes=list(SCRATCH.values()),
        compiler_params=pltpu.CompilerParams(
            collective_id=0, has_side_effects=True, vmem_limit_bytes=VMEM_LIMIT
        ),
    )(*args)


VECTORS = ((0, 2), (2, 2), (4, 2), (6, 2), (11, 2), (13, 4), (11, 2))


def widen_kernel(given, small, y_in, g_in, down, up, out, qkv, y_out, g_out, *rest):
    targets, (staged, held, rows, sems, copy_sems, row_sems) = rest[:8], rest[8:]
    passing = [(pltpu.make_async_copy(src, held.at[i], copy_sems.at[0, i]),
                pltpu.make_async_copy(held.at[i], dst, copy_sems.at[1, i]))
               for i, (src, dst) in enumerate(((y_in, y_out), (g_in, g_out)))]
    for come, _ in passing:
        come.start()
    values = small[...].astype(F32)
    moves = []
    for v, (row, count) in enumerate(VECTORS):
        for i in range(count):
            rows[v, :, pl.ds(i * COLS, COLS)] = values[row + i:row + i + 1]
        moves.append(pltpu.make_async_copy(rows.at[v, :, pl.ds(0, count * COLS)], targets[v], row_sems.at[v]))
    for t in range(3):
        moves.append(pltpu.make_async_copy(rows.at[7, :, pl.ds(t * COLS, COLS)], targets[7].at[t], row_sems.at[7 + t]))
        rows[7, :, pl.ds(t * COLS, COLS)] = values[8 + t:9 + t]
    for move in moves:
        move.start()

    def target(b):
        if b < 8:
            return down.at[pl.ds((b // 2) * COLS, COLS), pl.ds((b % 2) * COLS, COLS)]
        if b < 16:
            return up.at[pl.ds((b // 4 - 2) * COLS, COLS), pl.ds((b % 4) * COLS, COLS)]
        if b < 18:
            return out.at[:, pl.ds((b - 16) * COLS, COLS)]
        return qkv.at[(b - 18) % 3, pl.ds((b - 18) // 3 * COLS, COLS)]

    count, depth = SLABS * 4, 4
    copies = []
    for b in range(count):
        if b >= depth:
            copies[b - depth].wait()
        if b == 2 * depth:
            for come, go in passing:
                come.wait()
                go.start()
        slot = b % depth
        staged[slot] = given[b // 4, pl.ds((b % 4) * COLS, COLS)].astype(F32)
        copies.append(pltpu.make_async_copy(staged.at[slot], target(b), sems.at[slot]))
        copies[b].start()
    for b in range(count - depth, count):
        copies[b].wait()
    for move in moves + [go for _, go in passing]:
        move.wait()


def widened(grads, small, y, g):
    hbm, vmem = pl.BlockSpec(memory_space=pl.ANY), pl.BlockSpec(memory_space=pltpu.VMEM)
    shapes = [((2048, WIDTH), F32), ((WIDTH, 2048), F32), ((COLS, WIDTH), F32), ((3, WIDTH, COLS), F32),
              (y.shape, BF16), (g.shape, BF16)]
    shapes += [((1, rows * COLS), F32) for _, rows in VECTORS] + [((3, 1, COLS), F32)]
    grads, small = (pltpu.with_memory_space_constraint(a, pltpu.VMEM) for a in (grads, small))
    y, g = (pltpu.with_memory_space_constraint(a, pltpu.HBM) for a in (y, g))
    return pl.pallas_call(
        widen_kernel,
        out_shape=tuple(jax.ShapeDtypeStruct(shape, dtype) for shape, dtype in shapes),
        in_specs=[vmem, vmem] + [pl.BlockSpec(memory_space=pltpu.HBM)] * 2,
        out_specs=(hbm,) * 14,
        scratch_shapes=[pltpu.VMEM((4, COLS, COLS), F32), pltpu.VMEM((2, TOKENS, WIDTH), BF16),
                        pltpu.VMEM((8, 1, 4 * COLS), F32), DMA((4,)), DMA((2, 2)), DMA((10,))],
        compiler_params=pltpu.CompilerParams(vmem_limit_bytes=10 * 2**20),
    )(grads, small, y, g)


def shards(layer_input, cotangent, order, ln1_scale, ln1_bias, ln2_scale, ln2_bias, qkv_weight, qkv_bias,
           out_weight, out_bias, up_weight, up_bias, down_weight, down_bias):
    cos, low_sin, high_sin = (jnp.asarray(table) for table in rotary_tables())
    y, g, grads, small = layer_call(
        layer_input.reshape(TOKENS, WIDTH), cotangent.reshape(TOKENS, WIDTH), order,
        ln1_scale, ln1_bias, ln2_scale, ln2_bias,
        qkv_weight[0].transpose(1, 0, 2), qkv_bias[0], out_weight[0], out_bias, up_weight[0], up_bias,
        down_weight[0], down_bias, cos, low_sin, high_sin,
    )
    down, up, out, qkv, y, g, s1, b1, s2, b2, b_out, b_up, b_down, b_qkv = widened(grads, small, y, g)
    rows = (1, 2, 1, SEQ, WIDTH)
    return (y.reshape(rows), g.reshape(rows), s1, b1, s2, b2, qkv.transpose(1, 0, 2)[None], b_qkv.transpose(1, 0, 2),
            out[None], b_out, up[None], b_up, down[None], b_down)


def solution(mesh):
    return jax.shard_map(
        shards,
        mesh=mesh,
        in_specs=(
            P(None, "dp", None, None),
            P(None, "dp", None, None),
            P(),
            P("section", None),
            P("section", None),
            P("section", None),
            P("section", None),
            P("section", None, None, "tensor"),
            P("section", None, "tensor"),
            P("section", "tensor", None),
            P("section", None),
            P("section", None, "tensor"),
            P("section", "tensor"),
            P("section", "tensor", None),
            P("section", None),
        ),
        out_specs=(
            P("section", None, "dp", None, None),
            P("section", None, "dp", None, None),
            P("section", None),
            P("section", None),
            P("section", None),
            P("section", None),
            P("section", None, None, "tensor"),
            P("section", None, "tensor"),
            P("section", "tensor", None),
            P("section", None),
            P("section", None, "tensor"),
            P("section", "tensor"),
            P("section", "tensor", None),
            P("section", None),
        ),
        check_vma=False,
    )
```

```python
import jax
import jax.numpy as jnp
import numpy as np
from jax import lax
from jax.experimental import pallas as pl
from jax.experimental.pallas import tpu as pltpu
from jax.sharding import PartitionSpec as P

MESH = pl.DeviceIdType.MESH
VMEM_LIMIT = 50 * 2**20

SLABS = 6
SLAB_ROWS = 2048
HALF = 1024
STREAM = 512
COLS = 512
CHUNK = (128, 32)
RX_ONE = (0, 768)
RX_TWO = (256, 832)
RX_ROWS = 960
SMALL = 32


def mod4(value):
    return lax.rem(value + 4, 4)


class Place:
    def __init__(self):
        self.section = lax.axis_index("section")
        self.tensor = lax.axis_index("tensor")
        dp = lax.axis_index("dp")
        self.core = lax.rem(dp, 2)
        self.x = lax.rem(dp // 2, 4)
        self.z = dp // 8

    def at(self, z, x, core):
        return (self.section, (z * 4 + x) * 2 + core, self.tensor)

    def other_core(self):
        return self.at(self.z, self.x, 1 - self.core)

    def along(self, axis, step):
        if axis == 0:
            return self.at(self.z, mod4(self.x + step), self.core)
        return self.at(mod4(self.z + step), self.x, self.core)

    def position(self, axis):
        return self.x if axis == 0 else self.z


def ds(start, size):
    return pl.ds(pl.multiple_of(start, 16), size)


def take(ref, sem):
    pltpu.make_async_copy(ref, ref, sem).wait()


def put(src, dst, send_sem, recv_sem, device):
    pltpu.make_async_remote_copy(
        src_ref=src, dst_ref=dst, send_sem=send_sem, recv_sem=recv_sem,
        device_id=device, device_id_type=MESH,
    ).start()


def added(*parts):
    if len(parts) == 2:
        return parts[0] + parts[1]
    total = parts[0].astype(jnp.float32)
    for part in parts[1:]:
        total = total + part.astype(jnp.float32)
    return total.astype(jnp.bfloat16)


class Reduce:
    def __init__(self, place, grads, out, arrived, landing, send, recv):
        self.place, self.grads, self.out = place, grads, out
        self.arrived, self.landing, self.send, self.recv = arrived, landing, send, recv

    def base(self, stream):
        return self.place.core * HALF + stream * STREAM

    def layout(self, stream, phase):
        axis = (stream + phase) % 2
        p = self.place.position(axis)
        start = self.base(stream)
        if phase == 1:
            start = start + self.place.position(stream) * CHUNK[0]
        return axis, p, start, CHUNK[phase]

    def first_sends(self, s, phase, sem):
        h = CHUNK[phase] // 2
        for stream in range(2):
            axis, p, start, size = self.layout(stream, phase)
            far = start + mod4(p + 2) * size
            for side, step in ((0, 1), (1, -1)):
                put(self.grads.at[s, ds(far + side * h, h)],
                    self.landing.at[s, pl.ds(RX_ONE[phase] + (stream * 2 + side) * h, h)],
                    self.send.at[s, 0], self.recv.at[s, sem], self.place.along(axis, step))

    def second_sends(self, s, phase, sem):
        h = CHUNK[phase] // 2
        take(self.landing.at[s, pl.ds(0, 4 * h)], self.recv.at[s, sem - 1])
        for stream in range(2):
            axis, p, start, size = self.layout(stream, phase)
            for side, step in ((0, 1), (1, -1)):
                near = start + mod4(p + step) * size
                rows = ds(near + side * h, h)
                came = pl.ds(RX_ONE[phase] + (stream * 2 + side) * h, h)
                self.grads[s, rows] = added(self.grads[s, rows], self.landing[s, came])
                put(self.grads.at[s, ds(near, size)],
                    self.landing.at[s, pl.ds(RX_TWO[phase] + (stream * 2 + side) * size, size)],
                    self.send.at[s, 0], self.recv.at[s, sem], self.place.along(axis, step))

    def finish(self, s, phase, sem, target):
        size = CHUNK[phase]
        take(self.landing.at[s, pl.ds(0, 4 * size)], self.recv.at[s, sem])
        for stream in range(2):
            axis, p, start, size = self.layout(stream, phase)
            rows = ds(start + p * size, size)
            left = pl.ds(RX_TWO[phase] + stream * 2 * size, size)
            right = pl.ds(RX_TWO[phase] + (stream * 2 + 1) * size, size)
            target[s, rows] = added(self.grads[s, rows], self.landing[s, left], self.landing[s, right])

    def spread(self, s, phase, sem):
        for stream in range(2):
            axis, p, start, size = self.layout(stream, phase)
            rows = ds(start + p * size, size)
            for step in (1, -1):
                put(self.out.at[s, rows], self.out.at[s, rows], self.send.at[s, 1],
                    self.recv.at[s, sem], self.place.along(axis, step))

    def forward(self, s, phase, sem):
        size = CHUNK[phase]
        take(self.out.at[s, pl.ds(0, 4 * size)], self.recv.at[s, sem - 1])
        for stream in range(2):
            axis, p, start, size = self.layout(stream, phase)
            for side, step in ((0, 1), (1, -1)):
                rows = ds(start + mod4(p - step) * size + side * (size // 2), size // 2)
                put(self.out.at[s, rows], self.out.at[s, rows], self.send.at[s, 1],
                    self.recv.at[s, sem], self.place.along(axis, step))

    def to_core(self, s, offsets):
        for stream in range(2):
            axis, p, start, size = self.layout(stream, 0)
            for offset in offsets:
                rows = ds(start + mod4(p + offset) * size, size)
                put(self.out.at[s, rows], self.out.at[s, rows], self.send.at[s, 1],
                    self.recv.at[s, 9], self.place.other_core())

    def step(self, s, k):
        core = self.place.core
        if k == 0:
            put(self.grads.at[s, ds((1 - core) * HALF, HALF)], self.arrived.at[s],
                self.send.at[s, 0], self.recv.at[s, 0], self.place.other_core())
        elif k == 1:
            take(self.arrived.at[s], self.recv.at[s, 0])

            def block(i, _):
                here = ds(core * HALF + i * 128, 128)
                self.grads[s, here] = added(self.grads[s, here], self.arrived[s, ds(i * 128, 128)])
                return 0

            lax.fori_loop(0, HALF // 128, block, 0)
            self.first_sends(s, 0, 1)
        elif k == 2:
            self.second_sends(s, 0, 2)
        elif k == 3:
            self.finish(s, 0, 2, self.grads)
            self.first_sends(s, 1, 3)
        elif k == 4:
            self.second_sends(s, 1, 4)
        elif k == 5:
            self.finish(s, 1, 4, self.out)
            self.spread(s, 1, 5)
        elif k == 6:
            self.forward(s, 1, 6)
        elif k == 7:
            take(self.out.at[s, pl.ds(0, 64)], self.recv.at[s, 6])
            self.spread(s, 0, 7)
            self.to_core(s, (0,))
        elif k == 8:
            self.forward(s, 0, 8)
            self.to_core(s, (1, -1))
        elif k == 9:
            take(self.out.at[s, pl.ds(0, 256)], self.recv.at[s, 8])
            self.to_core(s, (2,))
        elif k == 10:
            take(self.out.at[s, pl.ds(0, 1024)], self.recv.at[s, 9])

    def drain(self, s):
        take(self.grads.at[s, pl.ds(0, 1984)], self.send.at[s, 0])
        take(self.grads.at[s, pl.ds(0, 1984)], self.send.at[s, 1])


class SmallReduce:
    def __init__(self, place, mine, out, landing, pair, send, recv):
        self.place, self.mine, self.out, self.landing, self.pair = place, mine, out, landing, pair
        self.send, self.recv = send, recv

    def exchange(self, axis):
        p = self.place.position(axis)
        for step in (1, 2, 3):
            put(self.landing.at[axis, p], self.landing.at[axis, p], self.send, self.recv.at[1 + axis],
                self.place.along(axis, step))

    def collected(self, axis):
        take(self.landing.at[axis, pl.ds(0, 3)], self.recv.at[1 + axis])
        return added(*[self.landing[axis, j] for j in range(4)])

    def step(self, k):
        half = SMALL // 2
        rows = ds(self.place.core * half, half)
        if k == 0:
            put(self.mine, self.pair, self.send, self.recv.at[0], self.place.other_core())
        elif k == 1:
            take(self.pair, self.recv.at[0])
            self.landing[0, self.place.x] = added(self.mine[rows], self.pair[rows])
            self.exchange(0)
        elif k == 2:
            self.landing[1, self.place.z] = self.collected(0)
            self.exchange(1)
        elif k == 3:
            self.out[rows] = self.collected(1)
            put(self.out.at[rows], self.out.at[rows], self.send, self.recv.at[3], self.place.other_core())
        elif k == 4:
            take(self.out.at[pl.ds(0, half)], self.recv.at[3])

    def drain(self):
        half = SMALL // 2
        take(self.landing.at[0, pl.ds(0, 3)], self.send)
        take(self.landing.at[0, pl.ds(0, 3)], self.send)
        take(self.mine, self.send)
        take(self.out.at[pl.ds(0, half)], self.send)


def greet(devices):
    for device in devices:
        pl.semaphore_signal(pltpu.get_barrier_semaphore(), inc=1, device_id=device, device_id_type=MESH)


def met(count):
    pl.semaphore_wait(pltpu.get_barrier_semaphore(), count)


def plane_partners(place):
    return [place.other_core()] + [place.along(axis, step) for axis in (0, 1) for step in (1, 2, 3)]


PLAN = (
    "down00", (0, 0), "down01", "down10", (1, 0), "down11", (0, 1), "back",
    (1, 1), "up0", (2, 0), (0, 2), "up1", (3, 0), (2, 1), (1, 2),
    "attend10", "attend11", "inputs10", (3, 1), "inputs11", "last0", (4, 0), (0, 3),
    "last1", (5, 0), (2, 2), (4, 1), (1, 3), "sums", (5, 1), (3, 2),
    (0, 4), (2, 3), (4, 2), (1, 4), "norms", "small0", (5, 2), (3, 3),
    (0, 5), (2, 4), (4, 3), (1, 5), "finish0", (5, 3), (3, 4), "small1",
    "finish1", (0, 6), "copies", (2, 5), (4, 4), (1, 6), (5, 4), (3, 5),
    "small2", (0, 7), (2, 6), (4, 5), (1, 7), (5, 5), (3, 6), (0, 8),
    (2, 7), "small3", (4, 6), (1, 8), (5, 6), (3, 7), (0, 9), (2, 8),
    (4, 7), (1, 9), "small4", (5, 7), (3, 8), (2, 9), (4, 8), (5, 8),
    (3, 9), (4, 9), (5, 9),
)

SEQ = 256
TOKENS = 2 * SEQ
OWN = SEQ // 2
PARTS = 8
PART = OWN // PARTS
WIDTH = 1024
HEAD = 64
ROT = 16
EPSILON = 1e-05
BF16 = jnp.bfloat16
F32 = jnp.float32


def nn(a, b):
    return lax.dot_general(a, b, (((1,), (0,)), ((), ())), preferred_element_type=F32)


def nt(a, b):
    return lax.dot_general(a, b, (((1,), (1,)), ((), ())), preferred_element_type=F32)


def tn(a, b):
    return lax.dot_general(a, b, (((0,), (0,)), ((), ())), preferred_element_type=F32)


def wide(ref):
    return ref[...].astype(F32)


def block(index, size):
    return pl.ds(pl.multiple_of(index * size, size), size)


def one_head(pair, h):
    lane = lax.broadcasted_iota(jnp.int32, pair.shape, 1)
    return jnp.where((lane < HEAD) if h == 0 else (lane >= HEAD), pair, jnp.zeros_like(pair))


def rotary_tables():
    frequency = (1.0 / 10000.0 ** (np.arange(ROT // 2) * 2.0 / ROT)).astype(np.float32)
    angles = np.arange(SEQ, dtype=np.float32)[:, None] * frequency[None, :]
    cos, sin = np.cos(angles), np.sin(angles)
    cos_table = np.ones((SEQ, 128), np.float32)
    low_sin, high_sin = np.zeros((SEQ, 128), np.float32), np.zeros((SEQ, 128), np.float32)
    for head in range(128 // HEAD):
        first, second = head * HEAD, head * HEAD + ROT // 2
        cos_table[:, first:second] = cos
        cos_table[:, second:second + ROT // 2] = cos
        low_sin[:, first:second] = sin
        high_sin[:, second:second + ROT // 2] = sin
    return cos_table, low_sin, high_sin


def rotated(u, tables, sign):
    cos, low_sin, high_sin = tables
    ahead = pltpu.roll(u, 128 - ROT // 2, 1)
    behind = pltpu.roll(u, ROT // 2, 1)
    return u * cos + (behind * high_sin - ahead * low_sin) * sign


class Layer:
    def __init__(self, refs):
        self.__dict__.update(refs)

    def up_block(self, n, rows):
        return self.out.at[4 + n // 2, pl.ds((n % 2) * WIDTH + rows[0], rows[1])]

    def slope_block(self, m, n):
        return self.grads.at[4, ds(n * COLS + m * SEQ, SEQ)]

    def norm(self, m):
        rows = block(m, SEQ)
        x = wide(self.x.at[rows])
        mean = jnp.mean(x, axis=1, keepdims=True)
        centered = x - mean
        rstd = lax.rsqrt(jnp.mean(centered * centered, axis=1, keepdims=True) + EPSILON)
        normed = centered * rstd
        self.mean[rows] = mean
        self.rstd[rows] = rstd
        self.first_in[rows] = (normed * wide(self.ln1_scale) + wide(self.ln1_bias)).astype(BF16)
        self.second_in[rows] = (normed * wide(self.ln2_scale) + wide(self.ln2_bias)).astype(BF16)

    def project(self, m):
        rows = block(m, SEQ)
        tables = (self.cos[...], self.low_sin[...], self.high_sin[...])
        bias = wide(self.qkv_bias)
        for t in range(3):
            part = nn(self.first_in[rows], self.qkv_w[t]) + bias[t:t + 1]
            for lane in range(0, COLS, 128):
                piece = part[:, lane:lane + 128]
                if t < 2:
                    piece = rotated(piece, tables, 1.0)
                if t == 0:
                    piece = piece * HEAD ** -0.5
                self.qkv[t, rows, pl.ds(lane, 128)] = piece.astype(BF16)

    def attend(self, m):
        rows = block(m, SEQ)
        causal = (lax.broadcasted_iota(jnp.int32, (SEQ, SEQ), 0)
                  >= lax.broadcasted_iota(jnp.int32, (SEQ, SEQ), 1))
        for hp in range(4):
            lanes = pl.ds(hp * 128, 128)
            q, k, v = (self.qkv[t, rows, lanes] for t in range(3))
            context = None
            for h in range(2):
                scores = jnp.where(causal, nt(one_head(q, h), k), -1e30)
                exp = jnp.exp(scores - jnp.max(scores, axis=1, keepdims=True))
                probs = (exp * (1.0 / jnp.sum(exp, axis=1, keepdims=True))).astype(BF16)
                self.probs[m, hp * 2 + h] = probs
                part = nn(probs, one_head(v, h))
                context = part if context is None else context + part
            self.context[rows, lanes] = context.astype(BF16)

    def up(self, m):
        rows = block(m, SEQ)
        bias = wide(self.up_bias)
        for n in range(4):
            hidden = nn(self.second_in[rows], self.up_block(n, (0, WIDTH))[...])
            hidden = hidden + bias[:, n * COLS:(n + 1) * COLS]
            cdf = 0.5 * (1.0 + lax.erf(hidden * 0.7071067811865476))
            density = jnp.exp(-0.5 * hidden * hidden) * 0.3989422804014327
            lanes = pl.ds(n * COLS, COLS)
            self.activated[rows, lanes] = (hidden * cdf).astype(BF16)
            self.slope_block(m, n)[...] = (cdf + hidden * density).astype(BF16)

    def branches(self, m, start=0, count=SEQ):
        rows, here = ds(m * SEQ + start, count), ds(start, count)
        for j in range(2):
            lanes = pl.ds(j * COLS, COLS)
            total = nn(self.context[rows], self.out_w[:, lanes])
            total = total + nn(self.activated[rows], self.out[2 + j])
            self.partial[m, here, lanes] = total.astype(BF16)

    def back_branches(self, m):
        rows = block(m, SEQ)
        upstream = self.upstream[rows]
        self.d_context[rows] = nt(upstream, self.out_w[...]).astype(BF16)
        for n in range(4):
            down = pl.ds(n * COLS, COLS)
            part = nt(upstream[:, :COLS], self.out[2, down]) + nt(upstream[:, COLS:], self.out[3, down])
            self.d_hidden[rows, down] = part.astype(BF16)

    def back_gelu(self, m):
        rows = block(m, SEQ)
        for n in range(4):
            lanes = pl.ds(n * COLS, COLS)
            self.d_hidden[rows, lanes] = (
                wide(self.d_hidden.at[rows, lanes]) * wide(self.slope_block(m, n))
            ).astype(BF16)

    def back_attend(self, m, pairs=range(4)):
        rows = block(m, SEQ)
        tables = (self.cos[...], self.low_sin[...], self.high_sin[...])
        for hp in pairs:
            lanes = pl.ds(hp * 128, 128)
            q, k, v = (self.qkv[t, rows, lanes] for t in range(3))
            d_context = self.d_context[rows, lanes]
            probs = [self.probs[m, hp * 2 + h] for h in range(2)]
            d_mine = [one_head(d_context, h) for h in range(2)]
            d_scores = []
            for h in range(2):
                wide_probs = probs[h].astype(F32)
                weighted = nt(d_mine[h], v) * wide_probs
                inner = jnp.sum(weighted, axis=1, keepdims=True)
                d_scores.append((weighted - wide_probs * inner).astype(BF16))
            both = [jnp.concatenate([one_head(u, 0), one_head(u, 1)], axis=0) for u in (q, k)]
            d_query = nn(jnp.concatenate(d_scores, axis=1), both[1])
            d_key = tn(jnp.concatenate(d_scores, axis=0), both[0])
            d_value = tn(jnp.concatenate(probs, axis=0), jnp.concatenate(d_mine, axis=0))
            d_query = rotated(d_query * HEAD ** -0.5, tables, -1.0)
            d_key = rotated(d_key, tables, -1.0)
            for t, part in enumerate((d_query, d_key, d_value)):
                self.d_projected[t, rows, lanes] = part.astype(BF16)

    def back_inputs(self, m, halves=range(2), start=0, count=SEQ):
        rows, here = ds(m * SEQ + start, count), ds(start, count)
        mean, rstd = self.mean[rows], self.rstd[rows]
        for j in halves:
            lanes = pl.ds(j * COLS, COLS)
            d_second = None
            for n in range(4):
                part = nt(self.d_hidden[rows, pl.ds(n * COLS, COLS)], self.up_block(n, (j * COLS, COLS))[...])
                d_second = part if d_second is None else d_second + part
            d_first = None
            for t in range(3):
                part = nt(self.d_projected[t, rows], self.qkv_w[t, lanes])
                d_first = part if d_first is None else d_first + part
            normed = (wide(self.x.at[rows, lanes]) - mean) * rstd
            sums = (d_first * normed, d_first, d_second * normed, d_second)
            for i, value in enumerate(sums):
                row = pl.ds(2 * i + j, 1)
                self.vectors[row] = self.vectors[row] + jnp.sum(value, axis=0, keepdims=True)
            d_normed = d_first * wide(self.ln1_scale.at[:, lanes]) + d_second * wide(self.ln2_scale.at[:, lanes])
            self.partial[m, here, lanes] = d_normed.astype(BF16)

    def weight_sum(self, name):
        def product(left, columns, targets):
            turned = left[:, columns].T
            for right, b in targets:
                self.grads[b // 4, pl.ds((b % 4) * COLS, COLS)] = nn(turned, right).astype(BF16)

        upstream = [self.upstream[:, pl.ds(c * COLS, COLS)] for c in range(2)]
        if name.startswith("down"):
            slab, half = int(name[-2]), self.core if int(name[-1]) else 1 - self.core
            turned = self.activated[:, ds((2 * slab + half) * COLS, COLS)].T
            for c in range(2):
                self.grads[slab, ds((2 * half + c) * COLS, COLS)] = nn(turned, upstream[c]).astype(BF16)
        elif name in ("up0", "up1"):
            r = int(name == "up1")
            d_hidden = [self.d_hidden[:, pl.ds(n * COLS, COLS)] for n in range(4)]
            product(self.second_in, pl.ds(r * COLS, COLS), [(d_hidden[n], 8 + 4 * r + n) for n in range(4)])
        else:
            r = int(name == "last1")
            if r == 0:
                product(self.context, pl.ds(0, COLS), [(upstream[c], 16 + c) for c in range(2)])
            d_projected = [self.d_projected[t] for t in range(3)]
            product(self.first_in, pl.ds(r * COLS, COLS), [(d_projected[t], 18 + 3 * r + t) for t in range(3)])

    def bias_sums(self):
        for t in range(3):
            self.vectors[pl.ds(8 + t, 1)] = jnp.sum(wide(self.d_projected.at[t]), axis=0, keepdims=True)
        for j in range(2):
            lanes = pl.ds(j * COLS, COLS)
            self.vectors[pl.ds(11 + j, 1)] = jnp.sum(wide(self.upstream.at[:, lanes]), axis=0, keepdims=True)
        for n in range(4):
            lanes = pl.ds(n * COLS, COLS)
            self.vectors[pl.ds(13 + n, 1)] = jnp.sum(wide(self.d_hidden.at[:, lanes]), axis=0, keepdims=True)


INPUTS = ("x_in", "cot_in", "order", "ln1_scale", "ln1_bias", "ln2_scale", "ln2_bias", "qkv_in", "qkv_bias",
          "out_in", "out_bias", "up_in", "up_bias", "down_in", "down_bias", "cos", "low_sin", "high_sin")
IN_HBM = ("x_in", "cot_in", "qkv_in", "out_in", "up_in", "down_in")
OUTPUTS = ("y_out", "g_out", "out", "small_out")
DMA = pltpu.SemaphoreType.DMA
SCRATCH = dict(
    grads=pltpu.VMEM((SLABS, SLAB_ROWS, COLS), BF16),
    arrived=pltpu.VMEM((SLABS, HALF, COLS), BF16),
    landing=pltpu.VMEM((SLABS, RX_ROWS, COLS), BF16),
    x=pltpu.VMEM((TOKENS, WIDTH), BF16),
    upstream=pltpu.VMEM((TOKENS, WIDTH), BF16),
    first_in=pltpu.VMEM((TOKENS, WIDTH), BF16),
    second_in=pltpu.VMEM((TOKENS, WIDTH), BF16),
    qkv=pltpu.VMEM((3, TOKENS, COLS), BF16),
    d_projected=pltpu.VMEM((3, TOKENS, COLS), BF16),
    context=pltpu.VMEM((TOKENS, COLS), BF16),
    d_context=pltpu.VMEM((TOKENS, COLS), BF16),
    probs=pltpu.VMEM((2, 8, SEQ, SEQ), BF16),
    activated=pltpu.VMEM((TOKENS, 4 * COLS), BF16),
    d_hidden=pltpu.VMEM((TOKENS, 4 * COLS), BF16),
    partial=pltpu.VMEM((2, SEQ, WIDTH), BF16),
    came=pltpu.VMEM((2, 2, OWN, WIDTH), BF16),
    mine=pltpu.VMEM((2, 2, OWN, WIDTH), BF16),
    mean=pltpu.VMEM((TOKENS, 1), F32),
    rstd=pltpu.VMEM((TOKENS, 1), F32),
    vectors=pltpu.VMEM((SMALL, COLS), F32),
    qkv_w=pltpu.VMEM((3, WIDTH, COLS), BF16),
    out_w=pltpu.VMEM((COLS, WIDTH), BF16),
    small_mine=pltpu.VMEM((SMALL, COLS), BF16),
    small_landing=pltpu.VMEM((2, 4, SMALL // 2, COLS), BF16),
    small_pair=pltpu.VMEM((SMALL, COLS), BF16),
    norms=pltpu.VMEM((2, 16, COLS), BF16),
    send=DMA((SLABS, 2)),
    recv=DMA((SLABS, 10)),
    small_send=DMA,
    small_recv=DMA((4,)),
    load=DMA((5,)),
    pair_send=DMA((2, 2)),
    pair_recv=DMA((2, 2, PARTS)),
    next_send=DMA((2,)),
    next_recv=DMA((2, PARTS)),
    far_send=DMA((2,)),
    far_recv=DMA((2,)),
    copy_send=DMA((2, 2)),
    copy_recv=DMA((2, 2)),
    copy_own=DMA((2, 2)),
    norms_sem=DMA((2,)),
)


class Refs:
    def __init__(self, pairs):
        self.__dict__.update(pairs)


def layer_kernel(*refs):
    names = INPUTS + OUTPUTS + tuple(SCRATCH)
    r = Refs(zip(names, refs))
    layer, place = Layer(vars(r)), Place()
    layer.core = place.core
    section, tensor = place.section, place.tensor
    first, last = section == 0, section == 1
    dp = lax.axis_index("dp")
    partner = (section, dp, 1 - tensor)
    near = (1 - section, dp, 1 - tensor)
    others = plane_partners(place) + [partner, near]
    load = r.load
    out, x, upstream = r.out, r.x, r.upstream

    greet(others)

    def fetch(src, dst, sem):
        pltpu.make_async_copy(src, dst, load.at[sem]).start()

    def fetch_out():
        fetch(r.out_in, r.out_w, 3)
        for c in range(2):
            fetch(r.down_in.at[:, pl.ds(c * COLS, COLS)], out.at[2 + c], 4)

    def fetch_up():
        for n in range(4):
            fetch(r.up_in.at[:, pl.ds(n * COLS, COLS)], layer.up_block(n, (0, WIDTH)), 2)

    @pl.when(first)
    def _():
        fetch(r.x_in, x, 0)
        fetch(r.qkv_in, r.qkv_w, 1)
        take(x, load.at[0])
        fetch_up()
        fetch_out()

    @pl.when(last)
    def _():
        fetch(r.cot_in, r.activated.at[:, pl.ds(0, WIDTH)], 0)
        fetch_out()
        fetch(r.qkv_in, r.qkv_w, 1)
        fetch_up()

    @pl.when(last)
    def _():
        given = r.activated
        take(upstream, load.at[0])
        swap = r.order[0] != 0
        one, two = given[pl.ds(0, SEQ), pl.ds(0, WIDTH)], given[pl.ds(SEQ, SEQ), pl.ds(0, WIDTH)]
        upstream[pl.ds(0, SEQ)] = jnp.where(swap, two, one)
        upstream[pl.ds(SEQ, SEQ)] = jnp.where(swap, one, two)
        take(r.out_w, load.at[3])
        take(out.at[pl.ds(2, 2)], load.at[4])

        def each(m, _):
            layer.back_branches(m)
            return 0

        lax.fori_loop(0, 2, each, 0)
        met(len(others))

    r.vectors[...] = jnp.zeros((SMALL, COLS), F32)

    own_half, other_half = tensor * OWN, (1 - tensor) * OWN

    def part_of(start, c):
        return ds(start + c * PART, PART)

    def exchange(m, kind):
        for c in range(PARTS):
            put(r.partial.at[m, part_of((1 - tensor) * OWN, c)], r.came.at[kind, m, part_of(0, c)],
                r.pair_send.at[kind, m], r.pair_recv.at[kind, m, c], partner)

    def finish_part(m, kind, c):
        rows = part_of(m * SEQ + tensor * OWN, c)
        here = part_of(0, c)
        came = r.came.at[kind, m, here]
        take(came, r.pair_recv.at[kind, m, c])
        total = wide(r.partial.at[m, part_of(tensor * OWN, c)]) + wide(came)
        if kind == 0:
            result = wide(x.at[rows]) + total + (wide(r.out_bias) + wide(r.down_bias))
        else:
            rstd = r.rstd[rows]
            normed = (wide(x.at[rows]) - r.mean[rows]) * rstd
            centered = (total - jnp.mean(total, axis=1, keepdims=True)
                        - normed * jnp.mean(total * normed, axis=1, keepdims=True))
            result = wide(upstream.at[rows]) + rstd * centered
        mine = r.mine.at[kind, m, here]
        mine[...] = result.astype(BF16)
        target = upstream if kind else x

        @pl.when(last if kind else first)
        def _():
            put(mine, target.at[rows], r.next_send.at[m], r.next_recv.at[m, c], near)

    def finish_parts(m, kind, parts):
        for c in parts:
            finish_part(m, kind, c)
        if PARTS - 1 in parts:
            take(r.came.at[kind, m], r.pair_send.at[kind, m])

    def finish(m):
        for kind, chosen in ((0, last), (1, first)):
            @pl.when(chosen)
            def _(kind=kind):
                finish_parts(m, kind, range(PARTS))

    def pass_on(m, target, parts):
        for c in parts:
            rows = target.at[part_of(m * SEQ + (1 - tensor) * OWN, c)]
            take(rows, r.next_recv.at[m, c])
            put(rows, rows, r.far_send.at[m], r.far_recv.at[m], partner)

    def arrived(m, target):
        take(target.at[pl.ds(0, OWN)], r.far_recv.at[m])

    def arrive(m, target):
        pass_on(m, target, range(PARTS))
        arrived(m, target)

    def tick(i, _):
        m = i

        def when(condition, action, *args):
            if isinstance(args[-1], range) and not args[-1]:
                return

            @pl.when(condition)
            def _():
                action(*args)

        def meanwhile(first_parts, next_parts, last_parts):
            when(jnp.logical_and(first, i == 1), finish_parts, 0, 0, first_parts)
            when(jnp.logical_and(last, i == 0), pass_on, 1, x, next_parts)
            when(jnp.logical_and(last, i == 1), finish_parts, 0, 1, last_parts)

        none = range(0)
        when(jnp.logical_and(last, i == 0), arrive, 0, x)
        when(jnp.logical_and(last, i == 1), arrived, 1, x)
        layer.norm(m)
        when(i == 0, take, r.qkv_w, load.at[1])
        layer.project(m)
        meanwhile(none, range(0, 2), none)
        layer.attend(m)
        meanwhile(range(0, 1), range(2, 5), range(0, 1))
        when(i == 0, take, out.at[pl.ds(4, 2)], load.at[2])
        layer.up(m)
        meanwhile(range(1, 4), range(5, PARTS), range(1, 4))

        @pl.when(jnp.logical_and(first, i == 0))
        def _():
            take(r.out_w, load.at[3])
            take(out.at[pl.ds(2, 2)], load.at[4])
            met(len(others))

        @pl.when(first)
        def _():
            layer.branches(m, other_half, OWN)
            meanwhile(range(4, PARTS), none, none)
            exchange(m, 0)
            layer.branches(m, own_half, OWN)

        @pl.when(last)
        def _():
            layer.back_gelu(m)
            layer.back_attend(m)
            meanwhile(none, none, range(4, PARTS))
            layer.back_inputs(m)
            exchange(m, 1)

        return 0

    lax.fori_loop(0, 2, tick, 0)

    @pl.when(first)
    def _():
        finish_parts(1, 0, range(PARTS))
        arrive(0, upstream)
        layer.back_branches(0)
        layer.back_gelu(0)
        layer.back_attend(0, range(0, 2))
        pass_on(1, upstream, range(0, 1))
        layer.back_attend(0, range(2, 4))
        pass_on(1, upstream, range(1, 3))
        layer.back_inputs(0, range(0, 1))
        pass_on(1, upstream, range(3, 5))
        layer.back_inputs(0, range(1, 2))
        pass_on(1, upstream, range(5, PARTS))
        exchange(0, 1)
        arrived(1, upstream)

    @pl.when(last)
    def _():
        finish_parts(1, 1, range(PARTS))

        def each(m, _):
            layer.branches(m)
            exchange(m, 0)
            return 0

        lax.fori_loop(0, 2, each, 0)

    grads = r.grads
    reduce = Reduce(place, grads, out, r.arrived, r.landing, r.send, r.recv)
    small = SmallReduce(place, r.small_mine, r.small_out, r.small_landing, r.small_pair,
                        r.small_send, r.small_recv)
    vectors, norms = r.vectors, r.norms

    def back(name):
        @pl.when(first)
        def _():
            if name == "back":
                layer.back_branches(1)
                layer.back_gelu(1)
                return
            m, half = int(name[-2]), int(name[-1])
            if name.startswith("attend"):
                layer.back_attend(m, range(2 * half, 2 * half + 2))
            else:
                layer.back_inputs(m, range(half, half + 1))
                if half:
                    exchange(m, 1)

    def sums():
        layer.bias_sums()
        norms[0] = vectors[pl.ds(0, 16)].astype(BF16)
        put(norms.at[0], norms.at[1], r.norms_sem.at[0], r.norms_sem.at[1], partner)
        r.small_mine[...] = vectors[...].astype(BF16)

    def norm_sums():
        take(norms.at[1], r.norms_sem.at[1])
        both = wide(norms.at[0]) + wide(norms.at[1])
        ln_row = lax.broadcasted_iota(jnp.int32, (16, COLS), 0) < 8
        r.small_mine[pl.ds(0, 16)] = jnp.where(ln_row, both, vectors[pl.ds(0, 16)]).astype(BF16)

    def copies():
        for m in range(2):
            for kind, final in ((0, r.y_out), (1, r.g_out)):
                rows = final.at[ds(m * SEQ + tensor * OWN, OWN)]
                mine = r.mine.at[kind, m]
                put(mine, rows, r.copy_send.at[kind, m], r.copy_recv.at[kind, m], partner)
                pltpu.make_async_copy(mine, rows, r.copy_own.at[kind, m]).start()

    for item in PLAN:
        if not isinstance(item, str):
            reduce.step(*item)
        elif item[:4] in ("back", "atte", "inpu"):
            back(item)
        elif item.startswith("finish"):
            finish(int(item[-1]))
        elif item.startswith("small"):
            small.step(int(item[-1]))
        elif item == "sums":
            sums()
        elif item == "norms":
            norm_sums()
        elif item == "copies":
            copies()
        else:
            layer.weight_sum(item)
    for s in range(SLABS):
        reduce.step(s, 10)
    for s in range(SLABS):
        reduce.drain(s)
    small.drain()
    take(norms.at[0], r.norms_sem.at[0])
    for m in range(2):
        for kind in range(2):
            take(r.mine.at[kind, m], r.copy_send.at[kind, m])
            take(r.mine.at[kind, m], r.copy_recv.at[kind, m])
            take(r.mine.at[kind, m], r.copy_own.at[kind, m])
        take(x.at[pl.ds(0, OWN)], r.next_send.at[m])
        take(x.at[pl.ds(0, OWN)], r.far_send.at[m])


def layer_call(*args):
    hbm, vmem = pl.BlockSpec(memory_space=pl.ANY), pl.BlockSpec(memory_space=pltpu.VMEM)
    smem = pl.BlockSpec(memory_space=pltpu.SMEM)
    rows = jax.ShapeDtypeStruct((TOKENS, WIDTH), BF16)
    return pl.pallas_call(
        layer_kernel,
        out_shape=(rows, rows, pltpu.VMEM((SLABS, SLAB_ROWS, COLS), BF16), pltpu.VMEM((SMALL, COLS), BF16)),
        in_specs=[hbm if name in IN_HBM else smem if name == "order" else vmem for name in INPUTS],
        out_specs=(hbm, hbm, vmem, vmem),
        scratch_shapes=list(SCRATCH.values()),
        compiler_params=pltpu.CompilerParams(
            collective_id=0, has_side_effects=True, vmem_limit_bytes=VMEM_LIMIT
        ),
    )(*args)


VECTORS = ((0, 2), (2, 2), (4, 2), (6, 2), (11, 2), (13, 4), (11, 2))


def widen_kernel(given, small, y_in, g_in, down, up, out, qkv, y_out, g_out, *rest):
    targets, (staged, held, rows, sems, copy_sems, row_sems) = rest[:8], rest[8:]
    passing = [(pltpu.make_async_copy(src, held.at[i], copy_sems.at[0, i]),
                pltpu.make_async_copy(held.at[i], dst, copy_sems.at[1, i]))
               for i, (src, dst) in enumerate(((y_in, y_out), (g_in, g_out)))]
    for come, _ in passing:
        come.start()
    values = small[...].astype(F32)
    moves = []
    for v, (row, count) in enumerate(VECTORS):
        for i in range(count):
            rows[v, :, pl.ds(i * COLS, COLS)] = values[row + i:row + i + 1]
        moves.append(pltpu.make_async_copy(rows.at[v, :, pl.ds(0, count * COLS)], targets[v], row_sems.at[v]))
    for t in range(3):
        moves.append(pltpu.make_async_copy(rows.at[7, :, pl.ds(t * COLS, COLS)], targets[7].at[t], row_sems.at[7 + t]))
        rows[7, :, pl.ds(t * COLS, COLS)] = values[8 + t:9 + t]
    for move in moves:
        move.start()

    def target(b):
        if b < 8:
            return down.at[pl.ds((b // 2) * COLS, COLS), pl.ds((b % 2) * COLS, COLS)]
        if b < 16:
            return up.at[pl.ds((b // 4 - 2) * COLS, COLS), pl.ds((b % 4) * COLS, COLS)]
        if b < 18:
            return out.at[:, pl.ds((b - 16) * COLS, COLS)]
        return qkv.at[(b - 18) % 3, pl.ds((b - 18) // 3 * COLS, COLS)]

    count, depth = SLABS * 4, 4
    copies = []
    for b in range(count):
        if b >= depth:
            copies[b - depth].wait()
        if b == 2 * depth:
            for come, go in passing:
                come.wait()
                go.start()
        slot = b % depth
        staged[slot] = given[b // 4, pl.ds((b % 4) * COLS, COLS)].astype(F32)
        copies.append(pltpu.make_async_copy(staged.at[slot], target(b), sems.at[slot]))
        copies[b].start()
    for b in range(count - depth, count):
        copies[b].wait()
    for move in moves + [go for _, go in passing]:
        move.wait()


def widened(grads, small, y, g):
    hbm, vmem = pl.BlockSpec(memory_space=pl.ANY), pl.BlockSpec(memory_space=pltpu.VMEM)
    shapes = [((2048, WIDTH), F32), ((WIDTH, 2048), F32), ((COLS, WIDTH), F32), ((3, WIDTH, COLS), F32),
              (y.shape, BF16), (g.shape, BF16)]
    shapes += [((1, rows * COLS), F32) for _, rows in VECTORS] + [((3, 1, COLS), F32)]
    grads, small = (pltpu.with_memory_space_constraint(a, pltpu.VMEM) for a in (grads, small))
    y, g = (pltpu.with_memory_space_constraint(a, pltpu.HBM) for a in (y, g))
    return pl.pallas_call(
        widen_kernel,
        out_shape=tuple(jax.ShapeDtypeStruct(shape, dtype) for shape, dtype in shapes),
        in_specs=[vmem, vmem] + [pl.BlockSpec(memory_space=pltpu.HBM)] * 2,
        out_specs=(hbm,) * 14,
        scratch_shapes=[pltpu.VMEM((4, COLS, COLS), F32), pltpu.VMEM((2, TOKENS, WIDTH), BF16),
                        pltpu.VMEM((8, 1, 4 * COLS), F32), DMA((4,)), DMA((2, 2)), DMA((10,))],
        compiler_params=pltpu.CompilerParams(vmem_limit_bytes=10 * 2**20),
    )(grads, small, y, g)


def shards(layer_input, cotangent, order, ln1_scale, ln1_bias, ln2_scale, ln2_bias, qkv_weight, qkv_bias,
           out_weight, out_bias, up_weight, up_bias, down_weight, down_bias):
    cos, low_sin, high_sin = (jnp.asarray(table) for table in rotary_tables())
    y, g, grads, small = layer_call(
        layer_input.reshape(TOKENS, WIDTH), cotangent.reshape(TOKENS, WIDTH), order,
        ln1_scale, ln1_bias, ln2_scale, ln2_bias,
        qkv_weight[0].transpose(1, 0, 2), qkv_bias[0], out_weight[0], out_bias, up_weight[0], up_bias,
        down_weight[0], down_bias, cos, low_sin, high_sin,
    )
    down, up, out, qkv, y, g, s1, b1, s2, b2, b_out, b_up, b_down, b_qkv = widened(grads, small, y, g)
    rows = (1, 2, 1, SEQ, WIDTH)
    return (y.reshape(rows), g.reshape(rows), s1, b1, s2, b2, qkv.transpose(1, 0, 2)[None], b_qkv.transpose(1, 0, 2),
            out[None], b_out, up[None], b_up, down[None], b_down)


def solution(mesh):
    return jax.shard_map(
        shards,
        mesh=mesh,
        in_specs=(
            P(None, "dp", None, None),
            P(None, "dp", None, None),
            P(),
            P("section", None),
            P("section", None),
            P("section", None),
            P("section", None),
            P("section", None, None, "tensor"),
            P("section", None, "tensor"),
            P("section", "tensor", None),
            P("section", None),
            P("section", None, "tensor"),
            P("section", "tensor"),
            P("section", "tensor", None),
            P("section", None),
        ),
        out_specs=(
            P("section", None, "dp", None, None),
            P("section", None, "dp", None, None),
            P("section", None),
            P("section", None),
            P("section", None),
            P("section", None),
            P("section", None, None, "tensor"),
            P("section", None, "tensor"),
            P("section", "tensor", None),
            P("section", None),
            P("section", None, "tensor"),
            P("section", "tensor"),
            P("section", "tensor", None),
            P("section", None),
        ),
        check_vma=False,
    )
```

```python
import jax
import jax.numpy as jnp
import numpy as np
from jax import lax
from jax.experimental import pallas as pl
from jax.experimental.pallas import tpu as pltpu
from jax.sharding import PartitionSpec as P

MESH = pl.DeviceIdType.MESH
VMEM_LIMIT = 50 * 2**20

SLABS = 6
SLAB_ROWS = 2048
HALF = 1024
STREAM = 512
COLS = 512
CHUNK = (128, 32)
RX_ONE = (0, 768)
RX_TWO = (256, 832)
RX_ROWS = 960
SMALL = 32


def mod4(value):
    return lax.rem(value + 4, 4)


class Place:
    def __init__(self):
        self.section = lax.axis_index("section")
        self.tensor = lax.axis_index("tensor")
        dp = lax.axis_index("dp")
        self.core = lax.rem(dp, 2)
        self.x = lax.rem(dp // 2, 4)
        self.z = dp // 8

    def at(self, z, x, core):
        return (self.section, (z * 4 + x) * 2 + core, self.tensor)

    def other_core(self):
        return self.at(self.z, self.x, 1 - self.core)

    def along(self, axis, step):
        if axis == 0:
            return self.at(self.z, mod4(self.x + step), self.core)
        return self.at(mod4(self.z + step), self.x, self.core)

    def position(self, axis):
        return self.x if axis == 0 else self.z


def ds(start, size):
    return pl.ds(pl.multiple_of(start, 16), size)


def take(ref, sem):
    pltpu.make_async_copy(ref, ref, sem).wait()


def put(src, dst, send_sem, recv_sem, device):
    pltpu.make_async_remote_copy(
        src_ref=src, dst_ref=dst, send_sem=send_sem, recv_sem=recv_sem,
        device_id=device, device_id_type=MESH,
    ).start()


def added(*parts):
    if len(parts) == 2:
        return parts[0] + parts[1]
    total = parts[0].astype(jnp.float32)
    for part in parts[1:]:
        total = total + part.astype(jnp.float32)
    return total.astype(jnp.bfloat16)


class Reduce:
    def __init__(self, place, grads, out, arrived, landing, send, recv):
        self.place, self.grads, self.out = place, grads, out
        self.arrived, self.landing, self.send, self.recv = arrived, landing, send, recv

    def base(self, stream):
        return self.place.core * HALF + stream * STREAM

    def layout(self, stream, phase):
        axis = (stream + phase) % 2
        p = self.place.position(axis)
        start = self.base(stream)
        if phase == 1:
            start = start + self.place.position(stream) * CHUNK[0]
        return axis, p, start, CHUNK[phase]

    def first_sends(self, s, phase, sem):
        h = CHUNK[phase] // 2
        for stream in range(2):
            axis, p, start, size = self.layout(stream, phase)
            far = start + mod4(p + 2) * size
            for side, step in ((0, 1), (1, -1)):
                put(self.grads.at[s, ds(far + side * h, h)],
                    self.landing.at[s, pl.ds(RX_ONE[phase] + (stream * 2 + side) * h, h)],
                    self.send.at[s, 0], self.recv.at[s, sem], self.place.along(axis, step))

    def second_sends(self, s, phase, sem):
        h = CHUNK[phase] // 2
        take(self.landing.at[s, pl.ds(0, 4 * h)], self.recv.at[s, sem - 1])
        for stream in range(2):
            axis, p, start, size = self.layout(stream, phase)
            for side, step in ((0, 1), (1, -1)):
                near = start + mod4(p + step) * size
                rows = ds(near + side * h, h)
                came = pl.ds(RX_ONE[phase] + (stream * 2 + side) * h, h)
                self.grads[s, rows] = added(self.grads[s, rows], self.landing[s, came])
                put(self.grads.at[s, ds(near, size)],
                    self.landing.at[s, pl.ds(RX_TWO[phase] + (stream * 2 + side) * size, size)],
                    self.send.at[s, 0], self.recv.at[s, sem], self.place.along(axis, step))

    def finish(self, s, phase, sem, target):
        size = CHUNK[phase]
        take(self.landing.at[s, pl.ds(0, 4 * size)], self.recv.at[s, sem])
        for stream in range(2):
            axis, p, start, size = self.layout(stream, phase)
            rows = ds(start + p * size, size)
            left = pl.ds(RX_TWO[phase] + stream * 2 * size, size)
            right = pl.ds(RX_TWO[phase] + (stream * 2 + 1) * size, size)
            target[s, rows] = added(self.grads[s, rows], self.landing[s, left], self.landing[s, right])

    def spread(self, s, phase, sem):
        for stream in range(2):
            axis, p, start, size = self.layout(stream, phase)
            rows = ds(start + p * size, size)
            for step in (1, -1):
                put(self.out.at[s, rows], self.out.at[s, rows], self.send.at[s, 1],
                    self.recv.at[s, sem], self.place.along(axis, step))

    def forward(self, s, phase, sem):
        size = CHUNK[phase]
        take(self.out.at[s, pl.ds(0, 4 * size)], self.recv.at[s, sem - 1])
        for stream in range(2):
            axis, p, start, size = self.layout(stream, phase)
            for side, step in ((0, 1), (1, -1)):
                rows = ds(start + mod4(p - step) * size + side * (size // 2), size // 2)
                put(self.out.at[s, rows], self.out.at[s, rows], self.send.at[s, 1],
                    self.recv.at[s, sem], self.place.along(axis, step))

    def to_core(self, s, offsets):
        for stream in range(2):
            axis, p, start, size = self.layout(stream, 0)
            for offset in offsets:
                rows = ds(start + mod4(p + offset) * size, size)
                put(self.out.at[s, rows], self.out.at[s, rows], self.send.at[s, 1],
                    self.recv.at[s, 9], self.place.other_core())

    def step(self, s, k):
        core = self.place.core
        if k == 0:
            put(self.grads.at[s, ds((1 - core) * HALF, HALF)], self.arrived.at[s],
                self.send.at[s, 0], self.recv.at[s, 0], self.place.other_core())
        elif k == 1:
            take(self.arrived.at[s], self.recv.at[s, 0])

            def block(i, _):
                here = ds(core * HALF + i * 128, 128)
                self.grads[s, here] = added(self.grads[s, here], self.arrived[s, ds(i * 128, 128)])
                return 0

            lax.fori_loop(0, HALF // 128, block, 0)
            self.first_sends(s, 0, 1)
        elif k == 2:
            self.second_sends(s, 0, 2)
        elif k == 3:
            self.finish(s, 0, 2, self.grads)
            self.first_sends(s, 1, 3)
        elif k == 4:
            self.second_sends(s, 1, 4)
        elif k == 5:
            self.finish(s, 1, 4, self.out)
            self.spread(s, 1, 5)
        elif k == 6:
            self.forward(s, 1, 6)
        elif k == 7:
            take(self.out.at[s, pl.ds(0, 64)], self.recv.at[s, 6])
            self.spread(s, 0, 7)
            self.to_core(s, (0,))
        elif k == 8:
            self.forward(s, 0, 8)
            self.to_core(s, (1, -1))
        elif k == 9:
            take(self.out.at[s, pl.ds(0, 256)], self.recv.at[s, 8])
            self.to_core(s, (2,))
        elif k == 10:
            take(self.out.at[s, pl.ds(0, 1024)], self.recv.at[s, 9])

    def drain(self, s):
        take(self.grads.at[s, pl.ds(0, 1984)], self.send.at[s, 0])
        take(self.grads.at[s, pl.ds(0, 1984)], self.send.at[s, 1])


class SmallReduce:
    def __init__(self, place, mine, out, landing, pair, send, recv):
        self.place, self.mine, self.out, self.landing, self.pair = place, mine, out, landing, pair
        self.send, self.recv = send, recv

    def exchange(self, axis):
        p = self.place.position(axis)
        for step in (1, 2, 3):
            put(self.landing.at[axis, p], self.landing.at[axis, p], self.send, self.recv.at[1 + axis],
                self.place.along(axis, step))

    def collected(self, axis):
        take(self.landing.at[axis, pl.ds(0, 3)], self.recv.at[1 + axis])
        return added(*[self.landing[axis, j] for j in range(4)])

    def step(self, k):
        half = SMALL // 2
        rows = ds(self.place.core * half, half)
        if k == 0:
            put(self.mine, self.pair, self.send, self.recv.at[0], self.place.other_core())
        elif k == 1:
            take(self.pair, self.recv.at[0])
            self.landing[0, self.place.x] = added(self.mine[rows], self.pair[rows])
            self.exchange(0)
        elif k == 2:
            self.landing[1, self.place.z] = self.collected(0)
            self.exchange(1)
        elif k == 3:
            self.out[rows] = self.collected(1)
            put(self.out.at[rows], self.out.at[rows], self.send, self.recv.at[3], self.place.other_core())
        elif k == 4:
            take(self.out.at[pl.ds(0, half)], self.recv.at[3])

    def drain(self):
        half = SMALL // 2
        take(self.landing.at[0, pl.ds(0, 3)], self.send)
        take(self.landing.at[0, pl.ds(0, 3)], self.send)
        take(self.mine, self.send)
        take(self.out.at[pl.ds(0, half)], self.send)


def greet(devices):
    for device in devices:
        pl.semaphore_signal(pltpu.get_barrier_semaphore(), inc=1, device_id=device, device_id_type=MESH)


def met(count):
    pl.semaphore_wait(pltpu.get_barrier_semaphore(), count)


def plane_partners(place):
    return [place.other_core()] + [place.along(axis, step) for axis in (0, 1) for step in (1, 2, 3)]


PLAN = (
    "down00", (0, 0), "down01", "down10", (1, 0), "down11", (0, 1), "back",
    (1, 1), "up0", (2, 0), (0, 2), "up1", (3, 0), (2, 1), "attend00",
    (1, 2), "attend01", (3, 1), "inputs00", "inputs01", (0, 3), "attend10", "attend11",
    (1, 3), "inputs10", (2, 2), "inputs11", (3, 2), (0, 4), (1, 4), "last0",
    (4, 0), "last1", (5, 0), (2, 3), (4, 1), (3, 3), "sums", (5, 1),
    (0, 5), (1, 5), (2, 4), (4, 2), (3, 4), "norms", "small0", (5, 2),
    (0, 6), (1, 6), (2, 5), (4, 3), (3, 5), "finish0", (5, 3), (0, 7),
    "small1", "finish1", (1, 7), "copies", (2, 6), (4, 4), (3, 6), (5, 4),
    (0, 8), "small2", (1, 8), (2, 7), (4, 5), (3, 7), (5, 5), (0, 9),
    (1, 9), (2, 8), "small3", (4, 6), (3, 8), (5, 6), (2, 9), (4, 7),
    (3, 9), (5, 7), (4, 8), "small4", (5, 8), (4, 9), (5, 9),
)

SEQ = 256
TOKENS = 2 * SEQ
OWN = SEQ // 2
PARTS = 8
PART = OWN // PARTS
WIDTH = 1024
HEAD = 64
ROT = 16
EPSILON = 1e-05
BF16 = jnp.bfloat16
F32 = jnp.float32


def nn(a, b):
    return lax.dot_general(a, b, (((1,), (0,)), ((), ())), preferred_element_type=F32)


def nt(a, b):
    return lax.dot_general(a, b, (((1,), (1,)), ((), ())), preferred_element_type=F32)


def tn(a, b):
    return lax.dot_general(a, b, (((0,), (0,)), ((), ())), preferred_element_type=F32)


def wide(ref):
    return ref[...].astype(F32)


def block(index, size):
    return pl.ds(pl.multiple_of(index * size, size), size)


def one_head(pair, h):
    lane = lax.broadcasted_iota(jnp.int32, pair.shape, 1)
    return jnp.where((lane < HEAD) if h == 0 else (lane >= HEAD), pair, jnp.zeros_like(pair))


def rotary_tables():
    frequency = (1.0 / 10000.0 ** (np.arange(ROT // 2) * 2.0 / ROT)).astype(np.float32)
    angles = np.arange(SEQ, dtype=np.float32)[:, None] * frequency[None, :]
    cos, sin = np.cos(angles), np.sin(angles)
    cos_table = np.ones((SEQ, 128), np.float32)
    low_sin, high_sin = np.zeros((SEQ, 128), np.float32), np.zeros((SEQ, 128), np.float32)
    for head in range(128 // HEAD):
        first, second = head * HEAD, head * HEAD + ROT // 2
        cos_table[:, first:second] = cos
        cos_table[:, second:second + ROT // 2] = cos
        low_sin[:, first:second] = sin
        high_sin[:, second:second + ROT // 2] = sin
    return cos_table, low_sin, high_sin


def rotated(u, tables, sign):
    cos, low_sin, high_sin = tables
    ahead = pltpu.roll(u, 128 - ROT // 2, 1)
    behind = pltpu.roll(u, ROT // 2, 1)
    return u * cos + (behind * high_sin - ahead * low_sin) * sign


class Layer:
    def __init__(self, refs):
        self.__dict__.update(refs)

    def up_block(self, n, rows):
        return self.out.at[4 + n // 2, pl.ds((n % 2) * WIDTH + rows[0], rows[1])]

    def slope_block(self, m, n):
        return self.grads.at[4, ds(n * COLS + m * SEQ, SEQ)]

    def norm(self, m):
        rows = block(m, SEQ)
        x = wide(self.x.at[rows])
        mean = jnp.mean(x, axis=1, keepdims=True)
        centered = x - mean
        rstd = lax.rsqrt(jnp.mean(centered * centered, axis=1, keepdims=True) + EPSILON)
        normed = centered * rstd
        self.mean[rows] = mean
        self.rstd[rows] = rstd
        self.first_in[rows] = (normed * wide(self.ln1_scale) + wide(self.ln1_bias)).astype(BF16)
        self.second_in[rows] = (normed * wide(self.ln2_scale) + wide(self.ln2_bias)).astype(BF16)

    def project(self, m):
        rows = block(m, SEQ)
        tables = (self.cos[...], self.low_sin[...], self.high_sin[...])
        bias = wide(self.qkv_bias)
        for t in range(3):
            part = nn(self.first_in[rows], self.qkv_w[t]) + bias[t:t + 1]
            for lane in range(0, COLS, 128):
                piece = part[:, lane:lane + 128]
                if t < 2:
                    piece = rotated(piece, tables, 1.0)
                if t == 0:
                    piece = piece * HEAD ** -0.5
                self.qkv[t, rows, pl.ds(lane, 128)] = piece.astype(BF16)

    def attend(self, m):
        rows = block(m, SEQ)
        causal = (lax.broadcasted_iota(jnp.int32, (SEQ, SEQ), 0)
                  >= lax.broadcasted_iota(jnp.int32, (SEQ, SEQ), 1))
        for hp in range(4):
            lanes = pl.ds(hp * 128, 128)
            q, k, v = (self.qkv[t, rows, lanes] for t in range(3))
            context = None
            for h in range(2):
                scores = jnp.where(causal, nt(one_head(q, h), k), -1e30)
                exp = jnp.exp(scores - jnp.max(scores, axis=1, keepdims=True))
                probs = (exp * (1.0 / jnp.sum(exp, axis=1, keepdims=True))).astype(BF16)
                self.probs[m, hp * 2 + h] = probs
                part = nn(probs, one_head(v, h))
                context = part if context is None else context + part
            self.context[rows, lanes] = context.astype(BF16)

    def up(self, m):
        rows = block(m, SEQ)
        bias = wide(self.up_bias)
        for n in range(4):
            hidden = nn(self.second_in[rows], self.up_block(n, (0, WIDTH))[...])
            hidden = hidden + bias[:, n * COLS:(n + 1) * COLS]
            cdf = 0.5 * (1.0 + lax.erf(hidden * 0.7071067811865476))
            density = jnp.exp(-0.5 * hidden * hidden) * 0.3989422804014327
            lanes = pl.ds(n * COLS, COLS)
            self.activated[rows, lanes] = (hidden * cdf).astype(BF16)
            self.slope_block(m, n)[...] = (cdf + hidden * density).astype(BF16)

    def branches(self, m, start=0, count=SEQ):
        rows, here = ds(m * SEQ + start, count), ds(start, count)
        for j in range(2):
            lanes = pl.ds(j * COLS, COLS)
            total = nn(self.context[rows], self.out_w[:, lanes])
            total = total + nn(self.activated[rows], self.out[2 + j])
            self.partial[m, here, lanes] = total.astype(BF16)

    def back_branches(self, m):
        rows = block(m, SEQ)
        upstream = self.upstream[rows]
        self.d_context[rows] = nt(upstream, self.out_w[...]).astype(BF16)
        for n in range(4):
            down = pl.ds(n * COLS, COLS)
            part = nt(upstream[:, :COLS], self.out[2, down]) + nt(upstream[:, COLS:], self.out[3, down])
            self.d_hidden[rows, down] = part.astype(BF16)

    def back_gelu(self, m):
        rows = block(m, SEQ)
        for n in range(4):
            lanes = pl.ds(n * COLS, COLS)
            self.d_hidden[rows, lanes] = (
                wide(self.d_hidden.at[rows, lanes]) * wide(self.slope_block(m, n))
            ).astype(BF16)

    def back_attend(self, m, pairs=range(4)):
        rows = block(m, SEQ)
        tables = (self.cos[...], self.low_sin[...], self.high_sin[...])
        for hp in pairs:
            lanes = pl.ds(hp * 128, 128)
            q, k, v = (self.qkv[t, rows, lanes] for t in range(3))
            d_context = self.d_context[rows, lanes]
            probs = [self.probs[m, hp * 2 + h] for h in range(2)]
            d_mine = [one_head(d_context, h) for h in range(2)]
            d_scores = []
            for h in range(2):
                wide_probs = probs[h].astype(F32)
                weighted = nt(d_mine[h], v) * wide_probs
                inner = jnp.sum(weighted, axis=1, keepdims=True)
                d_scores.append((weighted - wide_probs * inner).astype(BF16))
            both = [jnp.concatenate([one_head(u, 0), one_head(u, 1)], axis=0) for u in (q, k)]
            d_query = nn(jnp.concatenate(d_scores, axis=1), both[1])
            d_key = tn(jnp.concatenate(d_scores, axis=0), both[0])
            d_value = tn(jnp.concatenate(probs, axis=0), jnp.concatenate(d_mine, axis=0))
            d_query = rotated(d_query * HEAD ** -0.5, tables, -1.0)
            d_key = rotated(d_key, tables, -1.0)
            for t, part in enumerate((d_query, d_key, d_value)):
                self.d_projected[t, rows, lanes] = part.astype(BF16)

    def back_inputs(self, m, halves=range(2), start=0, count=SEQ):
        rows, here = ds(m * SEQ + start, count), ds(start, count)
        mean, rstd = self.mean[rows], self.rstd[rows]
        for j in halves:
            lanes = pl.ds(j * COLS, COLS)
            d_second = None
            for n in range(4):
                part = nt(self.d_hidden[rows, pl.ds(n * COLS, COLS)], self.up_block(n, (j * COLS, COLS))[...])
                d_second = part if d_second is None else d_second + part
            d_first = None
            for t in range(3):
                part = nt(self.d_projected[t, rows], self.qkv_w[t, lanes])
                d_first = part if d_first is None else d_first + part
            normed = (wide(self.x.at[rows, lanes]) - mean) * rstd
            sums = (d_first * normed, d_first, d_second * normed, d_second)
            for i, value in enumerate(sums):
                row = pl.ds(2 * i + j, 1)
                self.vectors[row] = self.vectors[row] + jnp.sum(value, axis=0, keepdims=True)
            d_normed = d_first * wide(self.ln1_scale.at[:, lanes]) + d_second * wide(self.ln2_scale.at[:, lanes])
            self.partial[m, here, lanes] = d_normed.astype(BF16)

    def weight_sum(self, name):
        def product(left, columns, targets):
            turned = left[:, columns].T
            for right, b in targets:
                self.grads[b // 4, pl.ds((b % 4) * COLS, COLS)] = nn(turned, right).astype(BF16)

        upstream = [self.upstream[:, pl.ds(c * COLS, COLS)] for c in range(2)]
        if name.startswith("down"):
            slab, half = int(name[-2]), self.core if int(name[-1]) else 1 - self.core
            turned = self.activated[:, ds((2 * slab + half) * COLS, COLS)].T
            for c in range(2):
                self.grads[slab, ds((2 * half + c) * COLS, COLS)] = nn(turned, upstream[c]).astype(BF16)
        elif name in ("up0", "up1"):
            r = int(name == "up1")
            d_hidden = [self.d_hidden[:, pl.ds(n * COLS, COLS)] for n in range(4)]
            product(self.second_in, pl.ds(r * COLS, COLS), [(d_hidden[n], 8 + 4 * r + n) for n in range(4)])
        else:
            r = int(name == "last1")
            if r == 0:
                product(self.context, pl.ds(0, COLS), [(upstream[c], 16 + c) for c in range(2)])
            d_projected = [self.d_projected[t] for t in range(3)]
            product(self.first_in, pl.ds(r * COLS, COLS), [(d_projected[t], 18 + 3 * r + t) for t in range(3)])

    def bias_sums(self):
        for t in range(3):
            self.vectors[pl.ds(8 + t, 1)] = jnp.sum(wide(self.d_projected.at[t]), axis=0, keepdims=True)
        for j in range(2):
            lanes = pl.ds(j * COLS, COLS)
            self.vectors[pl.ds(11 + j, 1)] = jnp.sum(wide(self.upstream.at[:, lanes]), axis=0, keepdims=True)
        for n in range(4):
            lanes = pl.ds(n * COLS, COLS)
            self.vectors[pl.ds(13 + n, 1)] = jnp.sum(wide(self.d_hidden.at[:, lanes]), axis=0, keepdims=True)


INPUTS = ("x_in", "cot_in", "order", "ln1_scale", "ln1_bias", "ln2_scale", "ln2_bias", "qkv_in", "qkv_bias",
          "out_in", "out_bias", "up_in", "up_bias", "down_in", "down_bias", "cos", "low_sin", "high_sin")
IN_HBM = ("x_in", "cot_in", "qkv_in", "out_in", "up_in", "down_in")
OUTPUTS = ("y_out", "g_out", "out", "small_out")
DMA = pltpu.SemaphoreType.DMA
SCRATCH = dict(
    grads=pltpu.VMEM((SLABS, SLAB_ROWS, COLS), BF16),
    arrived=pltpu.VMEM((SLABS, HALF, COLS), BF16),
    landing=pltpu.VMEM((SLABS, RX_ROWS, COLS), BF16),
    x=pltpu.VMEM((TOKENS, WIDTH), BF16),
    upstream=pltpu.VMEM((TOKENS, WIDTH), BF16),
    first_in=pltpu.VMEM((TOKENS, WIDTH), BF16),
    second_in=pltpu.VMEM((TOKENS, WIDTH), BF16),
    qkv=pltpu.VMEM((3, TOKENS, COLS), BF16),
    d_projected=pltpu.VMEM((3, TOKENS, COLS), BF16),
    context=pltpu.VMEM((TOKENS, COLS), BF16),
    d_context=pltpu.VMEM((TOKENS, COLS), BF16),
    probs=pltpu.VMEM((2, 8, SEQ, SEQ), BF16),
    activated=pltpu.VMEM((TOKENS, 4 * COLS), BF16),
    d_hidden=pltpu.VMEM((TOKENS, 4 * COLS), BF16),
    partial=pltpu.VMEM((2, SEQ, WIDTH), BF16),
    came=pltpu.VMEM((2, 2, OWN, WIDTH), BF16),
    mine=pltpu.VMEM((2, 2, OWN, WIDTH), BF16),
    mean=pltpu.VMEM((TOKENS, 1), F32),
    rstd=pltpu.VMEM((TOKENS, 1), F32),
    vectors=pltpu.VMEM((SMALL, COLS), F32),
    qkv_w=pltpu.VMEM((3, WIDTH, COLS), BF16),
    out_w=pltpu.VMEM((COLS, WIDTH), BF16),
    small_mine=pltpu.VMEM((SMALL, COLS), BF16),
    small_landing=pltpu.VMEM((2, 4, SMALL // 2, COLS), BF16),
    small_pair=pltpu.VMEM((SMALL, COLS), BF16),
    norms=pltpu.VMEM((2, 16, COLS), BF16),
    send=DMA((SLABS, 2)),
    recv=DMA((SLABS, 10)),
    small_send=DMA,
    small_recv=DMA((4,)),
    load=DMA((5,)),
    pair_send=DMA((2, 2)),
    pair_recv=DMA((2, 2, PARTS)),
    next_send=DMA((2,)),
    next_recv=DMA((2, PARTS)),
    far_send=DMA((2,)),
    far_recv=DMA((2,)),
    copy_send=DMA((2, 2)),
    copy_recv=DMA((2, 2)),
    copy_own=DMA((2, 2)),
    norms_sem=DMA((2,)),
)


class Refs:
    def __init__(self, pairs):
        self.__dict__.update(pairs)


def layer_kernel(*refs):
    names = INPUTS + OUTPUTS + tuple(SCRATCH)
    r = Refs(zip(names, refs))
    layer, place = Layer(vars(r)), Place()
    layer.core = place.core
    section, tensor = place.section, place.tensor
    first, last = section == 0, section == 1
    dp = lax.axis_index("dp")
    partner = (section, dp, 1 - tensor)
    near = (1 - section, dp, 1 - tensor)
    others = plane_partners(place) + [partner, near]
    load = r.load
    out, x, upstream = r.out, r.x, r.upstream

    greet(others)

    def fetch(src, dst, sem):
        pltpu.make_async_copy(src, dst, load.at[sem]).start()

    def fetch_out():
        fetch(r.out_in, r.out_w, 3)
        for c in range(2):
            fetch(r.down_in.at[:, pl.ds(c * COLS, COLS)], out.at[2 + c], 4)

    def fetch_up():
        for n in range(4):
            fetch(r.up_in.at[:, pl.ds(n * COLS, COLS)], layer.up_block(n, (0, WIDTH)), 2)

    @pl.when(first)
    def _():
        fetch(r.x_in, x, 0)
        fetch(r.qkv_in, r.qkv_w, 1)
        take(x, load.at[0])
        fetch_up()
        fetch_out()

    @pl.when(last)
    def _():
        fetch(r.cot_in, r.activated.at[:, pl.ds(0, WIDTH)], 0)
        fetch_out()
        fetch(r.qkv_in, r.qkv_w, 1)
        fetch_up()

    @pl.when(last)
    def _():
        given = r.activated
        take(upstream, load.at[0])
        swap = r.order[0] != 0
        one, two = given[pl.ds(0, SEQ), pl.ds(0, WIDTH)], given[pl.ds(SEQ, SEQ), pl.ds(0, WIDTH)]
        upstream[pl.ds(0, SEQ)] = jnp.where(swap, two, one)
        upstream[pl.ds(SEQ, SEQ)] = jnp.where(swap, one, two)
        take(r.out_w, load.at[3])
        take(out.at[pl.ds(2, 2)], load.at[4])

        def each(m, _):
            layer.back_branches(m)
            return 0

        lax.fori_loop(0, 2, each, 0)
        met(len(others))

    r.vectors[...] = jnp.zeros((SMALL, COLS), F32)

    own_half, other_half = tensor * OWN, (1 - tensor) * OWN

    def part_of(start, c):
        return ds(start + c * PART, PART)

    def exchange(m, kind):
        for c in range(PARTS):
            put(r.partial.at[m, part_of((1 - tensor) * OWN, c)], r.came.at[kind, m, part_of(0, c)],
                r.pair_send.at[kind, m], r.pair_recv.at[kind, m, c], partner)

    def finish_part(m, kind, c):
        rows = part_of(m * SEQ + tensor * OWN, c)
        here = part_of(0, c)
        came = r.came.at[kind, m, here]
        take(came, r.pair_recv.at[kind, m, c])
        total = wide(r.partial.at[m, part_of(tensor * OWN, c)]) + wide(came)
        if kind == 0:
            result = wide(x.at[rows]) + total + (wide(r.out_bias) + wide(r.down_bias))
        else:
            rstd = r.rstd[rows]
            normed = (wide(x.at[rows]) - r.mean[rows]) * rstd
            centered = (total - jnp.mean(total, axis=1, keepdims=True)
                        - normed * jnp.mean(total * normed, axis=1, keepdims=True))
            result = wide(upstream.at[rows]) + rstd * centered
        mine = r.mine.at[kind, m, here]
        mine[...] = result.astype(BF16)
        target = upstream if kind else x

        @pl.when(last if kind else first)
        def _():
            put(mine, target.at[rows], r.next_send.at[m], r.next_recv.at[m, c], near)

    def finish_parts(m, kind, parts):
        for c in parts:
            finish_part(m, kind, c)
        if PARTS - 1 in parts:
            take(r.came.at[kind, m], r.pair_send.at[kind, m])

    def finish(m):
        for kind, chosen in ((0, last), (1, first)):
            @pl.when(chosen)
            def _(kind=kind):
                finish_parts(m, kind, range(PARTS))

    def pass_on(m, target, parts):
        for c in parts:
            rows = target.at[part_of(m * SEQ + (1 - tensor) * OWN, c)]
            take(rows, r.next_recv.at[m, c])
            put(rows, rows, r.far_send.at[m], r.far_recv.at[m], partner)

    def arrived(m, target):
        take(target.at[pl.ds(0, OWN)], r.far_recv.at[m])

    def arrive(m, target):
        pass_on(m, target, range(PARTS))
        arrived(m, target)

    def tick(i, _):
        m = i

        def when(condition, action, *args):
            if isinstance(args[-1], range) and not args[-1]:
                return

            @pl.when(condition)
            def _():
                action(*args)

        def meanwhile(first_parts, next_parts, last_parts):
            when(jnp.logical_and(first, i == 1), finish_parts, 0, 0, first_parts)
            when(jnp.logical_and(last, i == 0), pass_on, 1, x, next_parts)
            when(jnp.logical_and(last, i == 1), finish_parts, 0, 1, last_parts)

        none = range(0)
        when(jnp.logical_and(last, i == 0), arrive, 0, x)
        when(jnp.logical_and(last, i == 1), arrived, 1, x)
        layer.norm(m)
        when(i == 0, take, r.qkv_w, load.at[1])
        layer.project(m)
        meanwhile(none, range(0, 2), none)
        layer.attend(m)
        meanwhile(range(0, 1), range(2, 5), range(0, 1))
        when(i == 0, take, out.at[pl.ds(4, 2)], load.at[2])
        layer.up(m)
        meanwhile(range(1, 4), range(5, PARTS), range(1, 4))

        @pl.when(jnp.logical_and(first, i == 0))
        def _():
            take(r.out_w, load.at[3])
            take(out.at[pl.ds(2, 2)], load.at[4])
            met(len(others))

        @pl.when(first)
        def _():
            layer.branches(m, other_half, OWN)
            meanwhile(range(4, PARTS), none, none)
            exchange(m, 0)
            layer.branches(m, own_half, OWN)

        @pl.when(last)
        def _():
            layer.back_gelu(m)
            layer.back_attend(m)
            meanwhile(none, none, range(4, PARTS))
            layer.back_inputs(m)
            exchange(m, 1)

        return 0

    lax.fori_loop(0, 2, tick, 0)

    @pl.when(first)
    def _():
        finish_parts(1, 0, range(PARTS))
        arrive(0, upstream)
        layer.back_branches(0)
        layer.back_gelu(0)
        pass_on(1, upstream, range(PARTS))
        arrived(1, upstream)

    @pl.when(last)
    def _():
        finish_parts(1, 1, range(PARTS))

        def each(m, _):
            layer.branches(m)
            exchange(m, 0)
            return 0

        lax.fori_loop(0, 2, each, 0)

    grads = r.grads
    reduce = Reduce(place, grads, out, r.arrived, r.landing, r.send, r.recv)
    small = SmallReduce(place, r.small_mine, r.small_out, r.small_landing, r.small_pair,
                        r.small_send, r.small_recv)
    vectors, norms = r.vectors, r.norms

    def back(name):
        @pl.when(first)
        def _():
            if name == "back":
                layer.back_branches(1)
                layer.back_gelu(1)
                return
            m, half = int(name[-2]), int(name[-1])
            if name.startswith("attend"):
                layer.back_attend(m, range(2 * half, 2 * half + 2))
            else:
                layer.back_inputs(m, range(half, half + 1))
                if half:
                    exchange(m, 1)

    def sums():
        layer.bias_sums()
        norms[0] = vectors[pl.ds(0, 16)].astype(BF16)
        put(norms.at[0], norms.at[1], r.norms_sem.at[0], r.norms_sem.at[1], partner)
        r.small_mine[...] = vectors[...].astype(BF16)

    def norm_sums():
        take(norms.at[1], r.norms_sem.at[1])
        both = wide(norms.at[0]) + wide(norms.at[1])
        ln_row = lax.broadcasted_iota(jnp.int32, (16, COLS), 0) < 8
        r.small_mine[pl.ds(0, 16)] = jnp.where(ln_row, both, vectors[pl.ds(0, 16)]).astype(BF16)

    def copies():
        for m in range(2):
            for kind, final in ((0, r.y_out), (1, r.g_out)):
                rows = final.at[ds(m * SEQ + tensor * OWN, OWN)]
                mine = r.mine.at[kind, m]
                put(mine, rows, r.copy_send.at[kind, m], r.copy_recv.at[kind, m], partner)
                pltpu.make_async_copy(mine, rows, r.copy_own.at[kind, m]).start()

    for item in PLAN:
        if not isinstance(item, str):
            reduce.step(*item)
        elif item[:4] in ("back", "atte", "inpu"):
            back(item)
        elif item.startswith("finish"):
            finish(int(item[-1]))
        elif item.startswith("small"):
            small.step(int(item[-1]))
        elif item == "sums":
            sums()
        elif item == "norms":
            norm_sums()
        elif item == "copies":
            copies()
        else:
            layer.weight_sum(item)
    for s in range(SLABS):
        reduce.step(s, 10)
    for s in range(SLABS):
        reduce.drain(s)
    small.drain()
    take(norms.at[0], r.norms_sem.at[0])
    for m in range(2):
        for kind in range(2):
            take(r.mine.at[kind, m], r.copy_send.at[kind, m])
            take(r.mine.at[kind, m], r.copy_recv.at[kind, m])
            take(r.mine.at[kind, m], r.copy_own.at[kind, m])
        take(x.at[pl.ds(0, OWN)], r.next_send.at[m])
        take(x.at[pl.ds(0, OWN)], r.far_send.at[m])


def layer_call(*args):
    hbm, vmem = pl.BlockSpec(memory_space=pl.ANY), pl.BlockSpec(memory_space=pltpu.VMEM)
    smem = pl.BlockSpec(memory_space=pltpu.SMEM)
    rows = jax.ShapeDtypeStruct((TOKENS, WIDTH), BF16)
    return pl.pallas_call(
        layer_kernel,
        out_shape=(rows, rows, pltpu.VMEM((SLABS, SLAB_ROWS, COLS), BF16), pltpu.VMEM((SMALL, COLS), BF16)),
        in_specs=[hbm if name in IN_HBM else smem if name == "order" else vmem for name in INPUTS],
        out_specs=(hbm, hbm, vmem, vmem),
        scratch_shapes=list(SCRATCH.values()),
        compiler_params=pltpu.CompilerParams(
            collective_id=0, has_side_effects=True, vmem_limit_bytes=VMEM_LIMIT
        ),
    )(*args)


VECTORS = ((0, 2), (2, 2), (4, 2), (6, 2), (11, 2), (13, 4), (11, 2))


def widen_kernel(given, small, y_in, g_in, down, up, out, qkv, y_out, g_out, *rest):
    targets, (staged, held, rows, sems, copy_sems, row_sems) = rest[:8], rest[8:]
    passing = [(pltpu.make_async_copy(src, held.at[i], copy_sems.at[0, i]),
                pltpu.make_async_copy(held.at[i], dst, copy_sems.at[1, i]))
               for i, (src, dst) in enumerate(((y_in, y_out), (g_in, g_out)))]
    for come, _ in passing:
        come.start()
    values = small[...].astype(F32)
    moves = []
    for v, (row, count) in enumerate(VECTORS):
        for i in range(count):
            rows[v, :, pl.ds(i * COLS, COLS)] = values[row + i:row + i + 1]
        moves.append(pltpu.make_async_copy(rows.at[v, :, pl.ds(0, count * COLS)], targets[v], row_sems.at[v]))
    for t in range(3):
        moves.append(pltpu.make_async_copy(rows.at[7, :, pl.ds(t * COLS, COLS)], targets[7].at[t], row_sems.at[7 + t]))
        rows[7, :, pl.ds(t * COLS, COLS)] = values[8 + t:9 + t]
    for move in moves:
        move.start()

    def target(b):
        if b < 8:
            return down.at[pl.ds((b // 2) * COLS, COLS), pl.ds((b % 2) * COLS, COLS)]
        if b < 16:
            return up.at[pl.ds((b // 4 - 2) * COLS, COLS), pl.ds((b % 4) * COLS, COLS)]
        if b < 18:
            return out.at[:, pl.ds((b - 16) * COLS, COLS)]
        return qkv.at[(b - 18) % 3, pl.ds((b - 18) // 3 * COLS, COLS)]

    count, depth = SLABS * 4, 4
    copies = []
    for b in range(count):
        if b >= depth:
            copies[b - depth].wait()
        if b == 2 * depth:
            for come, go in passing:
                come.wait()
                go.start()
        slot = b % depth
        staged[slot] = given[b // 4, pl.ds((b % 4) * COLS, COLS)].astype(F32)
        copies.append(pltpu.make_async_copy(staged.at[slot], target(b), sems.at[slot]))
        copies[b].start()
    for b in range(count - depth, count):
        copies[b].wait()
    for move in moves + [go for _, go in passing]:
        move.wait()


def widened(grads, small, y, g):
    hbm, vmem = pl.BlockSpec(memory_space=pl.ANY), pl.BlockSpec(memory_space=pltpu.VMEM)
    shapes = [((2048, WIDTH), F32), ((WIDTH, 2048), F32), ((COLS, WIDTH), F32), ((3, WIDTH, COLS), F32),
              (y.shape, BF16), (g.shape, BF16)]
    shapes += [((1, rows * COLS), F32) for _, rows in VECTORS] + [((3, 1, COLS), F32)]
    grads, small = (pltpu.with_memory_space_constraint(a, pltpu.VMEM) for a in (grads, small))
    y, g = (pltpu.with_memory_space_constraint(a, pltpu.HBM) for a in (y, g))
    return pl.pallas_call(
        widen_kernel,
        out_shape=tuple(jax.ShapeDtypeStruct(shape, dtype) for shape, dtype in shapes),
        in_specs=[vmem, vmem] + [pl.BlockSpec(memory_space=pltpu.HBM)] * 2,
        out_specs=(hbm,) * 14,
        scratch_shapes=[pltpu.VMEM((4, COLS, COLS), F32), pltpu.VMEM((2, TOKENS, WIDTH), BF16),
                        pltpu.VMEM((8, 1, 4 * COLS), F32), DMA((4,)), DMA((2, 2)), DMA((10,))],
        compiler_params=pltpu.CompilerParams(vmem_limit_bytes=10 * 2**20),
    )(grads, small, y, g)


def shards(layer_input, cotangent, order, ln1_scale, ln1_bias, ln2_scale, ln2_bias, qkv_weight, qkv_bias,
           out_weight, out_bias, up_weight, up_bias, down_weight, down_bias):
    cos, low_sin, high_sin = (jnp.asarray(table) for table in rotary_tables())
    y, g, grads, small = layer_call(
        layer_input.reshape(TOKENS, WIDTH), cotangent.reshape(TOKENS, WIDTH), order,
        ln1_scale, ln1_bias, ln2_scale, ln2_bias,
        qkv_weight[0].transpose(1, 0, 2), qkv_bias[0], out_weight[0], out_bias, up_weight[0], up_bias,
        down_weight[0], down_bias, cos, low_sin, high_sin,
    )
    down, up, out, qkv, y, g, s1, b1, s2, b2, b_out, b_up, b_down, b_qkv = widened(grads, small, y, g)
    rows = (1, 2, 1, SEQ, WIDTH)
    return (y.reshape(rows), g.reshape(rows), s1, b1, s2, b2, qkv.transpose(1, 0, 2)[None], b_qkv.transpose(1, 0, 2),
            out[None], b_out, up[None], b_up, down[None], b_down)


def solution(mesh):
    return jax.shard_map(
        shards,
        mesh=mesh,
        in_specs=(
            P(None, "dp", None, None),
            P(None, "dp", None, None),
            P(),
            P("section", None),
            P("section", None),
            P("section", None),
            P("section", None),
            P("section", None, None, "tensor"),
            P("section", None, "tensor"),
            P("section", "tensor", None),
            P("section", None),
            P("section", None, "tensor"),
            P("section", "tensor"),
            P("section", "tensor", None),
            P("section", None),
        ),
        out_specs=(
            P("section", None, "dp", None, None),
            P("section", None, "dp", None, None),
            P("section", None),
            P("section", None),
            P("section", None),
            P("section", None),
            P("section", None, None, "tensor"),
            P("section", None, "tensor"),
            P("section", "tensor", None),
            P("section", None),
            P("section", None, "tensor"),
            P("section", "tensor"),
            P("section", "tensor", None),
            P("section", None),
        ),
        check_vma=False,
    )
```

```python
import jax
import jax.numpy as jnp
import numpy as np
from jax import lax
from jax.experimental import pallas as pl
from jax.experimental.pallas import tpu as pltpu
from jax.sharding import PartitionSpec as P

MESH = pl.DeviceIdType.MESH
VMEM_LIMIT = 50 * 2**20

SLABS = 6
SLAB_ROWS = 2048
HALF = 1024
STREAM = 512
COLS = 512
CHUNK = (128, 32)
RX_ONE = (0, 768)
RX_TWO = (256, 832)
RX_ROWS = 960
SMALL = 32


def mod4(value):
    return lax.rem(value + 4, 4)


class Place:
    def __init__(self):
        self.section = lax.axis_index("section")
        self.tensor = lax.axis_index("tensor")
        dp = lax.axis_index("dp")
        self.core = lax.rem(dp, 2)
        self.x = lax.rem(dp // 2, 4)
        self.z = dp // 8

    def at(self, z, x, core):
        return (self.section, (z * 4 + x) * 2 + core, self.tensor)

    def other_core(self):
        return self.at(self.z, self.x, 1 - self.core)

    def along(self, axis, step):
        if axis == 0:
            return self.at(self.z, mod4(self.x + step), self.core)
        return self.at(mod4(self.z + step), self.x, self.core)

    def position(self, axis):
        return self.x if axis == 0 else self.z


def ds(start, size):
    return pl.ds(pl.multiple_of(start, 16), size)


def take(ref, sem):
    pltpu.make_async_copy(ref, ref, sem).wait()


def put(src, dst, send_sem, recv_sem, device):
    pltpu.make_async_remote_copy(
        src_ref=src, dst_ref=dst, send_sem=send_sem, recv_sem=recv_sem,
        device_id=device, device_id_type=MESH,
    ).start()


def added(*parts):
    if len(parts) == 2:
        return parts[0] + parts[1]
    total = parts[0].astype(jnp.float32)
    for part in parts[1:]:
        total = total + part.astype(jnp.float32)
    return total.astype(jnp.bfloat16)


class Reduce:
    def __init__(self, place, grads, out, arrived, landing, send, recv):
        self.place, self.grads, self.out = place, grads, out
        self.arrived, self.landing, self.send, self.recv = arrived, landing, send, recv

    def base(self, stream):
        return self.place.core * HALF + stream * STREAM

    def layout(self, stream, phase):
        axis = (stream + phase) % 2
        p = self.place.position(axis)
        start = self.base(stream)
        if phase == 1:
            start = start + self.place.position(stream) * CHUNK[0]
        return axis, p, start, CHUNK[phase]

    def first_sends(self, s, phase, sem):
        h = CHUNK[phase] // 2
        for stream in range(2):
            axis, p, start, size = self.layout(stream, phase)
            far = start + mod4(p + 2) * size
            for side, step in ((0, 1), (1, -1)):
                put(self.grads.at[s, ds(far + side * h, h)],
                    self.landing.at[s, pl.ds(RX_ONE[phase] + (stream * 2 + side) * h, h)],
                    self.send.at[s, 0], self.recv.at[s, sem], self.place.along(axis, step))

    def second_sends(self, s, phase, sem):
        h = CHUNK[phase] // 2
        take(self.landing.at[s, pl.ds(0, 4 * h)], self.recv.at[s, sem - 1])
        for stream in range(2):
            axis, p, start, size = self.layout(stream, phase)
            for side, step in ((0, 1), (1, -1)):
                near = start + mod4(p + step) * size
                rows = ds(near + side * h, h)
                came = pl.ds(RX_ONE[phase] + (stream * 2 + side) * h, h)
                self.grads[s, rows] = added(self.grads[s, rows], self.landing[s, came])
                put(self.grads.at[s, ds(near, size)],
                    self.landing.at[s, pl.ds(RX_TWO[phase] + (stream * 2 + side) * size, size)],
                    self.send.at[s, 0], self.recv.at[s, sem], self.place.along(axis, step))

    def finish(self, s, phase, sem, target):
        size = CHUNK[phase]
        take(self.landing.at[s, pl.ds(0, 4 * size)], self.recv.at[s, sem])
        for stream in range(2):
            axis, p, start, size = self.layout(stream, phase)
            rows = ds(start + p * size, size)
            left = pl.ds(RX_TWO[phase] + stream * 2 * size, size)
            right = pl.ds(RX_TWO[phase] + (stream * 2 + 1) * size, size)
            target[s, rows] = added(self.grads[s, rows], self.landing[s, left], self.landing[s, right])

    def spread(self, s, phase, sem):
        for stream in range(2):
            axis, p, start, size = self.layout(stream, phase)
            rows = ds(start + p * size, size)
            for step in (1, -1):
                put(self.out.at[s, rows], self.out.at[s, rows], self.send.at[s, 1],
                    self.recv.at[s, sem], self.place.along(axis, step))

    def forward(self, s, phase, sem):
        size = CHUNK[phase]
        take(self.out.at[s, pl.ds(0, 4 * size)], self.recv.at[s, sem - 1])
        for stream in range(2):
            axis, p, start, size = self.layout(stream, phase)
            for side, step in ((0, 1), (1, -1)):
                rows = ds(start + mod4(p - step) * size + side * (size // 2), size // 2)
                put(self.out.at[s, rows], self.out.at[s, rows], self.send.at[s, 1],
                    self.recv.at[s, sem], self.place.along(axis, step))

    def to_core(self, s, offsets):
        for stream in range(2):
            axis, p, start, size = self.layout(stream, 0)
            for offset in offsets:
                rows = ds(start + mod4(p + offset) * size, size)
                put(self.out.at[s, rows], self.out.at[s, rows], self.send.at[s, 1],
                    self.recv.at[s, 9], self.place.other_core())

    def step(self, s, k):
        core = self.place.core
        if k == 0:
            put(self.grads.at[s, ds((1 - core) * HALF, HALF)], self.arrived.at[s],
                self.send.at[s, 0], self.recv.at[s, 0], self.place.other_core())
        elif k == 1:
            take(self.arrived.at[s], self.recv.at[s, 0])

            def block(i, _):
                here = ds(core * HALF + i * 128, 128)
                self.grads[s, here] = added(self.grads[s, here], self.arrived[s, ds(i * 128, 128)])
                return 0

            lax.fori_loop(0, HALF // 128, block, 0)
            self.first_sends(s, 0, 1)
        elif k == 2:
            self.second_sends(s, 0, 2)
        elif k == 3:
            self.finish(s, 0, 2, self.grads)
            self.first_sends(s, 1, 3)
        elif k == 4:
            self.second_sends(s, 1, 4)
        elif k == 5:
            self.finish(s, 1, 4, self.out)
            self.spread(s, 1, 5)
        elif k == 6:
            self.forward(s, 1, 6)
        elif k == 7:
            take(self.out.at[s, pl.ds(0, 64)], self.recv.at[s, 6])
            self.spread(s, 0, 7)
            self.to_core(s, (0,))
        elif k == 8:
            self.forward(s, 0, 8)
            self.to_core(s, (1, -1))
        elif k == 9:
            take(self.out.at[s, pl.ds(0, 256)], self.recv.at[s, 8])
            self.to_core(s, (2,))
        elif k == 10:
            take(self.out.at[s, pl.ds(0, 1024)], self.recv.at[s, 9])

    def drain(self, s):
        take(self.grads.at[s, pl.ds(0, 1984)], self.send.at[s, 0])
        take(self.grads.at[s, pl.ds(0, 1984)], self.send.at[s, 1])


class SmallReduce:
    def __init__(self, place, mine, out, landing, pair, send, recv):
        self.place, self.mine, self.out, self.landing, self.pair = place, mine, out, landing, pair
        self.send, self.recv = send, recv

    def exchange(self, axis):
        p = self.place.position(axis)
        for step in (1, 2, 3):
            put(self.landing.at[axis, p], self.landing.at[axis, p], self.send, self.recv.at[1 + axis],
                self.place.along(axis, step))

    def collected(self, axis):
        take(self.landing.at[axis, pl.ds(0, 3)], self.recv.at[1 + axis])
        return added(*[self.landing[axis, j] for j in range(4)])

    def step(self, k):
        half = SMALL // 2
        rows = ds(self.place.core * half, half)
        if k == 0:
            put(self.mine, self.pair, self.send, self.recv.at[0], self.place.other_core())
        elif k == 1:
            take(self.pair, self.recv.at[0])
            self.landing[0, self.place.x] = added(self.mine[rows], self.pair[rows])
            self.exchange(0)
        elif k == 2:
            self.landing[1, self.place.z] = self.collected(0)
            self.exchange(1)
        elif k == 3:
            self.out[rows] = self.collected(1)
            put(self.out.at[rows], self.out.at[rows], self.send, self.recv.at[3], self.place.other_core())
        elif k == 4:
            take(self.out.at[pl.ds(0, half)], self.recv.at[3])

    def drain(self):
        half = SMALL // 2
        take(self.landing.at[0, pl.ds(0, 3)], self.send)
        take(self.landing.at[0, pl.ds(0, 3)], self.send)
        take(self.mine, self.send)
        take(self.out.at[pl.ds(0, half)], self.send)


def greet(devices):
    for device in devices:
        pl.semaphore_signal(pltpu.get_barrier_semaphore(), inc=1, device_id=device, device_id_type=MESH)


def met(count):
    pl.semaphore_wait(pltpu.get_barrier_semaphore(), count)


def plane_partners(place):
    return [place.other_core()] + [place.along(axis, step) for axis in (0, 1) for step in (1, 2, 3)]


PLAN = (
    "down00", (0, 0), "down01", "down10", (1, 0), "down11", (0, 1), "back",
    (1, 1), "up0", (2, 0), (0, 2), "up1", (3, 0), (2, 1), "attend01",
    (1, 2), (3, 1), "inputs00", "inputs01", "attend10", (0, 3), "attend11", "inputs10",
    (1, 3), "inputs11", (2, 2), "last0", (4, 0), (3, 2), (0, 4), (1, 4),
    "last1", (5, 0), (4, 1), (2, 3), (5, 1), "sums", (3, 3), (0, 5),
    (1, 5), (4, 2), (2, 4), (5, 2), "norms", "small0", (3, 4), (0, 6),
    (1, 6), (4, 3), (2, 5), (5, 3), "finish0", (3, 5), (0, 7), "small1",
    "finish1", (1, 7), "copies", (4, 4), (2, 6), (5, 4), (3, 6), (0, 8),
    "small2", (1, 8), (4, 5), (2, 7), (5, 5), (3, 7), (0, 9), (1, 9),
    (4, 6), "small3", (2, 8), (5, 6), (3, 8), (4, 7), (2, 9), (5, 7),
    (3, 9), (4, 8), "small4", (5, 8), (4, 9), (5, 9),
)

SEQ = 256
TOKENS = 2 * SEQ
OWN = SEQ // 2
PARTS = 8
PART = OWN // PARTS
WIDTH = 1024
HEAD = 64
ROT = 16
EPSILON = 1e-05
BF16 = jnp.bfloat16
F32 = jnp.float32


def nn(a, b):
    return lax.dot_general(a, b, (((1,), (0,)), ((), ())), preferred_element_type=F32)


def nt(a, b):
    return lax.dot_general(a, b, (((1,), (1,)), ((), ())), preferred_element_type=F32)


def tn(a, b):
    return lax.dot_general(a, b, (((0,), (0,)), ((), ())), preferred_element_type=F32)


def wide(ref):
    return ref[...].astype(F32)


def block(index, size):
    return pl.ds(pl.multiple_of(index * size, size), size)


def one_head(pair, h):
    lane = lax.broadcasted_iota(jnp.int32, pair.shape, 1)
    return jnp.where((lane < HEAD) if h == 0 else (lane >= HEAD), pair, jnp.zeros_like(pair))


def rotary_tables():
    frequency = (1.0 / 10000.0 ** (np.arange(ROT // 2) * 2.0 / ROT)).astype(np.float32)
    angles = np.arange(SEQ, dtype=np.float32)[:, None] * frequency[None, :]
    cos, sin = np.cos(angles), np.sin(angles)
    cos_table = np.ones((SEQ, 128), np.float32)
    low_sin, high_sin = np.zeros((SEQ, 128), np.float32), np.zeros((SEQ, 128), np.float32)
    for head in range(128 // HEAD):
        first, second = head * HEAD, head * HEAD + ROT // 2
        cos_table[:, first:second] = cos
        cos_table[:, second:second + ROT // 2] = cos
        low_sin[:, first:second] = sin
        high_sin[:, second:second + ROT // 2] = sin
    return cos_table, low_sin, high_sin


def rotated(u, tables, sign):
    cos, low_sin, high_sin = tables
    ahead = pltpu.roll(u, 128 - ROT // 2, 1)
    behind = pltpu.roll(u, ROT // 2, 1)
    return u * cos + (behind * high_sin - ahead * low_sin) * sign


class Layer:
    def __init__(self, refs):
        self.__dict__.update(refs)

    def up_block(self, n, rows):
        return self.out.at[4 + n // 2, pl.ds((n % 2) * WIDTH + rows[0], rows[1])]

    def slope_block(self, m, n):
        return self.grads.at[4, ds(n * COLS + m * SEQ, SEQ)]

    def norm(self, m):
        rows = block(m, SEQ)
        x = wide(self.x.at[rows])
        mean = jnp.mean(x, axis=1, keepdims=True)
        centered = x - mean
        rstd = lax.rsqrt(jnp.mean(centered * centered, axis=1, keepdims=True) + EPSILON)
        normed = centered * rstd
        self.mean[rows] = mean
        self.rstd[rows] = rstd
        self.first_in[rows] = (normed * wide(self.ln1_scale) + wide(self.ln1_bias)).astype(BF16)
        self.second_in[rows] = (normed * wide(self.ln2_scale) + wide(self.ln2_bias)).astype(BF16)

    def project(self, m):
        rows = block(m, SEQ)
        tables = (self.cos[...], self.low_sin[...], self.high_sin[...])
        bias = wide(self.qkv_bias)
        for t in range(3):
            part = nn(self.first_in[rows], self.qkv_w[t]) + bias[t:t + 1]
            for lane in range(0, COLS, 128):
                piece = part[:, lane:lane + 128]
                if t < 2:
                    piece = rotated(piece, tables, 1.0)
                if t == 0:
                    piece = piece * HEAD ** -0.5
                self.qkv[t, rows, pl.ds(lane, 128)] = piece.astype(BF16)

    def attend(self, m):
        rows = block(m, SEQ)
        causal = (lax.broadcasted_iota(jnp.int32, (SEQ, SEQ), 0)
                  >= lax.broadcasted_iota(jnp.int32, (SEQ, SEQ), 1))
        for hp in range(4):
            lanes = pl.ds(hp * 128, 128)
            q, k, v = (self.qkv[t, rows, lanes] for t in range(3))
            context = None
            for h in range(2):
                scores = jnp.where(causal, nt(one_head(q, h), k), -1e30)
                exp = jnp.exp(scores - jnp.max(scores, axis=1, keepdims=True))
                probs = (exp * (1.0 / jnp.sum(exp, axis=1, keepdims=True))).astype(BF16)
                self.probs[m, hp * 2 + h] = probs
                part = nn(probs, one_head(v, h))
                context = part if context is None else context + part
            self.context[rows, lanes] = context.astype(BF16)

    def up(self, m):
        rows = block(m, SEQ)
        bias = wide(self.up_bias)
        for n in range(4):
            hidden = nn(self.second_in[rows], self.up_block(n, (0, WIDTH))[...])
            hidden = hidden + bias[:, n * COLS:(n + 1) * COLS]
            cdf = 0.5 * (1.0 + lax.erf(hidden * 0.7071067811865476))
            density = jnp.exp(-0.5 * hidden * hidden) * 0.3989422804014327
            lanes = pl.ds(n * COLS, COLS)
            self.activated[rows, lanes] = (hidden * cdf).astype(BF16)
            self.slope_block(m, n)[...] = (cdf + hidden * density).astype(BF16)

    def branches(self, m, start=0, count=SEQ):
        rows, here = ds(m * SEQ + start, count), ds(start, count)
        for j in range(2):
            lanes = pl.ds(j * COLS, COLS)
            total = nn(self.context[rows], self.out_w[:, lanes])
            total = total + nn(self.activated[rows], self.out[2 + j])
            self.partial[m, here, lanes] = total.astype(BF16)

    def back_branches(self, m):
        rows = block(m, SEQ)
        upstream = self.upstream[rows]
        self.d_context[rows] = nt(upstream, self.out_w[...]).astype(BF16)
        for n in range(4):
            down = pl.ds(n * COLS, COLS)
            part = nt(upstream[:, :COLS], self.out[2, down]) + nt(upstream[:, COLS:], self.out[3, down])
            self.d_hidden[rows, down] = part.astype(BF16)

    def back_gelu(self, m):
        rows = block(m, SEQ)
        for n in range(4):
            lanes = pl.ds(n * COLS, COLS)
            self.d_hidden[rows, lanes] = (
                wide(self.d_hidden.at[rows, lanes]) * wide(self.slope_block(m, n))
            ).astype(BF16)

    def back_attend(self, m, pairs=range(4)):
        rows = block(m, SEQ)
        tables = (self.cos[...], self.low_sin[...], self.high_sin[...])
        for hp in pairs:
            lanes = pl.ds(hp * 128, 128)
            q, k, v = (self.qkv[t, rows, lanes] for t in range(3))
            d_context = self.d_context[rows, lanes]
            probs = [self.probs[m, hp * 2 + h] for h in range(2)]
            d_mine = [one_head(d_context, h) for h in range(2)]
            d_scores = []
            for h in range(2):
                wide_probs = probs[h].astype(F32)
                weighted = nt(d_mine[h], v) * wide_probs
                inner = jnp.sum(weighted, axis=1, keepdims=True)
                d_scores.append((weighted - wide_probs * inner).astype(BF16))
            both = [jnp.concatenate([one_head(u, 0), one_head(u, 1)], axis=0) for u in (q, k)]
            d_query = nn(jnp.concatenate(d_scores, axis=1), both[1])
            d_key = tn(jnp.concatenate(d_scores, axis=0), both[0])
            d_value = tn(jnp.concatenate(probs, axis=0), jnp.concatenate(d_mine, axis=0))
            d_query = rotated(d_query * HEAD ** -0.5, tables, -1.0)
            d_key = rotated(d_key, tables, -1.0)
            for t, part in enumerate((d_query, d_key, d_value)):
                self.d_projected[t, rows, lanes] = part.astype(BF16)

    def back_inputs(self, m, halves=range(2), start=0, count=SEQ):
        rows, here = ds(m * SEQ + start, count), ds(start, count)
        mean, rstd = self.mean[rows], self.rstd[rows]
        for j in halves:
            lanes = pl.ds(j * COLS, COLS)
            d_second = None
            for n in range(4):
                part = nt(self.d_hidden[rows, pl.ds(n * COLS, COLS)], self.up_block(n, (j * COLS, COLS))[...])
                d_second = part if d_second is None else d_second + part
            d_first = None
            for t in range(3):
                part = nt(self.d_projected[t, rows], self.qkv_w[t, lanes])
                d_first = part if d_first is None else d_first + part
            normed = (wide(self.x.at[rows, lanes]) - mean) * rstd
            sums = (d_first * normed, d_first, d_second * normed, d_second)
            for i, value in enumerate(sums):
                row = pl.ds(2 * i + j, 1)
                self.vectors[row] = self.vectors[row] + jnp.sum(value, axis=0, keepdims=True)
            d_normed = d_first * wide(self.ln1_scale.at[:, lanes]) + d_second * wide(self.ln2_scale.at[:, lanes])
            self.partial[m, here, lanes] = d_normed.astype(BF16)

    def weight_sum(self, name):
        def product(left, columns, targets):
            turned = left[:, columns].T
            for right, b in targets:
                self.grads[b // 4, pl.ds((b % 4) * COLS, COLS)] = nn(turned, right).astype(BF16)

        upstream = [self.upstream[:, pl.ds(c * COLS, COLS)] for c in range(2)]
        if name.startswith("down"):
            slab, half = int(name[-2]), self.core if int(name[-1]) else 1 - self.core
            turned = self.activated[:, ds((2 * slab + half) * COLS, COLS)].T
            for c in range(2):
                self.grads[slab, ds((2 * half + c) * COLS, COLS)] = nn(turned, upstream[c]).astype(BF16)
        elif name in ("up0", "up1"):
            r = int(name == "up1")
            d_hidden = [self.d_hidden[:, pl.ds(n * COLS, COLS)] for n in range(4)]
            product(self.second_in, pl.ds(r * COLS, COLS), [(d_hidden[n], 8 + 4 * r + n) for n in range(4)])
        else:
            r = int(name == "last1")
            if r == 0:
                product(self.context, pl.ds(0, COLS), [(upstream[c], 16 + c) for c in range(2)])
            d_projected = [self.d_projected[t] for t in range(3)]
            product(self.first_in, pl.ds(r * COLS, COLS), [(d_projected[t], 18 + 3 * r + t) for t in range(3)])

    def bias_sums(self):
        for t in range(3):
            self.vectors[pl.ds(8 + t, 1)] = jnp.sum(wide(self.d_projected.at[t]), axis=0, keepdims=True)
        for j in range(2):
            lanes = pl.ds(j * COLS, COLS)
            self.vectors[pl.ds(11 + j, 1)] = jnp.sum(wide(self.upstream.at[:, lanes]), axis=0, keepdims=True)
        for n in range(4):
            lanes = pl.ds(n * COLS, COLS)
            self.vectors[pl.ds(13 + n, 1)] = jnp.sum(wide(self.d_hidden.at[:, lanes]), axis=0, keepdims=True)


INPUTS = ("x_in", "cot_in", "order", "ln1_scale", "ln1_bias", "ln2_scale", "ln2_bias", "qkv_in", "qkv_bias",
          "out_in", "out_bias", "up_in", "up_bias", "down_in", "down_bias", "cos", "low_sin", "high_sin")
IN_HBM = ("x_in", "cot_in", "qkv_in", "out_in", "up_in", "down_in")
OUTPUTS = ("y_out", "g_out", "out", "small_out")
DMA = pltpu.SemaphoreType.DMA
SCRATCH = dict(
    grads=pltpu.VMEM((SLABS, SLAB_ROWS, COLS), BF16),
    arrived=pltpu.VMEM((SLABS, HALF, COLS), BF16),
    landing=pltpu.VMEM((SLABS, RX_ROWS, COLS), BF16),
    x=pltpu.VMEM((TOKENS, WIDTH), BF16),
    upstream=pltpu.VMEM((TOKENS, WIDTH), BF16),
    first_in=pltpu.VMEM((TOKENS, WIDTH), BF16),
    second_in=pltpu.VMEM((TOKENS, WIDTH), BF16),
    qkv=pltpu.VMEM((3, TOKENS, COLS), BF16),
    d_projected=pltpu.VMEM((3, TOKENS, COLS), BF16),
    context=pltpu.VMEM((TOKENS, COLS), BF16),
    d_context=pltpu.VMEM((TOKENS, COLS), BF16),
    probs=pltpu.VMEM((2, 8, SEQ, SEQ), BF16),
    activated=pltpu.VMEM((TOKENS, 4 * COLS), BF16),
    d_hidden=pltpu.VMEM((TOKENS, 4 * COLS), BF16),
    partial=pltpu.VMEM((2, SEQ, WIDTH), BF16),
    came=pltpu.VMEM((2, 2, OWN, WIDTH), BF16),
    mine=pltpu.VMEM((2, 2, OWN, WIDTH), BF16),
    mean=pltpu.VMEM((TOKENS, 1), F32),
    rstd=pltpu.VMEM((TOKENS, 1), F32),
    vectors=pltpu.VMEM((SMALL, COLS), F32),
    qkv_w=pltpu.VMEM((3, WIDTH, COLS), BF16),
    out_w=pltpu.VMEM((COLS, WIDTH), BF16),
    small_mine=pltpu.VMEM((SMALL, COLS), BF16),
    small_landing=pltpu.VMEM((2, 4, SMALL // 2, COLS), BF16),
    small_pair=pltpu.VMEM((SMALL, COLS), BF16),
    norms=pltpu.VMEM((2, 16, COLS), BF16),
    send=DMA((SLABS, 2)),
    recv=DMA((SLABS, 10)),
    small_send=DMA,
    small_recv=DMA((4,)),
    load=DMA((5,)),
    pair_send=DMA((2, 2)),
    pair_recv=DMA((2, 2, PARTS)),
    next_send=DMA((2,)),
    next_recv=DMA((2, PARTS)),
    far_send=DMA((2,)),
    far_recv=DMA((2,)),
    copy_send=DMA((2, 2)),
    copy_recv=DMA((2, 2)),
    copy_own=DMA((2, 2)),
    norms_sem=DMA((2,)),
)


class Refs:
    def __init__(self, pairs):
        self.__dict__.update(pairs)


def layer_kernel(*refs):
    names = INPUTS + OUTPUTS + tuple(SCRATCH)
    r = Refs(zip(names, refs))
    layer, place = Layer(vars(r)), Place()
    layer.core = place.core
    section, tensor = place.section, place.tensor
    first, last = section == 0, section == 1
    dp = lax.axis_index("dp")
    partner = (section, dp, 1 - tensor)
    near = (1 - section, dp, 1 - tensor)
    others = plane_partners(place) + [partner, near]
    load = r.load
    out, x, upstream = r.out, r.x, r.upstream

    greet(others)

    def fetch(src, dst, sem):
        pltpu.make_async_copy(src, dst, load.at[sem]).start()

    def fetch_out():
        fetch(r.out_in, r.out_w, 3)
        for c in range(2):
            fetch(r.down_in.at[:, pl.ds(c * COLS, COLS)], out.at[2 + c], 4)

    def fetch_up():
        for n in range(4):
            fetch(r.up_in.at[:, pl.ds(n * COLS, COLS)], layer.up_block(n, (0, WIDTH)), 2)

    @pl.when(first)
    def _():
        fetch(r.x_in, x, 0)
        fetch(r.qkv_in, r.qkv_w, 1)
        take(x, load.at[0])
        fetch_up()
        fetch_out()

    @pl.when(last)
    def _():
        fetch(r.cot_in, r.activated.at[:, pl.ds(0, WIDTH)], 0)
        fetch_out()
        fetch(r.qkv_in, r.qkv_w, 1)
        fetch_up()

    @pl.when(last)
    def _():
        given = r.activated
        take(upstream, load.at[0])
        swap = r.order[0] != 0
        one, two = given[pl.ds(0, SEQ), pl.ds(0, WIDTH)], given[pl.ds(SEQ, SEQ), pl.ds(0, WIDTH)]
        upstream[pl.ds(0, SEQ)] = jnp.where(swap, two, one)
        upstream[pl.ds(SEQ, SEQ)] = jnp.where(swap, one, two)
        take(r.out_w, load.at[3])
        take(out.at[pl.ds(2, 2)], load.at[4])

        def each(m, _):
            layer.back_branches(m)
            return 0

        lax.fori_loop(0, 2, each, 0)
        met(len(others))

    r.vectors[...] = jnp.zeros((SMALL, COLS), F32)

    own_half, other_half = tensor * OWN, (1 - tensor) * OWN

    def part_of(start, c):
        return ds(start + c * PART, PART)

    def exchange(m, kind):
        for c in range(PARTS):
            put(r.partial.at[m, part_of((1 - tensor) * OWN, c)], r.came.at[kind, m, part_of(0, c)],
                r.pair_send.at[kind, m], r.pair_recv.at[kind, m, c], partner)

    def finish_part(m, kind, c):
        rows = part_of(m * SEQ + tensor * OWN, c)
        here = part_of(0, c)
        came = r.came.at[kind, m, here]
        take(came, r.pair_recv.at[kind, m, c])
        total = wide(r.partial.at[m, part_of(tensor * OWN, c)]) + wide(came)
        if kind == 0:
            result = wide(x.at[rows]) + total + (wide(r.out_bias) + wide(r.down_bias))
        else:
            rstd = r.rstd[rows]
            normed = (wide(x.at[rows]) - r.mean[rows]) * rstd
            centered = (total - jnp.mean(total, axis=1, keepdims=True)
                        - normed * jnp.mean(total * normed, axis=1, keepdims=True))
            result = wide(upstream.at[rows]) + rstd * centered
        mine = r.mine.at[kind, m, here]
        mine[...] = result.astype(BF16)
        target = upstream if kind else x

        @pl.when(last if kind else first)
        def _():
            put(mine, target.at[rows], r.next_send.at[m], r.next_recv.at[m, c], near)

    def finish_parts(m, kind, parts):
        for c in parts:
            finish_part(m, kind, c)
        if PARTS - 1 in parts:
            take(r.came.at[kind, m], r.pair_send.at[kind, m])

    def finish(m):
        for kind, chosen in ((0, last), (1, first)):
            @pl.when(chosen)
            def _(kind=kind):
                finish_parts(m, kind, range(PARTS))

    def pass_on(m, target, parts):
        for c in parts:
            rows = target.at[part_of(m * SEQ + (1 - tensor) * OWN, c)]
            take(rows, r.next_recv.at[m, c])
            put(rows, rows, r.far_send.at[m], r.far_recv.at[m], partner)

    def arrived(m, target):
        take(target.at[pl.ds(0, OWN)], r.far_recv.at[m])

    def arrive(m, target):
        pass_on(m, target, range(PARTS))
        arrived(m, target)

    def tick(i, _):
        m = i

        def when(condition, action, *args):
            if isinstance(args[-1], range) and not args[-1]:
                return

            @pl.when(condition)
            def _():
                action(*args)

        def meanwhile(first_parts, next_parts, last_parts):
            when(jnp.logical_and(first, i == 1), finish_parts, 0, 0, first_parts)
            when(jnp.logical_and(last, i == 0), pass_on, 1, x, next_parts)
            when(jnp.logical_and(last, i == 1), finish_parts, 0, 1, last_parts)

        none = range(0)
        when(jnp.logical_and(last, i == 0), arrive, 0, x)
        when(jnp.logical_and(last, i == 1), arrived, 1, x)
        layer.norm(m)
        when(i == 0, take, r.qkv_w, load.at[1])
        layer.project(m)
        meanwhile(none, range(0, 2), none)
        layer.attend(m)
        meanwhile(range(0, 1), range(2, 5), range(0, 1))
        when(i == 0, take, out.at[pl.ds(4, 2)], load.at[2])
        layer.up(m)
        meanwhile(range(1, 4), range(5, PARTS), range(1, 4))

        @pl.when(jnp.logical_and(first, i == 0))
        def _():
            take(r.out_w, load.at[3])
            take(out.at[pl.ds(2, 2)], load.at[4])
            met(len(others))

        @pl.when(first)
        def _():
            layer.branches(m, other_half, OWN)
            meanwhile(range(4, PARTS), none, none)
            exchange(m, 0)
            layer.branches(m, own_half, OWN)

        @pl.when(last)
        def _():
            layer.back_gelu(m)
            layer.back_attend(m)
            layer.back_inputs(m)
            meanwhile(none, none, range(4, PARTS))
            exchange(m, 1)

        return 0

    lax.fori_loop(0, 2, tick, 0)

    @pl.when(first)
    def _():
        finish_parts(1, 0, range(PARTS))
        pass_on(0, upstream, range(PARTS))
        pass_on(1, upstream, range(PARTS))
        arrived(0, upstream)
        layer.back_branches(0)
        layer.back_gelu(0)
        layer.back_attend(0, range(0, 2))
        arrived(1, upstream)

    @pl.when(last)
    def _():
        finish_parts(1, 1, range(PARTS))

        def each(m, _):
            layer.branches(m)
            exchange(m, 0)
            return 0

        lax.fori_loop(0, 2, each, 0)

    grads = r.grads
    reduce = Reduce(place, grads, out, r.arrived, r.landing, r.send, r.recv)
    small = SmallReduce(place, r.small_mine, r.small_out, r.small_landing, r.small_pair,
                        r.small_send, r.small_recv)
    vectors, norms = r.vectors, r.norms

    def back(name):
        @pl.when(first)
        def _():
            if name == "back":
                layer.back_branches(1)
                layer.back_gelu(1)
                return
            m, half = int(name[-2]), int(name[-1])
            if name.startswith("attend"):
                layer.back_attend(m, range(2 * half, 2 * half + 2))
            else:
                layer.back_inputs(m, range(half, half + 1))
                if half:
                    exchange(m, 1)

    def sums():
        layer.bias_sums()
        norms[0] = vectors[pl.ds(0, 16)].astype(BF16)
        put(norms.at[0], norms.at[1], r.norms_sem.at[0], r.norms_sem.at[1], partner)
        r.small_mine[...] = vectors[...].astype(BF16)

    def norm_sums():
        take(norms.at[1], r.norms_sem.at[1])
        both = wide(norms.at[0]) + wide(norms.at[1])
        ln_row = lax.broadcasted_iota(jnp.int32, (16, COLS), 0) < 8
        r.small_mine[pl.ds(0, 16)] = jnp.where(ln_row, both, vectors[pl.ds(0, 16)]).astype(BF16)

    def copies():
        for m in range(2):
            for kind, final in ((0, r.y_out), (1, r.g_out)):
                rows = final.at[ds(m * SEQ + tensor * OWN, OWN)]
                mine = r.mine.at[kind, m]
                put(mine, rows, r.copy_send.at[kind, m], r.copy_recv.at[kind, m], partner)
                pltpu.make_async_copy(mine, rows, r.copy_own.at[kind, m]).start()

    for item in PLAN:
        if not isinstance(item, str):
            reduce.step(*item)
        elif item[:4] in ("back", "atte", "inpu"):
            back(item)
        elif item.startswith("finish"):
            finish(int(item[-1]))
        elif item.startswith("small"):
            small.step(int(item[-1]))
        elif item == "sums":
            sums()
        elif item == "norms":
            norm_sums()
        elif item == "copies":
            copies()
        else:
            layer.weight_sum(item)
    for s in range(SLABS):
        reduce.step(s, 10)
    for s in range(SLABS):
        reduce.drain(s)
    small.drain()
    take(norms.at[0], r.norms_sem.at[0])
    for m in range(2):
        for kind in range(2):
            take(r.mine.at[kind, m], r.copy_send.at[kind, m])
            take(r.mine.at[kind, m], r.copy_recv.at[kind, m])
            take(r.mine.at[kind, m], r.copy_own.at[kind, m])
        take(x.at[pl.ds(0, OWN)], r.next_send.at[m])
        take(x.at[pl.ds(0, OWN)], r.far_send.at[m])


def layer_call(*args):
    hbm, vmem = pl.BlockSpec(memory_space=pl.ANY), pl.BlockSpec(memory_space=pltpu.VMEM)
    smem = pl.BlockSpec(memory_space=pltpu.SMEM)
    rows = jax.ShapeDtypeStruct((TOKENS, WIDTH), BF16)
    return pl.pallas_call(
        layer_kernel,
        out_shape=(rows, rows, pltpu.VMEM((SLABS, SLAB_ROWS, COLS), BF16), pltpu.VMEM((SMALL, COLS), BF16)),
        in_specs=[hbm if name in IN_HBM else smem if name == "order" else vmem for name in INPUTS],
        out_specs=(hbm, hbm, vmem, vmem),
        scratch_shapes=list(SCRATCH.values()),
        compiler_params=pltpu.CompilerParams(
            collective_id=0, has_side_effects=True, vmem_limit_bytes=VMEM_LIMIT
        ),
    )(*args)


VECTORS = ((0, 2), (2, 2), (4, 2), (6, 2), (11, 2), (13, 4), (11, 2))


def widen_kernel(given, small, y_in, g_in, down, up, out, qkv, y_out, g_out, *rest):
    targets, (staged, held, rows, sems, copy_sems, row_sems) = rest[:8], rest[8:]
    passing = [(pltpu.make_async_copy(src, held.at[i], copy_sems.at[0, i]),
                pltpu.make_async_copy(held.at[i], dst, copy_sems.at[1, i]))
               for i, (src, dst) in enumerate(((y_in, y_out), (g_in, g_out)))]
    for come, _ in passing:
        come.start()
    values = small[...].astype(F32)
    moves = []
    for v, (row, count) in enumerate(VECTORS):
        for i in range(count):
            rows[v, :, pl.ds(i * COLS, COLS)] = values[row + i:row + i + 1]
        moves.append(pltpu.make_async_copy(rows.at[v, :, pl.ds(0, count * COLS)], targets[v], row_sems.at[v]))
    for t in range(3):
        moves.append(pltpu.make_async_copy(rows.at[7, :, pl.ds(t * COLS, COLS)], targets[7].at[t], row_sems.at[7 + t]))
        rows[7, :, pl.ds(t * COLS, COLS)] = values[8 + t:9 + t]
    for move in moves:
        move.start()

    def target(b):
        if b < 8:
            return down.at[pl.ds((b // 2) * COLS, COLS), pl.ds((b % 2) * COLS, COLS)]
        if b < 16:
            return up.at[pl.ds((b // 4 - 2) * COLS, COLS), pl.ds((b % 4) * COLS, COLS)]
        if b < 18:
            return out.at[:, pl.ds((b - 16) * COLS, COLS)]
        return qkv.at[(b - 18) % 3, pl.ds((b - 18) // 3 * COLS, COLS)]

    count, depth = SLABS * 4, 4
    copies = []
    for b in range(count):
        if b >= depth:
            copies[b - depth].wait()
        if b == 2 * depth:
            for come, go in passing:
                come.wait()
                go.start()
        slot = b % depth
        staged[slot] = given[b // 4, pl.ds((b % 4) * COLS, COLS)].astype(F32)
        copies.append(pltpu.make_async_copy(staged.at[slot], target(b), sems.at[slot]))
        copies[b].start()
    for b in range(count - depth, count):
        copies[b].wait()
    for move in moves + [go for _, go in passing]:
        move.wait()


def widened(grads, small, y, g):
    hbm, vmem = pl.BlockSpec(memory_space=pl.ANY), pl.BlockSpec(memory_space=pltpu.VMEM)
    shapes = [((2048, WIDTH), F32), ((WIDTH, 2048), F32), ((COLS, WIDTH), F32), ((3, WIDTH, COLS), F32),
              (y.shape, BF16), (g.shape, BF16)]
    shapes += [((1, rows * COLS), F32) for _, rows in VECTORS] + [((3, 1, COLS), F32)]
    grads, small = (pltpu.with_memory_space_constraint(a, pltpu.VMEM) for a in (grads, small))
    y, g = (pltpu.with_memory_space_constraint(a, pltpu.HBM) for a in (y, g))
    return pl.pallas_call(
        widen_kernel,
        out_shape=tuple(jax.ShapeDtypeStruct(shape, dtype) for shape, dtype in shapes),
        in_specs=[vmem, vmem] + [pl.BlockSpec(memory_space=pltpu.HBM)] * 2,
        out_specs=(hbm,) * 14,
        scratch_shapes=[pltpu.VMEM((4, COLS, COLS), F32), pltpu.VMEM((2, TOKENS, WIDTH), BF16),
                        pltpu.VMEM((8, 1, 4 * COLS), F32), DMA((4,)), DMA((2, 2)), DMA((10,))],
        compiler_params=pltpu.CompilerParams(vmem_limit_bytes=10 * 2**20),
    )(grads, small, y, g)


def shards(layer_input, cotangent, order, ln1_scale, ln1_bias, ln2_scale, ln2_bias, qkv_weight, qkv_bias,
           out_weight, out_bias, up_weight, up_bias, down_weight, down_bias):
    cos, low_sin, high_sin = (jnp.asarray(table) for table in rotary_tables())
    y, g, grads, small = layer_call(
        layer_input.reshape(TOKENS, WIDTH), cotangent.reshape(TOKENS, WIDTH), order,
        ln1_scale, ln1_bias, ln2_scale, ln2_bias,
        qkv_weight[0].transpose(1, 0, 2), qkv_bias[0], out_weight[0], out_bias, up_weight[0], up_bias,
        down_weight[0], down_bias, cos, low_sin, high_sin,
    )
    down, up, out, qkv, y, g, s1, b1, s2, b2, b_out, b_up, b_down, b_qkv = widened(grads, small, y, g)
    rows = (1, 2, 1, SEQ, WIDTH)
    return (y.reshape(rows), g.reshape(rows), s1, b1, s2, b2, qkv.transpose(1, 0, 2)[None], b_qkv.transpose(1, 0, 2),
            out[None], b_out, up[None], b_up, down[None], b_down)


def solution(mesh):
    return jax.shard_map(
        shards,
        mesh=mesh,
        in_specs=(
            P(None, "dp", None, None),
            P(None, "dp", None, None),
            P(),
            P("section", None),
            P("section", None),
            P("section", None),
            P("section", None),
            P("section", None, None, "tensor"),
            P("section", None, "tensor"),
            P("section", "tensor", None),
            P("section", None),
            P("section", None, "tensor"),
            P("section", "tensor"),
            P("section", "tensor", None),
            P("section", None),
        ),
        out_specs=(
            P("section", None, "dp", None, None),
            P("section", None, "dp", None, None),
            P("section", None),
            P("section", None),
            P("section", None),
            P("section", None),
            P("section", None, None, "tensor"),
            P("section", None, "tensor"),
            P("section", "tensor", None),
            P("section", None),
            P("section", None, "tensor"),
            P("section", "tensor"),
            P("section", "tensor", None),
            P("section", None),
        ),
        check_vma=False,
    )
```
